32 devices in a mesh: seq: 4 (over y, x), dp: 2 (over core), mp: 4 (over z).
Axes of the slice: x: 2, y: 2, z: 4, core: 2. Of those that a mesh axis runs over, the one named last changes fastest.
Arguments:
- inputs: bfloat16 [8, 512, 768], P('dp', 'seq'), may hold values from -6 to 6
- lengths: int32 [8], P('dp'), may hold values from 40 to 512, as said below
- query_weight: bfloat16 [768, 768], P(None, 'mp'), may hold values from -0.21875 to 0.21875
- query_bias: float32 [768], P('mp'), may hold values from -3 to 3
- key_weight: bfloat16 [768, 768], P(None, 'mp'), may hold values from -0.21875 to 0.21875
- value_weight: bfloat16 [768, 768], P(None, 'mp'), may hold values from -0.21875 to 0.21875
- value_bias: float32 [768], P('mp'), may hold values from -3 to 3
- rel_weight: float32 [12, 8], P('mp'), may hold values from -6 to 6
- out_weight: bfloat16 [768, 768], P('mp'), may hold values from -0.875 to 0.875
- out_bias: float32 [768], replicated, may hold values from -1.75 to 1.75
- attn_gain: float32 [768], replicated, may hold values from 0.5 to 1.5
- attn_shift: float32 [768], replicated, may hold values from -1.75 to 1.75
- up_weight: bfloat16 [768, 3072], P(None, 'mp'), may hold values from -0.21875 to 0.21875
- up_bias: float32 [3072], P('mp'), may hold values from -3 to 3
- down_weight: bfloat16 [3072, 768], P('mp'), may hold values from -0.109375 to 0.109375
- down_bias: float32 [768], replicated, may hold values from -1.75 to 1.75
- ffn_gain: float32 [768], replicated, may hold values from 0.5 to 1.5
- ffn_shift: float32 [768], replicated, may hold values from -1.75 to 1.75
- cotangent: bfloat16 [8, 256, 768], P('dp', 'seq'), may hold values from -6 to 6
Outputs:
- output: bfloat16 [8, 256, 768], P('dp', 'seq')
- input_grad: float32 [8, 512, 768], P('dp', 'seq')
- query_weight_grad: float32 [768, 768], P(None, 'mp')
- query_bias_grad: float32 [768], P('mp')
- key_weight_grad: float32 [768, 768], P(None, 'mp')
- value_weight_grad: float32 [768, 768], P(None, 'mp')
- value_bias_grad: float32 [768], P('mp')
- rel_weight_grad: float32 [12, 8], P('mp')
- out_weight_grad: float32 [768, 768], P('mp')
- out_bias_grad: float32 [768], replicated
- attn_gain_grad: float32 [768], replicated
- attn_shift_grad: float32 [768], replicated
- up_weight_grad: float32 [768, 3072], P(None, 'mp')
- up_bias_grad: float32 [3072], P('mp')
- down_weight_grad: float32 [3072, 768], P('mp')
- down_bias_grad: float32 [768], replicated
- ffn_gain_grad: float32 [768], replicated
- ffn_shift_grad: float32 [768], replicated
The draws below stay inside these ranges and needn't reach their ends.
Inputs may be any that keep to these rules, and one draw needn't show every extreme that they name: `lengths`: the number of valid tokens of each sentence, which are its first ones; in each aligned block of 4 sentences one, drawn from the seed, has all 512.
All inputs are finite; a program needn't handle non-finite values.
Results may differ from the reference program's by a relative error of at most 0.019.
Values may be sent and summed in bfloat16 or wider, within the bound.
No kernel may reach another device: no remote copies, remote signals or barrier semaphores. Data moves between devices by JAX's collectives and lax.ppermute only.
A program may use at most 64 MiB of HBM per device.

```python
import jax
import jax.numpy as jnp
from jax import lax

D = 768
HEADS = 12
HEAD_DIM = 64
FF = 3072
BASES = 8
LENGTH = 512
SENT_DEV = 4
SENTENCES = 8


def draw_lengths(key, part):
    key = jax.random.fold_in(key, 11)
    lowest = max(1, LENGTH * 5 // 64)
    drawn = jax.random.randint(jax.random.fold_in(key, 1), (SENTENCES,), lowest, LENGTH + 1)
    groups = SENTENCES // SENT_DEV
    chosen = jax.random.randint(jax.random.fold_in(key, 2), (groups,), 0, SENT_DEV)
    filled = jnp.arange(SENTENCES) % SENT_DEV == jnp.repeat(chosen, SENT_DEV)
    return jnp.where(filled, LENGTH, drawn).astype(jnp.int32)


def steps_of(stream_key, shape, pieces, low, largest):
    loudness = 1.0
    for position, shards_of in pieces:
        heights = jax.random.uniform(jax.random.fold_in(jax.random.fold_in(stream_key, 6), position), (shards_of,), jnp.float32, low / len(pieces), largest / len(pieces))
        loudness = loudness * jnp.repeat(jnp.exp(heights), shape[position] // shards_of).reshape((-1,) + (1,) * (len(shape) - 1 - position))
    return loudness


def bell_draw(key, shape, scale, reach, shards=(), held_as=jnp.bfloat16):
    array = scale * jax.random.normal(key, shape, jnp.float32)
    if shards:
        array = array * steps_of(key, shape, shards, -0.22, 0.18)
    return jnp.clip(array, -reach, reach).astype(held_as)


def setup_inputs(seed: int = 0) -> dict:
    key_of = jax.random.split(jax.random.key(seed), 20)
    inputs = bell_draw(key_of[0], (SENTENCES, LENGTH, D), 1.0, 6.0, ((0, 2), (1, 4)))
    lengths = draw_lengths(jax.random.fold_in(key_of[19], 71), 0)
    query_weight = bell_draw(key_of[2], (D, D), D ** -0.5, 0.21875, ((1, 4),))
    query_bias = bell_draw(key_of[3], (D,), 0.5, 3.0, ((0, 4),), jnp.float32)
    key_weight = bell_draw(key_of[4], (D, D), D ** -0.5, 0.21875, ((1, 4),))
    value_weight = bell_draw(key_of[5], (D, D), D ** -0.5, 0.21875, ((1, 4),))
    value_bias = bell_draw(key_of[6], (D,), 0.5, 3.0, ((0, 4),), jnp.float32)
    rel_weight = bell_draw(key_of[7], (HEADS, BASES), 1.0, 6.0, ((0, 4),), jnp.float32)
    out_weight = bell_draw(key_of[8], (D, D), (D // 16) ** -0.5, 0.875, ((0, 4),))
    out_bias = bell_draw(key_of[9], (D,), 0.3, 1.75, (), jnp.float32)
    attn_gain = jnp.clip(1.0 + 0.1 * jax.random.normal(key_of[10], (D,), jnp.float32), 0.5, 1.5)
    attn_shift = bell_draw(key_of[11], (D,), 0.3, 1.75, (), jnp.float32)
    up_weight = bell_draw(key_of[12], (D, FF), D ** -0.5, 0.21875, ((1, 4),))
    up_bias = bell_draw(key_of[13], (FF,), 0.5, 3.0, ((0, 4),), jnp.float32)
    down_weight = bell_draw(key_of[14], (FF, D), FF ** -0.5, 0.109375, ((0, 4),))
    down_bias = bell_draw(key_of[15], (D,), 0.3, 1.75, (), jnp.float32)
    ffn_gain = jnp.clip(1.0 + 0.1 * jax.random.normal(key_of[16], (D,), jnp.float32), 0.5, 1.5)
    ffn_shift = bell_draw(key_of[17], (D,), 0.3, 1.75, (), jnp.float32)
    cotangent = bell_draw(key_of[18], (SENTENCES, LENGTH // 2, D), 1.0, 6.0, ((0, 2), (1, 4)))
    return dict(inputs=inputs, lengths=lengths, query_weight=query_weight, query_bias=query_bias, key_weight=key_weight, value_weight=value_weight, value_bias=value_bias, rel_weight=rel_weight, out_weight=out_weight, out_bias=out_bias, attn_gain=attn_gain, attn_shift=attn_shift, up_weight=up_weight, up_bias=up_bias, down_weight=down_weight, down_bias=down_bias, ffn_gain=ffn_gain, ffn_shift=ffn_shift, cotangent=cotangent)


EPSILON = 1e-05
MASKED_SCORE = -1e+30
HIGHEST = lax.Precision.HIGHEST

@jax.custom_vjp
def low(v):
    return lax.optimization_barrier(v.astype(jnp.bfloat16)).astype(jnp.float32)

@jax.custom_vjp
def low_back(v):
    return v

def low_keep(v):
    return (low(v), None)

def low_pass(kept, grad):
    return (grad,)

def back_keep(v):
    return (v, None)

def back_low(kept, grad):
    return (low(grad),)
low.defvjp(low_keep, low_pass)
low_back.defvjp(back_keep, back_low)

def product(left_side, right_side):
    return jnp.einsum('...d,df->...f', left_side, right_side, precision=HIGHEST)

def layer_norm(vector_rows, norm_gain, norm_shift):
    center = vector_rows - lax.optimization_barrier(jnp.mean(vector_rows, axis=-1, keepdims=True))
    spread = lax.optimization_barrier(jnp.mean(center * center, axis=-1, keepdims=True))
    return center * lax.rsqrt(spread + EPSILON) * norm_gain + norm_shift

def basis_table(query_pos, key_pos, span_len):
    distance = key_pos[None, :] - query_pos[:, None]
    nearness = jnp.abs(distance)
    tables = []
    for degree in range(BASES // 2):
        reach_len = span_len * 4.0 ** degree / 64.0
        tables.append(jnp.exp(-nearness / reach_len))
    for degree in range(BASES // 2):
        reach_len = span_len * 4.0 ** degree / 64.0
        tables.append(jnp.tanh(distance / reach_len))
    return jnp.stack(tables)

def forward(inputs, key_valid, query_valid, basis_maps, params):
    query_weight, query_bias, key_weight, value_weight, value_bias, rel_weight, out_weight, out_bias, attn_gain, attn_shift, up_weight, up_bias, down_weight, down_bias, ffn_gain, ffn_shift = params
    groups = inputs.shape[0]
    pooled = 0.5 * (inputs[:, 0::2] + inputs[:, 1::2])
    queries = low((low_back(product(low(pooled), query_weight)) + query_bias) * HEAD_DIM ** (-0.5))
    keys = low(low_back(product(inputs, key_weight)))
    values = low(low_back(product(inputs, value_weight)) + value_bias)
    head_split = (groups, -1, HEADS, HEAD_DIM)
    position_bias = jnp.einsum('hm,mqk->hqk', rel_weight, basis_maps, precision=HIGHEST)
    raw_scores = jnp.einsum('gqhe,gkhe->ghqk', queries.reshape(head_split), keys.reshape(head_split), precision=HIGHEST)
    scores = low_back(raw_scores) + position_bias[None]
    scores = jnp.where(key_valid[:, None, None, :], scores, MASKED_SCORE)
    weights = jax.nn.softmax(scores, axis=-1)
    context = jnp.einsum('ghqk,gkhe->gqhe', low(weights), values.reshape(head_split), precision=HIGHEST)
    context = low(low_back(context.reshape(groups, -1, D)))
    attended = pooled + low_back(product(context, out_weight)) + out_bias
    normed = layer_norm(attended, attn_gain, attn_shift)
    upward = low_back(product(low(normed), up_weight)) + up_bias
    hidden = low(low_back(jax.nn.gelu(upward, approximate=False)))
    mixed = normed + low_back(product(hidden, down_weight)) + down_bias
    return layer_norm(mixed, ffn_gain, ffn_shift) * query_valid[:, :, None]

def reference(inputs, lengths, query_weight, query_bias, key_weight, value_weight, value_bias, rel_weight, out_weight, out_bias, attn_gain, attn_shift, up_weight, up_bias, down_weight, down_bias, ffn_gain, ffn_shift, cotangent):
    params = tuple((member.astype(jnp.float32) for member in (query_weight, query_bias, key_weight, value_weight, value_bias, rel_weight, out_weight, out_bias, attn_gain, attn_shift, up_weight, up_bias, down_weight, down_bias, ffn_gain, ffn_shift)))
    basis_maps = basis_table(2.0 * jnp.arange(LENGTH // 2).astype(jnp.float32), jnp.arange(LENGTH).astype(jnp.float32), LENGTH)
    positions = jnp.arange(LENGTH).astype(jnp.int32)
    pooled_pos = 2 * jnp.arange(LENGTH // 2).astype(jnp.int32)
    blocks = SENTENCES // SENT_DEV

    def group_step(running, member):
        block_inputs, block_lengths, block_cotangent = member
        key_valid = positions[None, :] < block_lengths[:, None]
        query_valid = (pooled_pos[None, :] < block_lengths[:, None]).astype(jnp.float32)

        def apply_layer(vector_rows, *weights):
            return forward(vector_rows, key_valid, query_valid, basis_maps, weights)
        result, pullback = jax.vjp(apply_layer, block_inputs.astype(jnp.float32), *params)
        gradients = pullback(block_cotangent.astype(jnp.float32))
        running = tuple((earlier + gradient for earlier, gradient in zip(running, gradients[1:])))
        return (running, (result.astype(jnp.bfloat16), gradients[0]))
    start_sums = tuple((jnp.zeros_like(member) for member in params))
    summed, (results, input_grads) = lax.scan(group_step, start_sums, (inputs.reshape(blocks, SENT_DEV, LENGTH, D), lengths.reshape(blocks, SENT_DEV), cotangent.reshape(blocks, SENT_DEV, LENGTH // 2, D)))
    return (results.reshape(SENTENCES, LENGTH // 2, D), input_grads.reshape(SENTENCES, LENGTH, D), summed[0], summed[1], summed[2], summed[3], summed[4], summed[5], summed[6], summed[7], summed[8], summed[9], summed[10], summed[11], summed[12], summed[13], summed[14], summed[15])
```

```python
import jax
import jax.numpy as jnp
from jax import lax
from jax.sharding import PartitionSpec as P

BASES = 8
EPSILON = 1e-05
MASKED_SCORE = -1e30
HIGHEST = lax.Precision.HIGHEST
F32 = jnp.float32
LOW = jnp.bfloat16


def mm(a, b, dims=((1,), (0,))):
    return lax.dot_general(a, b, (dims, ((), ())), preferred_element_type=F32)


def mm_nt(a, b):
    return mm(a, b, ((1,), (1,)))


def mm_tn(a, b):
    return mm(a, b, ((0,), (0,)))


def pick(stacked, index):
    return lax.dynamic_index_in_dim(stacked, index, 0, keepdims=False)


def reorder(stacked, base):
    return jnp.stack([pick(stacked, base ^ k) for k in range(stacked.shape[0])])


def swap(block, axis, size, k):
    return lax.ppermute(block, axis, [(s, s ^ k) for s in range(size)])


def gather_low(block, axis, size):
    return [block] + [swap(block, axis, size, k) for k in range(1, size)]


def scatter_sum(partial, axis, size):
    low = partial.astype(LOW)
    total = partial[0]
    for arrived in [swap(low[k], axis, size, k) for k in range(1, size)]:
        total = total + arrived.astype(F32)
    return total


def norm_stats(vector_rows):
    center = vector_rows - jnp.mean(vector_rows, axis=-1, keepdims=True)
    scale_inv = lax.rsqrt(jnp.mean(center * center, axis=-1, keepdims=True) + EPSILON)
    return (center * scale_inv, scale_inv)


def norm_back(grad_out, normed, scale_inv, norm_gain):
    grad_normed = grad_out * norm_gain
    centered = grad_normed - jnp.mean(grad_normed, axis=-1, keepdims=True)
    return scale_inv * (centered - normed * jnp.mean(grad_normed * normed, axis=-1, keepdims=True))


def gelu_exact(upward_vals):
    return jax.nn.gelu(upward_vals, approximate=False)


def basis_table(query_pos, key_pos, span_len):
    distance = key_pos[None, :] - query_pos[:, None]
    nearness = jnp.abs(distance)
    tables = []
    for degree in range(BASES // 2):
        reach_len = span_len * 4.0**degree / 64.0
        tables.append(jnp.exp(-nearness / reach_len))
    for degree in range(BASES // 2):
        reach_len = span_len * 4.0**degree / 64.0
        tables.append(jnp.tanh(distance / reach_len))
    return jnp.stack(tables)


def sum_plane(package, seq_size, dp_size, pieces):
    mine = lax.axis_index("dp") % 2
    here = lax.axis_index("seq")
    half = package.reshape((2, seq_size) + package.shape[1:])
    own = pick(half, mine).astype(F32)
    got = lax.ppermute(pick(half, 1 - mine), "dp", [(s, s ^ 1) for s in range(dp_size)])
    own = own + got.astype(F32)
    step = 2
    while step < dp_size:
        low = own.astype(LOW)
        own = low.astype(F32) + lax.ppermute(low, "dp", [(s, s ^ step) for s in range(dp_size)]).astype(F32)
        step *= 2
    own = reorder(own, here)
    total = scatter_sum(own, "seq", seq_size).astype(LOW)
    full = jnp.stack(gather_low(total, "seq", seq_size))
    full = reorder(full, here)
    other = lax.ppermute(full, "dp", [(s, s ^ 1) for s in range(dp_size)])
    both = reorder(jnp.stack([full, other]), mine)
    return both.reshape(package.shape)


def shards(
    inputs,
    lengths,
    query_weight,
    query_bias,
    key_weight,
    value_weight,
    value_bias,
    rel_weight,
    out_weight,
    out_bias,
    attn_gain,
    attn_shift,
    up_weight,
    up_bias,
    down_weight,
    down_bias,
    ffn_gain,
    ffn_shift,
    cotangent,
):
    seq_size, dp_size, mp_size = (lax.axis_size(a) for a in ("seq", "dp", "mp"))
    j, m = lax.axis_index("seq"), lax.axis_index("mp")
    sentences, block_len, width = inputs.shape
    assert sentences == seq_size == mp_size
    pooled_len = block_len // 2
    full_len = block_len * seq_size
    heads_here = rel_weight.shape[0]
    head_width = query_weight.shape[1] // heads_here
    part = heads_here * head_width
    query_scale = head_width ** (-0.5)
    turn = [(a * mp_size + b, b * mp_size + a) for a in range(seq_size) for b in range(mp_size)]

    blocks = jnp.stack(
        [pick(inputs, j)] + [swap(pick(inputs, j ^ k), "seq", seq_size, k) for k in range(1, seq_size)]
    )
    blocks = reorder(blocks, j ^ m)
    tokens = blocks.reshape(full_len, width)
    own_cotangent = lax.ppermute(pick(cotangent, m), ("seq", "mp"), turn)
    length = pick(lengths, j)
    order = m ^ jnp.arange(mp_size, dtype=jnp.int32)
    slot_pos = 2 * (order[:, None] * pooled_len + jnp.arange(pooled_len, dtype=jnp.int32)).reshape(-1)
    key_pos = (order[:, None] * block_len + jnp.arange(block_len, dtype=jnp.int32)).reshape(-1)
    basis_maps = basis_table(slot_pos.astype(F32), key_pos.astype(F32), full_len)
    key_valid = key_pos < length
    own_valid = (slot_pos[:pooled_len] < length).astype(F32)[:, None]

    widened = tokens.astype(F32)
    pooled = 0.5 * (widened[0::2] + widened[1::2])
    pooled_low = pooled.astype(LOW)
    own_pooled = pooled[:pooled_len]
    queries = ((mm(pooled_low, query_weight) + query_bias) * query_scale).astype(LOW)
    keys = mm(tokens, key_weight).astype(LOW)
    values = (mm(tokens, value_weight) + value_bias).astype(LOW)
    slots = queries.shape[0]
    heads = lambda a: a.reshape(-1, heads_here, head_width)
    position_bias = jnp.einsum("hm,mqk->hqk", rel_weight, basis_maps, precision=HIGHEST)
    raw = jnp.einsum("qhe,khe->hqk", heads(queries), heads(keys), preferred_element_type=F32)
    masked = jnp.where(key_valid[None, None, :], raw + position_bias, MASKED_SCORE)
    probs = jax.nn.softmax(masked, axis=-1)
    probs_low = probs.astype(LOW)
    context = jnp.einsum("hqk,khe->qhe", probs_low, heads(values), preferred_element_type=F32)
    context_low = context.reshape(slots, part).astype(LOW)
    stack = lambda a: a.reshape((mp_size, -1) + a.shape[1:])
    attended = own_pooled + scatter_sum(stack(mm(context_low, out_weight)), "mp", mp_size) + out_bias
    normed_attn, inv_attn = norm_stats(attended)
    normed = normed_attn * attn_gain + attn_shift
    normed_low = jnp.concatenate(gather_low(normed.astype(LOW), "mp", mp_size))
    upward = mm(normed_low, up_weight) + up_bias
    activated, gelu_pull = jax.vjp(gelu_exact, upward)
    hidden_low = activated.astype(LOW)
    mixed = normed + scatter_sum(stack(mm(hidden_low, down_weight)), "mp", mp_size) + down_bias
    normed_ffn, inv_ffn = norm_stats(mixed)
    output = ((normed_ffn * ffn_gain + ffn_shift) * own_valid).astype(LOW)
    grad_top = own_cotangent.astype(F32) * own_valid
    grad_mixed = norm_back(grad_top, normed_ffn, inv_ffn, ffn_gain)
    small = jnp.stack(
        [jnp.sum(grad_top * normed_ffn, 0), jnp.sum(grad_top, 0), jnp.sum(grad_mixed, 0)]
        + [jnp.zeros((width,), F32)] * 13
    )
    sent = jnp.concatenate([grad_mixed, small]).astype(LOW)
    arrived = jnp.stack(gather_low(sent, "mp", mp_size))
    grad_mixed_low = arrived[:, :pooled_len].reshape(slots, width)
    small_ffn = jnp.sum(arrived[:, pooled_len:].astype(F32), 0)
    grad_hidden = mm_nt(grad_mixed_low, down_weight).astype(LOW).astype(F32)
    grad_upward = gelu_pull(grad_hidden)[0]
    grad_upward_low = grad_upward.astype(LOW)
    back = scatter_sum(stack(mm_nt(grad_upward_low, up_weight)), "mp", mp_size)
    grad_normed = grad_mixed + back
    down_weight_grad = mm_tn(hidden_low, grad_mixed_low)
    up_weight_grad = mm_tn(normed_low, grad_upward_low)
    hidden_here = up_weight.shape[1]
    assert hidden_here == width
    up_bias_grad = jnp.sum(grad_upward, 0, keepdims=True)
    ffn_package = jnp.concatenate(
        [
            down_weight_grad.astype(LOW),
            up_weight_grad.astype(LOW),
            small_ffn[: 16 - up_bias_grad.shape[0]].astype(LOW),
            up_bias_grad.astype(LOW),
        ]
    )
    ffn_sum = lax.psum(ffn_package, ("seq", "dp"))

    grad_attended = norm_back(grad_normed, normed_attn, inv_attn, attn_gain)
    small = jnp.stack(
        [jnp.sum(grad_normed * normed_attn, 0), jnp.sum(grad_normed, 0), jnp.sum(grad_attended, 0)]
        + [jnp.zeros((width,), F32)] * 13
    )
    sent = jnp.concatenate([grad_attended, small]).astype(LOW)
    arrived = jnp.stack(gather_low(sent, "mp", mp_size))
    grad_attended_low = arrived[:, :pooled_len].reshape(slots, width)
    small_attn = jnp.sum(arrived[:, pooled_len:].astype(F32), 0)
    turned = lax.ppermute(jnp.stack([output, grad_attended.astype(LOW)]), ("seq", "mp"), turn)
    turned_output, turned_residual = turned[0], turned[1].astype(F32)
    output_all = reorder(jnp.stack(gather_low(turned_output, "mp", mp_size)), m)

    grad_context = mm_nt(grad_attended_low, out_weight).astype(LOW)
    grad_probs = jnp.einsum("qhe,khe->hqk", heads(grad_context), heads(values), preferred_element_type=F32)
    grad_values = jnp.einsum("hqk,qhe->khe", probs_low, heads(grad_context), preferred_element_type=F32)
    grad_scores = probs * (grad_probs - jnp.sum(probs * grad_probs, axis=-1, keepdims=True))
    grad_scores_low = grad_scores.astype(LOW)
    grad_queries = jnp.einsum("hqk,khe->qhe", grad_scores_low, heads(keys), preferred_element_type=F32) * query_scale
    grad_keys = jnp.einsum("hqk,qhe->khe", grad_scores_low, heads(queries), preferred_element_type=F32)
    grad_queries = grad_queries.reshape(slots, part)
    grad_values = grad_values.reshape(full_len, part)
    grad_queries_low = grad_queries.astype(LOW)
    grad_keys_low = grad_keys.reshape(full_len, part).astype(LOW)
    grad_values_low = grad_values.astype(LOW)
    from_keys = mm_nt(grad_keys_low, key_weight) + mm_nt(grad_values_low, value_weight)
    from_queries = mm_nt(grad_queries_low, query_weight)
    partial = stack(from_keys + jnp.repeat(0.5 * from_queries, 2, axis=0)).astype(LOW)
    own_input = jnp.repeat(0.5 * turned_residual, 2, axis=0)
    for k in range(mp_size):
        route = [(a * mp_size + b, (b ^ k) * mp_size + a) for a in range(seq_size) for b in range(mp_size)]
        own_input = own_input + lax.ppermute(partial[k], ("seq", "mp"), route).astype(F32)
    input_all = reorder(jnp.stack(gather_low(own_input.astype(LOW), "mp", mp_size)), m).astype(F32)

    rel_weight_grad = jnp.einsum("hqk,mqk->hm", grad_scores, basis_maps, precision=HIGHEST)
    tail = jnp.concatenate(
        [jnp.sum(grad_queries, 0), jnp.sum(grad_values, 0), rel_weight_grad.reshape(-1)]
    )
    tail = jnp.pad(tail, (0, -tail.shape[0] % width)).reshape(-1, width)
    package = jnp.concatenate(
        [
            mm_tn(grad_queries_low, pooled_low),
            mm_tn(grad_keys_low, tokens),
            mm_tn(grad_values_low, tokens),
            mm_tn(context_low, grad_attended_low),
            small_attn[:3],
            tail,
        ]
    )
    pieces = 2 * seq_size
    package = jnp.pad(package, ((0, -package.shape[0] % (pieces * 16)), (0, 0))).astype(LOW)
    summed = sum_plane(package.reshape(pieces, -1, width), seq_size, dp_size, pieces).reshape(-1, width).astype(F32)
    ffn_sum = ffn_sum.astype(F32)
    small_attn = summed[4 * part : 4 * part + 3]
    tail = summed[4 * part + 3 : 4 * part + 3 + tail.shape[0]].reshape(-1)
    small_ffn = ffn_sum[2 * hidden_here :]
    up_sum = ffn_sum[hidden_here : hidden_here + width]
    return (
        output_all,
        input_all,
        summed[:part].T,
        tail[:part],
        summed[part : 2 * part].T,
        summed[2 * part : 3 * part].T,
        tail[part : 2 * part],
        tail[2 * part : 2 * part + rel_weight.size].reshape(rel_weight.shape),
        summed[3 * part : 4 * part],
        small_attn[2],
        small_attn[0],
        small_attn[1],
        up_sum,
        small_ffn[16 - up_bias_grad.shape[0] :].reshape(-1)[:hidden_here],
        ffn_sum[:hidden_here],
        small_ffn[2],
        small_ffn[0],
        small_ffn[1],
    )


def solution(mesh):
    return jax.shard_map(
        shards,
        mesh=mesh,
        in_specs=(
            P("dp", "seq", None),
            P("dp"),
            P(None, "mp"),
            P("mp"),
            P(None, "mp"),
            P(None, "mp"),
            P("mp"),
            P("mp", None),
            P("mp", None),
            P(),
            P(),
            P(),
            P(None, "mp"),
            P("mp"),
            P("mp", None),
            P(),
            P(),
            P(),
            P("dp", "seq", None),
        ),
        out_specs=(
            P("dp", "seq", None),
            P("dp", "seq", None),
            P(None, "mp"),
            P("mp"),
            P(None, "mp"),
            P(None, "mp"),
            P("mp"),
            P("mp", None),
            P("mp", None),
            P(),
            P(),
            P(),
            P(None, "mp"),
            P("mp"),
            P("mp", None),
            P(),
            P(),
            P(),
        ),
        check_vma=False,
    )
```

```python
import functools

import jax
import jax.numpy as jnp
from jax import lax
from jax.experimental import pallas as pl
from jax.experimental.pallas import tpu as pltpu
from jax.sharding import PartitionSpec as P

BASES = 8
EPSILON = 1e-05
MASKED_SCORE = -1e30
F32 = jnp.float32
LOW = jnp.bfloat16
SMALL_ROWS = 16
MIB = 1024 * 1024


def f32(*shape):
    return jax.ShapeDtypeStruct(shape, F32)


def low(*shape):
    return jax.ShapeDtypeStruct(shape, LOW)


def kernel(body, outs, args, smem=0, scratch=(), micros=1.0, limit=16, hbm=()):
    in_specs = [pl.BlockSpec(memory_space=pltpu.SMEM)] * smem
    in_specs += [pl.BlockSpec(memory_space=pltpu.VMEM)] * (len(args) - smem)
    whole = pl.BlockSpec(memory_space=pltpu.VMEM)
    if isinstance(outs, list):
        out_specs = [pl.BlockSpec(memory_space=pltpu.HBM) if n in hbm else whole for n in range(len(outs))]
    else:
        out_specs = whole
    return pl.pallas_call(
        body,
        out_shape=outs,
        in_specs=in_specs,
        out_specs=out_specs,
        scratch_shapes=list(scratch),
        compiler_params=pltpu.CompilerParams(vmem_limit_bytes=limit * MIB),
        cost_estimate=pl.CostEstimate(
            flops=int(micros * 4e8), bytes_accessed=int(micros * 3e6), transcendentals=0
        ),
    )(*args)


def after(value, *events):
    return lax.optimization_barrier((value, events))[0]


def dot_of(dims, a, b):
    return lax.dot_general(a, b, (dims, ((), ())), preferred_element_type=F32)


mm = functools.partial(dot_of, ((1,), (0,)))
mm_nt = functools.partial(dot_of, ((1,), (1,)))
mm_tn = functools.partial(dot_of, ((0,), (0,)))


def swap(block, axis, size, k):
    return lax.ppermute(block, axis, [(s, s ^ k) for s in range(size)])


def gather_low(block, axis, size):
    return [swap(block, axis, size, k) for k in range(1, size)]


def scatter_low(blocks, axis, size):
    return [swap(blocks[k - 1], axis, size, k) for k in range(1, size)]


def pick(stacked, index):
    return lax.dynamic_index_in_dim(stacked, index, 0, keepdims=False)


def norm_stats(rows):
    center = rows - jnp.mean(rows, axis=-1, keepdims=True)
    scale_inv = lax.rsqrt(jnp.mean(center * center, axis=-1, keepdims=True) + EPSILON)
    return center * scale_inv, scale_inv


def norm_back(grad_out, normed, scale_inv, gain):
    grad_normed = grad_out * gain
    centered = grad_normed - jnp.mean(grad_normed, axis=-1, keepdims=True)
    return scale_inv * (centered - normed * jnp.mean(grad_normed * normed, axis=-1, keepdims=True))


def total_of(own_ref, arrived_refs):
    total = own_ref[...]
    for ref in arrived_refs:
        total = total + ref[...].astype(F32)
    return total


def pair_matrix(rows, cols, tall):
    r = lax.broadcasted_iota(jnp.int32, (rows, cols), 0)
    c = lax.broadcasted_iota(jnp.int32, (rows, cols), 1)
    hit = (r >> 1) == c if tall else r == (c >> 1)
    return jnp.where(hit, 0.5, 0.0).astype(LOW)


def distances(ids, chunk, rows, block_len, slots):
    j = ids[0]
    start = chunk * rows
    token = (j ^ (start // block_len)) * block_len + start % block_len
    token = token + lax.broadcasted_iota(jnp.int32, (rows, slots), 0)
    s = lax.broadcasted_iota(jnp.int32, (rows, slots), 1)
    half = block_len // 2
    slot = (j ^ (s // half)) * half + s % half
    return token, (token - 2 * slot).astype(F32)


def basis_of(distance, index, span):
    degree = index % (BASES // 2)
    inverse = 64.0 / (span * 4.0**degree)
    if index < BASES // 2:
        return jnp.exp(jnp.abs(distance) * (-inverse))
    return jnp.tanh(distance * inverse)


def bias_body(heads, block_len, rows, ids, rel, out):
    full, slots = out.shape[1:]

    def step(chunk, carry):
        token, distance = distances(ids, chunk, rows, block_len, slots)
        sums = [jnp.zeros((rows, slots), F32)] * heads
        for index in range(BASES):
            base = basis_of(distance, index, full)
            sums = [sums[h] + rel[h, index] * base for h in range(heads)]
        valid = token < ids[3]
        for h in range(heads):
            out[h, pl.ds(pl.multiple_of(chunk * rows, rows), rows), :] = jnp.where(valid, sums[h], MASKED_SCORE)
        return carry

    lax.fori_loop(0, full // rows, step, 0)


def rel_body(heads, block_len, rows, ids, scores_ref, out, acc):
    full, slots = scores_ref.shape[1:]
    acc[...] = jnp.zeros_like(acc)

    def step(chunk, carry):
        _, distance = distances(ids, chunk, rows, block_len, slots)
        at = pl.ds(pl.multiple_of(chunk * rows, rows), rows)
        grads = [scores_ref[h, at, :] for h in range(heads)]
        for index in range(BASES):
            base = basis_of(distance, index, full)
            for h in range(heads):
                acc[h * BASES + index] += jnp.sum((grads[h] * base).reshape(rows // 8, 8, slots), axis=0)
        return carry

    lax.fori_loop(0, full // rows, step, 0)
    for row in range(heads * BASES):
        col = jnp.sum(jnp.sum(acc[row], axis=0, keepdims=True), axis=1, keepdims=True)
        out[row : row + 1, :] = jnp.broadcast_to(col, (1, out.shape[1]))


def attend_body(heads, query_scale, ids, *refs):
    x = refs[:4]
    wq, wk, wv, wo, qb, vb, ob, bias, own_out, p1, p2, p3 = refs[4:16]
    hbm = refs[16:23]
    scr, probs_ref, qt, kt, vt, ct, pooled_low, sem = refs[23:]
    probs_hbm, qt_hbm, kt_hbm, vt_hbm, ct_hbm, pooled_hbm, x_hbm = hbm
    block_len = x[0].shape[0]
    half = block_len // 2
    head = wq.shape[0] // heads
    copies = []

    def send(source, target):
        copy = pltpu.make_async_copy(source, target, sem.at[len(copies)])
        copy.start()
        copies.append(copy)

    for b in range(4):
        send(x[b], x_hbm.at[pl.ds(b * block_len, block_len), :])
    pairs = pair_matrix(half, block_len, False)
    for b in range(4):
        span = slice(b * block_len, (b + 1) * block_len)
        kt[:, span] = mm_nt(wk[...], x[b][...]).astype(LOW)
        vt[:, span] = (mm_nt(wv[...], x[b][...]) + vb[...]).astype(LOW)
        pooled = mm(pairs, x[b][...])
        scr[b] = pooled
        pooled_low[b * half : (b + 1) * half, :] = pooled.astype(LOW)
    turn = ids[0] ^ ids[1]
    own_out[...] = scr[turn] + ob[...]
    qt[...] = ((mm_nt(wq[...], pooled_low[...]) + qb[...]) * query_scale).astype(LOW)
    send(kt, kt_hbm)
    send(vt, vt_hbm)
    send(qt, qt_hbm)
    send(pooled_low, pooled_hbm)
    for h in range(heads):
        at = slice(h * head, (h + 1) * head)
        scores = mm_tn(kt[at, :], qt[at, :]) + bias[h]
        grown = jnp.exp(scores - jnp.max(scores, axis=0, keepdims=True))
        probs = grown * (1.0 / jnp.sum(grown, axis=0, keepdims=True))
        probs_ref[h] = probs
        send(probs_ref.at[h], probs_hbm.at[h])
        ct[at, :] = mm(vt[at, :], probs.astype(LOW)).astype(LOW)
    send(ct, ct_hbm)
    result = mm_tn(ct[...], wo[...])
    for b in range(4):
        scr[b] = result[b * half : (b + 1) * half, :]
    own_out[...] += scr[turn]
    for k, out in ((1, p1), (2, p2), (3, p3)):
        out[...] = scr[turn ^ k].astype(LOW)
    for copy in copies:
        copy.wait()


def feed_body(ids, a0, a1, a2, a3, gain, shift, wu, ub, wd, db, own, p1, p2, p3, *refs):
    hidden_out, slope_out, normed_out, unit_out, inv_out, scr = refs
    rows, width = a0.shape
    turn = ids[0] ^ ids[1]
    for k, a in enumerate((a0, a1, a2, a3)):
        scr[turn ^ k] = a[...].astype(F32)
    unit, inv = norm_stats(scr[...].reshape(4 * rows, width))
    normed = unit * gain[...] + shift[...]
    unit_out[...] = unit
    inv_out[...] = jnp.broadcast_to(inv, inv_out.shape)
    normed_low = normed.astype(LOW)
    normed_out[...] = normed_low
    scr[...] = normed.reshape(scr.shape)
    own[...] = scr[turn] + db[...]
    up = mm(normed_low, wu[...]) + ub[...]
    phi = 0.5 * (1.0 + lax.erf(up * (0.5**0.5)))
    density = jnp.exp(up * up * -0.5) * 0.3989422804014327
    hidden = (up * phi).astype(LOW)
    hidden_out[...] = hidden
    slope_out[...] = phi + up * density
    scr[...] = mm(hidden, wd[...]).reshape(scr.shape)
    own[...] += scr[turn]
    for k, out in ((1, p1), (2, p2), (3, p3)):
        out[...] = scr[turn ^ k].astype(LOW)


def small_rows(*sums):
    return jnp.concatenate(list(sums) + [jnp.zeros((SMALL_ROWS - len(sums), sums[0].shape[1]), F32)])


def feed_back_body(ids, *refs):
    pieces, cots = refs[:4], refs[4:8]
    gain, shift, slope, wd, wu, own, p1, p2, p3 = refs[8:17]
    outs = refs[17:21]
    grad_out, upward_out, small_out, scr, low_scr = refs[21:]
    rows, width = own.shape
    slots = 4 * rows
    turn = ids[0] ^ ids[1]
    for k, piece in enumerate(pieces):
        scr[turn ^ k] = piece[...].astype(F32)
    unit, inv = norm_stats(scr[...].reshape(slots, width))
    s = lax.broadcasted_iota(jnp.int32, (slots, 1), 0)
    slot = (ids[0] ^ (s // rows)) * rows + s % rows
    valid = jnp.where(2 * slot < ids[3], 1.0, 0.0)
    output = ((unit * gain[...] + shift[...]) * valid).astype(LOW)
    for b in range(4):
        outs[b][...] = output[b * rows : (b + 1) * rows, :]
        low_scr[b * rows : (b + 1) * rows, :] = cots[b][...]
    top = low_scr[...].astype(F32) * valid
    grad = norm_back(top, unit, inv, gain[...])
    grad_low = grad.astype(LOW)
    grad_out[...] = grad_low
    scr[...] = grad.reshape(scr.shape)
    own[...] = scr[turn]
    hidden = mm_nt(grad_low, wd[...]).astype(LOW).astype(F32)
    upward = hidden * slope[...]
    upward_low = upward.astype(LOW)
    upward_out[...] = upward_low
    total = lambda a: jnp.sum(a, axis=0, keepdims=True)
    small_out[...] = small_rows(total(top * unit), total(top), total(grad), total(upward))
    scr[...] = mm_nt(upward_low, wu[...]).reshape(scr.shape)
    own[...] += scr[turn]
    for k, out in ((1, p1), (2, p2), (3, p3)):
        out[...] = scr[turn ^ k].astype(LOW)


def feed_weights_body(flip, ids, hidden, grad, normed, upward, out, left, right):
    which = ids[2] ^ flip

    @pl.when(which == 0)
    def _():
        left[...] = hidden[...]
        right[...] = grad[...]

    @pl.when(which != 0)
    def _():
        left[...] = normed[...]
        right[...] = upward[...]

    step = 256
    for at in range(0, left.shape[1], step):
        out[at : at + step, :] = mm_tn(left[:, at : at + step], right[...]).astype(out.dtype)


def row_sums(rows):
    high = rows.astype(LOW)
    rest = (rows - high.astype(F32)).astype(LOW)
    ones = jnp.ones((8, rows.shape[1]), LOW)
    return mm_nt(ones, high) + mm_nt(ones, rest)


def attend_back_body(heads, query_scale, ids, *refs):
    s = refs[:4]
    unit, inv, gain, wq, wk, wv, wo, probs_ref, qt, kt, vt = refs[4:15]
    o = refs[15:19]
    scores_out, stack, grad_out, small_out, sums_out, scr, weights, dct, repeated, result = refs[19:]
    part = wq.shape[0]
    head = part // heads
    slots, full = qt.shape[1], kt.shape[1]
    half, block_len = slots // 4, full // 4
    quarter = block_len // 4
    turn = ids[0] ^ ids[1]
    for k in range(4):
        scr[turn ^ k] = s[k][...].astype(F32)
    grad_normed = scr[...].reshape(unit.shape)
    grad = norm_back(grad_normed, unit[...], inv[:, :1], gain[...])
    grad_low = grad.astype(LOW)
    grad_out[...] = grad_low
    total = lambda a: jnp.sum(a, axis=0, keepdims=True)
    small_out[...] = small_rows(total(grad_normed * unit[...]), total(grad_normed), total(grad))
    weights[:part, :] = wk[...]
    weights[part : 2 * part, :] = wv[...]
    weights[2 * part :, :] = wq[...]
    dct[...] = mm_nt(wo[...], grad_low).astype(LOW)
    for h in range(heads):
        at = slice(h * head, (h + 1) * head)
        probs = probs_ref[h]
        grad_probs = mm_tn(vt[at, :], dct[at, :])
        grad_values = mm_nt(dct[at, :], probs.astype(LOW))
        scores = probs * (grad_probs - jnp.sum(probs * grad_probs, axis=0, keepdims=True))
        scores_out[h] = scores
        scores_low = scores.astype(LOW)
        grad_queries = mm(kt[at, :], scores_low) * query_scale
        stack[at, :] = mm_nt(qt[at, :], scores_low).astype(LOW)
        stack[part + h * head : part + (h + 1) * head, :] = grad_values.astype(LOW)
        stack[2 * part + h * head : 2 * part + (h + 1) * head, :slots] = grad_queries.astype(LOW)
        sums_out[h, :8, :] = row_sums(grad_queries)
        sums_out[h, 8:, :] = row_sums(grad_values)
    pairs = pair_matrix(half, block_len, False)
    for b in range(4):
        repeated[:, b * block_len : (b + 1) * block_len] = mm(
            stack[2 * part :, b * half : (b + 1) * half], pairs
        ).astype(LOW)
    result[...] = mm_tn(stack[: 2 * part, :], weights[: 2 * part, :]) + mm_tn(repeated[...], weights[2 * part :, :])
    spread = pair_matrix(quarter, quarter // 2, True)
    scr[...] = grad.reshape(scr.shape)
    for b in range(4):
        to = slice(b * quarter, (b + 1) * quarter)
        rows = lambda k: pl.ds(pl.multiple_of(b * block_len + (ids[1] ^ k) * quarter, quarter), quarter)
        residual = scr[b, pl.ds(pl.multiple_of(ids[1] * (quarter // 2), quarter // 2), quarter // 2), :]
        high = residual.astype(LOW)
        rest = (residual - high.astype(F32)).astype(LOW)
        o[0][to, :] = result[rows(0), :] + (mm(spread, high) + mm(spread, rest))
        for k in range(1, 4):
            o[k][to, :] = result[rows(k), :].astype(LOW)


def attend_weights_body(ids, x, grad, pooled_low, stack, ct, small_feed, small_attend, sums, rel, keep, send, scr):
    part, slots = ct.shape
    heads = sums.shape[0]
    scr[0, :part, :] = mm(stack[2 * part :, :slots], pooled_low[...])
    scr[0, part : 2 * part, :] = mm(stack[:part, :], x[...])
    scr[1, :part, :] = mm(stack[part : 2 * part, :], x[...])
    scr[1, part : 2 * part, :] = mm(ct[...], grad[...])
    scr[:, 2 * part :, :] = jnp.zeros((2, scr.shape[1] - 2 * part, scr.shape[2]), F32)
    scr[0, 2 * part : 2 * part + SMALL_ROWS, :] = small_feed[...]
    scr[0, 2 * part + SMALL_ROWS : 2 * part + 2 * SMALL_ROWS, :] = small_attend[...]
    for h in range(heads):
        scr[1, 2 * part + h * SMALL_ROWS : 2 * part + (h + 1) * SMALL_ROWS, : sums.shape[2]] = sums[h]
    scr[0, 2 * part + 2 * SMALL_ROWS :, : rel.shape[1]] = rel[...]
    keep[...] = scr[ids[2]]
    send[...] = scr[1 - ids[2]].astype(LOW)


def halves_body(ids, keep, arrived, own, p1, p2, p3):
    rows = own.shape[0]
    for k, out in enumerate((own, p1, p2, p3)):
        at = pl.ds(pl.multiple_of((ids[0] ^ k) * rows, rows), rows)
        out[...] = (keep[at, :] + arrived[at, :].astype(F32)).astype(out.dtype)


def total_body(own, r1, r2, r3, out):
    out[...] = total_of(own, (r1, r2, r3)).astype(LOW)


def stack_body(ids, t0, t1, t2, t3, out):
    rows = t0.shape[0]
    for k, t in enumerate((t0, t1, t2, t3)):
        out[pl.ds(pl.multiple_of((ids[0] ^ k) * rows, rows), rows), :] = t[...]


def unpack_feed_body(ids, mine, other, first, second):
    for c, (a, b) in ((0, (mine, other)), (1, (other, mine))):

        @pl.when(ids[2] == c)
        def _(a=a, b=b):
            first[...] = a[...].astype(F32)
            second[...] = b[...].astype(F32)


def unpack_attend_body(ids, mine, other, dq, dk, dv, do, tail_a, tail_b):
    part = dq.shape[0]
    for c, (a, b) in ((0, (mine, other)), (1, (other, mine))):

        @pl.when(ids[2] == c)
        def _(a=a, b=b):
            dq[...] = a[:part, :].astype(F32)
            dk[...] = a[part : 2 * part, :].astype(F32)
            tail_a[...] = a[2 * part :, :].astype(F32)
            dv[...] = b[:part, :].astype(F32)
            do[...] = b[part : 2 * part, :].astype(F32)
            tail_b[...] = b[2 * part :, :].astype(F32)


def quarters_body(own, r1, r2, r3, q0, q1, q2, q3):
    total = total_of(own, (r1, r2, r3)).astype(LOW)
    rows = q0.shape[0]
    for b, q in enumerate((q0, q1, q2, q3)):
        q[...] = total[b * rows : (b + 1) * rows, :]


def join_body(q0, q1, q2, q3, out):
    rows = q0.shape[0]
    for b, q in enumerate((q0, q1, q2, q3)):
        out[b * rows : (b + 1) * rows, :] = q[...]


def place_body(ids, t0, t1, t2, t3, out):
    rows = out.shape[1] // 4
    for k, t in enumerate((t0, t1, t2, t3)):
        at = pl.ds(pl.multiple_of((ids[1] ^ k) * rows, rows), rows)
        for b in range(4):
            out[ids[0] ^ b, at, :] = t[b * rows : (b + 1) * rows, :].astype(out.dtype)


def place_output_body(ids, t0, t1, t2, t3, out):
    for b, t in enumerate((t0, t1, t2, t3)):
        out[ids[0] ^ b] = t[...]


def plane_halves(ids, keep, arrived):
    rows, width = keep.shape[0] // 4, keep.shape[1]
    return kernel(
        halves_body, [f32(rows, width)] + [low(rows, width)] * 3, (ids, keep, arrived), smem=1, micros=1.5
    )


def plane_total(own, arrived, dp_size):
    total = kernel(total_body, low(*own.shape), (own, *arrived), micros=0.5)
    step = 2
    while step < dp_size:
        total = (total.astype(F32) + swap(total, "dp", dp_size, step).astype(F32)).astype(LOW)
        step *= 2
    return total


def plane_join(ids, pieces):
    rows, width = pieces[0].shape
    return kernel(stack_body, low(4 * rows, width), (ids, *pieces), smem=1, micros=0.8)


def shards(
    inputs,
    lengths,
    query_weight,
    query_bias,
    key_weight,
    value_weight,
    value_bias,
    rel_weight,
    out_weight,
    out_bias,
    attn_gain,
    attn_shift,
    up_weight,
    up_bias,
    down_weight,
    down_bias,
    ffn_gain,
    ffn_shift,
    cotangent,
):
    seq_size, dp_size, mp_size = (lax.axis_size(a) for a in ("seq", "dp", "mp"))
    j, m, c = lax.axis_index("seq"), lax.axis_index("mp"), lax.axis_index("dp") % 2
    sentences, block_len, width = inputs.shape
    assert sentences == seq_size == mp_size == 4 and dp_size % 2 == 0
    half = block_len // 2
    full, slots = 4 * block_len, 4 * half
    heads = rel_weight.shape[0]
    part = query_weight.shape[1]
    head = part // heads
    hidden_here = up_weight.shape[1]
    assert hidden_here == width
    query_scale = head ** (-0.5)
    row = lambda v: v.reshape(1, -1)
    column = lambda v: v.reshape(-1, 1)
    ids = jnp.stack([j, m, c, pick(lengths, j)]).astype(jnp.int32)
    wq, wk, wv = query_weight.T, key_weight.T, value_weight.T

    x = [pick(inputs, j)] + [swap(pick(inputs, j ^ k), "seq", seq_size, k) for k in range(1, 4)]
    bias = kernel(
        functools.partial(bias_body, heads, block_len, 32), f32(heads, full, slots), (ids, rel_weight), smem=2, micros=3.0
    )
    own, p1, p2, p3, probs, qt, kt, vt, ct, pooled_low, tokens = kernel(
        functools.partial(attend_body, heads, query_scale),
        [f32(half, width)]
        + [low(half, width)] * 3
        + [f32(heads, full, slots), low(part, slots), low(part, full), low(part, full), low(part, slots)]
        + [low(slots, width), low(full, width)],
        (ids, *x, wq, wk, wv, out_weight, column(query_bias), column(value_bias), row(out_bias), bias),
        smem=1,
        scratch=[
            pltpu.VMEM((4, half, width), F32),
            pltpu.VMEM((heads, full, slots), F32),
            pltpu.VMEM((part, slots), LOW),
            pltpu.VMEM((part, full), LOW),
            pltpu.VMEM((part, full), LOW),
            pltpu.VMEM((part, slots), LOW),
            pltpu.VMEM((slots, width), LOW),
            pltpu.SemaphoreType.DMA((9 + heads,)),
        ],
        micros=5.0,
        hbm=range(4, 11),
    )
    arrived = scatter_low((p1, p2, p3), "mp", mp_size)
    later = after(cotangent, arrived[0])
    cots = [pick(later, j)] + [swap(pick(later, j ^ k), "seq", seq_size, k) for k in range(1, 4)]
    attended = kernel(total_body, low(half, width), (own, *arrived), micros=0.5)
    own, p1, p2, p3, hidden, slope, normed, unit, inv = kernel(
        feed_body,
        [f32(half, width)]
        + [low(half, width)] * 3
        + [low(slots, hidden_here), f32(slots, hidden_here), low(slots, width), f32(slots, width), f32(slots, 128)],
        (ids, attended, *gather_low(attended, "mp", mp_size), row(attn_gain), row(attn_shift), up_weight)
        + (row(up_bias), down_weight, row(down_bias)),
        smem=1,
        scratch=[pltpu.VMEM((4, half, width), F32)],
        micros=3.0,
    )
    mixed = kernel(total_body, low(half, width), (own, *scatter_low((p1, p2, p3), "mp", mp_size)), micros=0.5)
    own, p1, p2, p3, *rest = kernel(
        feed_back_body,
        [f32(half, width)]
        + [low(half, width)] * 7
        + [low(slots, width), low(slots, hidden_here), f32(SMALL_ROWS, width)],
        (ids, mixed, *gather_low(mixed, "mp", mp_size), *cots, row(ffn_gain), row(ffn_shift), slope)
        + (down_weight, up_weight),
        smem=1,
        scratch=[pltpu.VMEM((4, half, width), F32), pltpu.VMEM((slots, width), LOW)],
        micros=3.0,
    )
    outputs, (grad_mixed, upward, small_feed) = rest[:4], rest[4:]
    arrived = scatter_low((p1, p2, p3), "mp", mp_size)
    feed_weights = lambda flip, out, event: kernel(
        functools.partial(feed_weights_body, flip),
        out,
        (ids, after(hidden, event), grad_mixed, normed, upward),
        smem=1,
        scratch=[pltpu.VMEM((slots, hidden_here), LOW)] * 2,
        micros=1.5,
    )
    feed_send = feed_weights(1, low(width, width), arrived[0])
    feed_arrived = swap(feed_send, "dp", dp_size, 1)
    feed_keep = feed_weights(0, f32(width, width), feed_send)
    grad_normed = kernel(total_body, low(half, width), (own, *arrived), micros=0.5)
    s = gather_low(grad_normed, "mp", mp_size)
    feed_own, *feed_blocks = plane_halves(ids, after(feed_keep, s[0]), feed_arrived)
    feed_landed = scatter_low(feed_blocks, "seq", seq_size)
    o0, o1, o2, o3, scores, stack, grad_attended, small_attend, sums = kernel(
        functools.partial(attend_back_body, heads, query_scale),
        [f32(block_len, width)]
        + [low(block_len, width)] * 3
        + [f32(heads, full, slots), low(3 * part, full), low(slots, width)]
        + [f32(SMALL_ROWS, width), f32(heads, 16, head)],
        (ids, grad_normed, *s, unit, inv, row(attn_gain), wq, wk, wv, out_weight, probs, qt, kt, vt),
        smem=1,
        scratch=[
            pltpu.VMEM((4, half, width), F32),
            pltpu.VMEM((3 * part, width), LOW),
            pltpu.VMEM((part, slots), LOW),
            pltpu.VMEM((part, full), LOW),
            pltpu.VMEM((full, width), F32),
        ],
        micros=6.0,
    )
    landed = scatter_low((o1, o2, o3), "mp", mp_size)
    rel = kernel(
        functools.partial(rel_body, heads, block_len, 32),
        f32(32, 128),
        (ids, after(scores, landed[0])),
        smem=1,
        scratch=[pltpu.VMEM((heads * BASES, 8, slots), F32)],
        micros=3.0,
    )
    half_rows = 2 * part + 2 * SMALL_ROWS + 32
    attend_keep, attend_send = kernel(
        attend_weights_body,
        [f32(half_rows, width), low(half_rows, width)],
        (ids, tokens, grad_attended, pooled_low, stack, ct, small_feed, small_attend, sums, rel),
        smem=1,
        scratch=[pltpu.VMEM((2, half_rows, width), F32)],
        micros=3.0,
    )
    attend_arrived = swap(attend_send, "dp", dp_size, 1)
    feed_total = plane_total(after(feed_own, attend_send), feed_landed, dp_size)
    feed_pieces = [feed_total] + gather_low(feed_total, "seq", seq_size)
    attend_own, *attend_blocks = plane_halves(ids, attend_keep, attend_arrived)
    attend_landed = scatter_low(attend_blocks, "seq", seq_size)

    quarter = block_len // 4
    q = kernel(quarters_body, [low(quarter, width)] * 4, (o0, *landed), micros=0.5)
    q = [q[0]] + scatter_low(q[1:], "seq", seq_size)
    joined = kernel(join_body, low(block_len, width), tuple(q), micros=0.5)
    spread = gather_low(joined, "mp", mp_size)
    attend_total = plane_total(after(attend_own, spread[0]), attend_landed, dp_size)
    attend_pieces = [attend_total] + gather_low(attend_total, "seq", seq_size)
    feed_mine = plane_join(ids, after(feed_pieces, attend_total))
    feed_other = swap(feed_mine, "dp", dp_size, 1)
    outputs = after(outputs, s[0])
    output_all = kernel(
        place_output_body,
        low(4, half, width),
        (ids, outputs[0], *scatter_low(outputs[1:], "seq", seq_size)),
        smem=1,
    )
    attend_mine = plane_join(ids, attend_pieces)
    attend_other = swap(attend_mine, "dp", dp_size, 1)
    input_all = kernel(place_body, f32(4, block_len, width), (ids, joined, *spread), smem=1)
    down_grad, up_grad = kernel(
        unpack_feed_body, [f32(width, width)] * 2, (ids, feed_mine, feed_other), smem=1, micros=2.0
    )
    tail_rows = half_rows - 2 * part
    dq, dk, dv, do, tail_a, tail_b = kernel(
        unpack_attend_body,
        [f32(part, width)] * 4 + [f32(tail_rows, width)] * 2,
        (ids, attend_mine, attend_other),
        smem=1,
        micros=1.5,
    )
    bias_sums = tail_b[: heads * SMALL_ROWS, :head].reshape(heads, SMALL_ROWS, head)
    rel_sums = tail_a[2 * SMALL_ROWS : 2 * SMALL_ROWS + heads * BASES, 0].reshape(heads, BASES)
    first = SMALL_ROWS
    return (
        output_all,
        input_all,
        dq.T,
        bias_sums[:, 0].reshape(-1),
        dk.T,
        dv.T,
        bias_sums[:, 8].reshape(-1),
        rel_sums,
        do,
        tail_a[first + 2],
        tail_a[first],
        tail_a[first + 1],
        up_grad,
        tail_a[3],
        down_grad,
        tail_a[2],
        tail_a[0],
        tail_a[1],
    )


def solution(mesh):
    return jax.shard_map(
        shards,
        mesh=mesh,
        in_specs=(
            P("dp", "seq", None),
            P("dp"),
            P(None, "mp"),
            P("mp"),
            P(None, "mp"),
            P(None, "mp"),
            P("mp"),
            P("mp", None),
            P("mp", None),
            P(),
            P(),
            P(),
            P(None, "mp"),
            P("mp"),
            P("mp", None),
            P(),
            P(),
            P(),
            P("dp", "seq", None),
        ),
        out_specs=(
            P("dp", "seq", None),
            P("dp", "seq", None),
            P(None, "mp"),
            P("mp"),
            P(None, "mp"),
            P(None, "mp"),
            P("mp"),
            P("mp", None),
            P("mp", None),
            P(),
            P(),
            P(),
            P(None, "mp"),
            P("mp"),
            P("mp", None),
            P(),
            P(),
            P(),
        ),
        check_vma=False,
    )
```

```python
import functools

import jax
import jax.numpy as jnp
from jax import lax
from jax.experimental import pallas as pl
from jax.experimental.pallas import tpu as pltpu
from jax.sharding import PartitionSpec as P

BASES = 8
EPSILON = 1e-05
MASKED_SCORE = -1e30
F32 = jnp.float32
LOW = jnp.bfloat16
SMALL_ROWS = 16
MIB = 1024 * 1024
DEPTH = 2


def f32(*shape):
    return jax.ShapeDtypeStruct(shape, F32)


def low(*shape):
    return jax.ShapeDtypeStruct(shape, LOW)


def kernel(body, outs, args, smem=0, scratch=(), micros=1.0, limit=16, hbm=()):
    in_specs = [pl.BlockSpec(memory_space=pltpu.SMEM)] * smem
    in_specs += [pl.BlockSpec(memory_space=pltpu.VMEM)] * (len(args) - smem)
    whole = pl.BlockSpec(memory_space=pltpu.VMEM)
    if isinstance(outs, list):
        out_specs = [pl.BlockSpec(memory_space=pltpu.HBM) if n in hbm else whole for n in range(len(outs))]
    else:
        out_specs = whole
    return pl.pallas_call(
        body,
        out_shape=outs,
        in_specs=in_specs,
        out_specs=out_specs,
        scratch_shapes=list(scratch),
        compiler_params=pltpu.CompilerParams(vmem_limit_bytes=limit * MIB),
        cost_estimate=pl.CostEstimate(
            flops=int(micros * 4e8), bytes_accessed=int(micros * 3e6), transcendentals=0
        ),
    )(*args)


def after(value, *events):
    return lax.optimization_barrier((value, events))[0]


def dot_of(dims, a, b):
    return lax.dot_general(a, b, (dims, ((), ())), preferred_element_type=F32)


mm = functools.partial(dot_of, ((1,), (0,)))
mm_nt = functools.partial(dot_of, ((1,), (1,)))
mm_tn = functools.partial(dot_of, ((0,), (0,)))


def swap(block, axis, size, k):
    return lax.ppermute(block, axis, [(s, s ^ k) for s in range(size)])


def deep(values):
    for _ in range(DEPTH):
        values = lax.optimization_barrier(values)
    return values


def gather_low(block, axis, size):
    landed = [swap(block, axis, size, k) for k in range(1, size)]
    return deep(landed) if axis == "mp" else landed


def scatter_low(blocks, axis, size):
    landed = [swap(blocks[k - 1], axis, size, k) for k in range(1, size)]
    return deep(landed) if axis == "mp" else landed


def pick(stacked, index):
    return lax.dynamic_index_in_dim(stacked, index, 0, keepdims=False)


def norm_stats(rows):
    center = rows - jnp.mean(rows, axis=-1, keepdims=True)
    scale_inv = lax.rsqrt(jnp.mean(center * center, axis=-1, keepdims=True) + EPSILON)
    return center * scale_inv, scale_inv


def norm_back(grad_out, normed, scale_inv, gain):
    grad_normed = grad_out * gain
    centered = grad_normed - jnp.mean(grad_normed, axis=-1, keepdims=True)
    return scale_inv * (centered - normed * jnp.mean(grad_normed * normed, axis=-1, keepdims=True))


def total_of(own_ref, arrived_refs):
    total = own_ref[...]
    for ref in arrived_refs:
        total = total + ref[...].astype(F32)
    return total


def pair_matrix(rows, cols, tall):
    r = lax.broadcasted_iota(jnp.int32, (rows, cols), 0)
    c = lax.broadcasted_iota(jnp.int32, (rows, cols), 1)
    hit = (r >> 1) == c if tall else r == (c >> 1)
    return jnp.where(hit, 0.5, 0.0).astype(LOW)


def distances(ids, chunk, rows, block_len, slots):
    j = ids[0]
    start = chunk * rows
    token = (j ^ (start // block_len)) * block_len + start % block_len
    token = token + lax.broadcasted_iota(jnp.int32, (rows, slots), 0)
    s = lax.broadcasted_iota(jnp.int32, (rows, slots), 1)
    half = block_len // 2
    slot = (j ^ (s // half)) * half + s % half
    return token, (token - 2 * slot).astype(F32)


def basis_of(distance, index, span):
    degree = index % (BASES // 2)
    inverse = 64.0 / (span * 4.0**degree)
    if index < BASES // 2:
        return jnp.exp(jnp.abs(distance) * (-inverse))
    return jnp.tanh(distance * inverse)


def bias_body(heads, block_len, rows, ids, rel, out):
    full, slots = out.shape[1:]

    def step(chunk, carry):
        token, distance = distances(ids, chunk, rows, block_len, slots)
        sums = [jnp.zeros((rows, slots), F32)] * heads
        for index in range(BASES):
            base = basis_of(distance, index, full)
            sums = [sums[h] + rel[h, index] * base for h in range(heads)]
        valid = token < ids[3]
        for h in range(heads):
            out[h, pl.ds(pl.multiple_of(chunk * rows, rows), rows), :] = jnp.where(valid, sums[h], MASKED_SCORE)
        return carry

    lax.fori_loop(0, full // rows, step, 0)


def rel_body(heads, block_len, rows, ids, scores_ref, out, acc):
    full, slots = scores_ref.shape[1:]
    acc[...] = jnp.zeros_like(acc)

    def step(chunk, carry):
        _, distance = distances(ids, chunk, rows, block_len, slots)
        at = pl.ds(pl.multiple_of(chunk * rows, rows), rows)
        grads = [scores_ref[h, at, :] for h in range(heads)]
        for index in range(BASES):
            base = basis_of(distance, index, full)
            for h in range(heads):
                acc[h * BASES + index] += jnp.sum((grads[h] * base).reshape(rows // 8, 8, slots), axis=0)
        return carry

    lax.fori_loop(0, full // rows, step, 0)
    for row in range(heads * BASES):
        col = jnp.sum(jnp.sum(acc[row], axis=0, keepdims=True), axis=1, keepdims=True)
        out[row : row + 1, :] = jnp.broadcast_to(col, (1, out.shape[1]))


def attend_body(heads, query_scale, ids, *refs):
    x = refs[:4]
    wq, wk, wv, wo, qb, vb, ob, bias, own_out, p1, p2, p3 = refs[4:16]
    hbm = refs[16:23]
    scr, probs_ref, qt, kt, vt, ct, pooled_low, sem = refs[23:]
    probs_hbm, qt_hbm, kt_hbm, vt_hbm, ct_hbm, pooled_hbm, x_hbm = hbm
    block_len = x[0].shape[0]
    half = block_len // 2
    head = wq.shape[0] // heads
    copies = []

    def send(source, target):
        copy = pltpu.make_async_copy(source, target, sem.at[len(copies)])
        copy.start()
        copies.append(copy)

    for b in range(4):
        send(x[b], x_hbm.at[pl.ds(b * block_len, block_len), :])
    pairs = pair_matrix(half, block_len, False)
    for b in range(4):
        span = slice(b * block_len, (b + 1) * block_len)
        kt[:, span] = mm_nt(wk[...], x[b][...]).astype(LOW)
        vt[:, span] = (mm_nt(wv[...], x[b][...]) + vb[...]).astype(LOW)
        pooled = mm(pairs, x[b][...])
        scr[b] = pooled
        pooled_low[b * half : (b + 1) * half, :] = pooled.astype(LOW)
    turn = ids[0] ^ ids[1]
    own_out[...] = scr[turn] + ob[...]
    qt[...] = ((mm_nt(wq[...], pooled_low[...]) + qb[...]) * query_scale).astype(LOW)
    send(kt, kt_hbm)
    send(vt, vt_hbm)
    send(qt, qt_hbm)
    send(pooled_low, pooled_hbm)
    for h in range(heads):
        at = slice(h * head, (h + 1) * head)
        scores = mm_tn(kt[at, :], qt[at, :]) + bias[h]
        grown = jnp.exp(scores - jnp.max(scores, axis=0, keepdims=True))
        probs = grown * (1.0 / jnp.sum(grown, axis=0, keepdims=True))
        probs_ref[h] = probs
        send(probs_ref.at[h], probs_hbm.at[h])
        ct[at, :] = mm(vt[at, :], probs.astype(LOW)).astype(LOW)
    send(ct, ct_hbm)
    result = mm_tn(ct[...], wo[...])
    for b in range(4):
        scr[b] = result[b * half : (b + 1) * half, :]
    own_out[...] += scr[turn]
    for k, out in ((1, p1), (2, p2), (3, p3)):
        out[...] = scr[turn ^ k].astype(LOW)
    for copy in copies:
        copy.wait()


def feed_body(ids, a0, a1, a2, a3, gain, shift, wu, ub, wd, db, own, p1, p2, p3, *refs):
    hidden_out, slope_out, normed_out, unit_out, inv_out, scr = refs
    rows, width = a0.shape
    turn = ids[0] ^ ids[1]
    for k, a in enumerate((a0, a1, a2, a3)):
        scr[turn ^ k] = a[...].astype(F32)
    unit, inv = norm_stats(scr[...].reshape(4 * rows, width))
    normed = unit * gain[...] + shift[...]
    unit_out[...] = unit
    inv_out[...] = jnp.broadcast_to(inv, inv_out.shape)
    normed_low = normed.astype(LOW)
    normed_out[...] = normed_low
    scr[...] = normed.reshape(scr.shape)
    own[...] = scr[turn] + db[...]
    up = mm(normed_low, wu[...]) + ub[...]
    phi = 0.5 * (1.0 + lax.erf(up * (0.5**0.5)))
    density = jnp.exp(up * up * -0.5) * 0.3989422804014327
    hidden = (up * phi).astype(LOW)
    hidden_out[...] = hidden
    slope_out[...] = phi + up * density
    scr[...] = mm(hidden, wd[...]).reshape(scr.shape)
    own[...] += scr[turn]
    for k, out in ((1, p1), (2, p2), (3, p3)):
        out[...] = scr[turn ^ k].astype(LOW)


def small_rows(*sums):
    return jnp.concatenate(list(sums) + [jnp.zeros((SMALL_ROWS - len(sums), sums[0].shape[1]), F32)])


def feed_back_body(ids, *refs):
    pieces, cots = refs[:4], refs[4:8]
    gain, shift, slope, wd, wu, own, p1, p2, p3 = refs[8:17]
    outs = refs[17:21]
    grad_out, upward_out, small_out, scr, low_scr = refs[21:]
    rows, width = own.shape
    slots = 4 * rows
    turn = ids[0] ^ ids[1]
    for k, piece in enumerate(pieces):
        scr[turn ^ k] = piece[...].astype(F32)
    unit, inv = norm_stats(scr[...].reshape(slots, width))
    s = lax.broadcasted_iota(jnp.int32, (slots, 1), 0)
    slot = (ids[0] ^ (s // rows)) * rows + s % rows
    valid = jnp.where(2 * slot < ids[3], 1.0, 0.0)
    output = ((unit * gain[...] + shift[...]) * valid).astype(LOW)
    for b in range(4):
        outs[b][...] = output[b * rows : (b + 1) * rows, :]
        low_scr[b * rows : (b + 1) * rows, :] = cots[b][...]
    top = low_scr[...].astype(F32) * valid
    grad = norm_back(top, unit, inv, gain[...])
    grad_low = grad.astype(LOW)
    grad_out[...] = grad_low
    scr[...] = grad.reshape(scr.shape)
    own[...] = scr[turn]
    hidden = mm_nt(grad_low, wd[...]).astype(LOW).astype(F32)
    upward = hidden * slope[...]
    upward_low = upward.astype(LOW)
    upward_out[...] = upward_low
    total = lambda a: jnp.sum(a, axis=0, keepdims=True)
    small_out[...] = small_rows(total(top * unit), total(top), total(grad), total(upward))
    scr[...] = mm_nt(upward_low, wu[...]).reshape(scr.shape)
    own[...] += scr[turn]
    for k, out in ((1, p1), (2, p2), (3, p3)):
        out[...] = scr[turn ^ k].astype(LOW)


def feed_product(which, hidden, grad, normed, upward, left, right, put):
    @pl.when(which == 0)
    def _():
        left[...] = hidden[...]
        right[...] = grad[...]

    @pl.when(which != 0)
    def _():
        left[...] = normed[...]
        right[...] = upward[...]

    step = 256
    for at in range(0, left.shape[1], step):
        put(slice(at, at + step), mm_tn(left[:, at : at + step], right[...]))


def first_step(base, total, kept, along1, along2):
    rows = along1[0] // 2
    block = lambda half, k: total(pl.ds(pl.multiple_of((4 * half + (base ^ k)) * rows, rows), rows))
    for n, (half, k) in enumerate(((0, 0), (0, 2), (1, 0), (1, 1))):
        kept[n * rows : (n + 1) * rows, :] = block(half, k)
    for (_, out), picks in ((along1, ((0, 1), (0, 3))), (along2, ((1, 2), (1, 3)))):
        for n, (half, k) in enumerate(picks):
            out[n * rows : (n + 1) * rows, :] = block(half, k).astype(LOW)


def second_step(kept, came1, came2, own, along1, along2):
    rows = along1.shape[0]
    part = lambda n: kept[n * rows : (n + 1) * rows, :]
    came = lambda ref, n: ref[n * rows : (n + 1) * rows, :].astype(F32)
    own[:rows, :] = part(0) + came(came1, 0)
    own[rows:, :] = part(2) + came(came2, 0)
    along2[...] = (part(1) + came(came1, 1)).astype(LOW)
    along1[...] = (part(3) + came(came2, 1)).astype(LOW)


def last_sums(own, came1, came2):
    rows = came1.shape[0]
    upper = own[:rows, :] + came2[...].astype(F32)
    lower = own[rows:, :] + came1[...].astype(F32)
    return upper.astype(LOW), lower.astype(LOW)


def join_half(base, mine1, mine2, came1, came2, out):
    rows = out.shape[0] // 8
    order = ((mine1, 0, (0, 2)), (came1, 0, (1, 3)), (mine2, 1, (0, 1)), (came2, 1, (2, 3)))
    for ref, half, ks in order:
        for n, k in enumerate(ks):
            at = pl.ds(pl.multiple_of((4 * half + (base ^ k)) * rows, rows), rows)
            out[at, :] = ref[n * rows : (n + 1) * rows, :]


def feed_send_body(ids, hidden, grad, normed, upward, out, left, right):
    def put(at, value):
        out[at, :] = value.astype(LOW)

    feed_product(1 - ids[2], hidden, grad, normed, upward, left, right, put)


def feed_keep_body(ids, hidden, grad, normed, upward, arrived, kept, along1, along2, left, right, scr):
    def put(at, value):
        scr[at, :] = value + arrived[at, :].astype(F32)

    feed_product(ids[2], hidden, grad, normed, upward, left, right, put)
    rows = along1.shape[0]
    first_step(ids[0], lambda at: scr[at, :], kept, (rows, along1), (rows, along2))


def feed_second_body(kept, came1, came2, own, along1, along2):
    second_step(kept, came1, came2, own, along1, along2)


def attend_first_body(ids, keep, arrived, rel, feed_own, came1, came2, kept, along1, along2, scr):
    rows = keep.shape[0] // 4
    scr[...] = keep[...] + arrived[...].astype(F32)
    scr[-rel.shape[0] :, : rel.shape[1]] = rel[...]
    first_step(ids[0], lambda at: scr[at, :], kept, (rows, along1), (rows, along2))
    upper, lower = last_sums(feed_own, came1, came2)
    for out, parts in ((along1, (lower, upper)), (along2, (upper, lower))):
        for n, part in enumerate(parts):
            out[rows + n * part.shape[0] : rows + (n + 1) * part.shape[0], :] = part


def attend_second_body(kept, came1, came2, own, along1, along2):
    rows = own.shape[0] // 2
    done = along1.shape[0] - rows
    at = slice(2 * rows, 2 * rows + done)
    along1[:done, :] = came2[at, :]
    along2[:done, :] = came1[at, :]
    second_step(kept, came1, came2, own, along1.at[done:, :], along2.at[done:, :])


def third_body(ids, own, sent1, sent2, near1, near2, came1, came2, feed, along1, along2):
    rows = along1.shape[0]
    done = came1.shape[0] - rows
    first, second = slice(2 * rows, 2 * rows + done), slice(2 * rows + done, 2 * (rows + done))
    upper = ((sent2, first), (near1, second), (near2, first), (came1, slice(0, done)))
    lower = ((sent1, first), (near1, first), (near2, second), (came2, slice(0, done)))
    for half, blocks in enumerate((upper, lower)):
        for k, (ref, at) in enumerate(blocks):
            to = pl.multiple_of((4 * half + (ids[0] ^ k)) * done, done)
            feed[pl.ds(to, done), :] = ref[at, :]
    along2[...], along1[...] = last_sums(own, came1.at[done:, :], came2.at[done:, :])


def fourth_body(sent1, sent2, came1, came2, along1, along2):
    rows = sent1.shape[0]
    along1[:rows, :] = sent2[...]
    along1[rows:, :] = came2[...]
    along2[:rows, :] = sent1[...]
    along2[rows:, :] = came1[...]


def attend_join_body(ids, sent1, sent2, came1, came2, out):
    join_half(ids[0], sent1, sent2, came1, came2, out)


def norm_back_body(ids, *refs):
    pieces, (unit, inv, gain, grad_out, low_out, small_out) = refs[:4], refs[4:]
    turn = ids[0] ^ ids[1]
    for k, piece in enumerate(pieces):
        grad_out[turn ^ k] = piece[...].astype(F32)
    grad_normed = grad_out[...].reshape(unit.shape)
    grad = norm_back(grad_normed, unit[...], inv[:, :1], gain[...])
    grad_out[...] = grad.reshape(grad_out.shape)
    low_out[...] = grad.astype(LOW)
    total = lambda a: jnp.sum(a, axis=0, keepdims=True)
    small_out[...] = small_rows(total(grad_normed * unit[...]), total(grad_normed), total(grad))


def row_sums(rows):
    high = rows.astype(LOW)
    rest = (rows - high.astype(F32)).astype(LOW)
    ones = jnp.ones((8, rows.shape[1]), LOW)
    return mm_nt(ones, high) + mm_nt(ones, rest)


def attend_back_body(heads, query_scale, ids, *refs):
    grad, grad_low, wq, wk, wv, wo, probs_ref, qt, kt, vt = refs[:10]
    o = refs[10:14]
    scores_out, stack, sums_out, weights, dct, repeated, result = refs[14:]
    part = wq.shape[0]
    head = part // heads
    slots, full = qt.shape[1], kt.shape[1]
    half, block_len = slots // 4, full // 4
    quarter = block_len // 4
    weights[:part, :] = wk[...]
    weights[part : 2 * part, :] = wv[...]
    weights[2 * part :, :] = wq[...]
    dct[...] = mm_nt(wo[...], grad_low[...]).astype(LOW)
    for h in range(heads):
        at = slice(h * head, (h + 1) * head)
        probs = probs_ref[h]
        grad_probs = mm_tn(vt[at, :], dct[at, :])
        grad_values = mm_nt(dct[at, :], probs.astype(LOW))
        scores = probs * (grad_probs - jnp.sum(probs * grad_probs, axis=0, keepdims=True))
        scores_out[h] = scores
        scores_low = scores.astype(LOW)
        grad_queries = mm(kt[at, :], scores_low) * query_scale
        stack[at, :] = mm_nt(qt[at, :], scores_low).astype(LOW)
        stack[part + h * head : part + (h + 1) * head, :] = grad_values.astype(LOW)
        stack[2 * part + h * head : 2 * part + (h + 1) * head, :slots] = grad_queries.astype(LOW)
        sums_out[h, :8, :] = row_sums(grad_queries)
        sums_out[h, 8:, :] = row_sums(grad_values)
    pairs = pair_matrix(half, block_len, False)
    for b in range(4):
        repeated[:, b * block_len : (b + 1) * block_len] = mm(
            stack[2 * part :, b * half : (b + 1) * half], pairs
        ).astype(LOW)
    result[...] = mm_tn(stack[: 2 * part, :], weights[: 2 * part, :]) + mm_tn(repeated[...], weights[2 * part :, :])
    spread = pair_matrix(quarter, quarter // 2, True)
    for b in range(4):
        to = slice(b * quarter, (b + 1) * quarter)
        rows = lambda k: pl.ds(pl.multiple_of(b * block_len + (ids[1] ^ k) * quarter, quarter), quarter)
        residual = grad[b, pl.ds(pl.multiple_of(ids[1] * (quarter // 2), quarter // 2), quarter // 2), :]
        high = residual.astype(LOW)
        rest = (residual - high.astype(F32)).astype(LOW)
        o[0][to, :] = result[rows(0), :] + (mm(spread, high) + mm(spread, rest))
        for k in range(1, 4):
            o[k][to, :] = result[rows(k), :].astype(LOW)


def attend_weights_body(ids, x, grad, pooled_low, stack, ct, small_feed, small_attend, sums, keep, send, scr):
    part, slots = ct.shape
    heads = sums.shape[0]
    scr[0, :part, :] = mm(stack[2 * part :, :slots], pooled_low[...])
    scr[0, part : 2 * part, :] = mm(stack[:part, :], x[...])
    scr[1, :part, :] = mm(stack[part : 2 * part, :], x[...])
    scr[1, part : 2 * part, :] = mm(ct[...], grad[...])
    scr[:, 2 * part :, :] = jnp.zeros((2, scr.shape[1] - 2 * part, scr.shape[2]), F32)
    scr[0, 2 * part : 2 * part + SMALL_ROWS, :] = small_feed[...]
    scr[0, 2 * part + SMALL_ROWS : 2 * part + 2 * SMALL_ROWS, :] = small_attend[...]
    for h in range(heads):
        scr[1, 2 * part + h * SMALL_ROWS : 2 * part + (h + 1) * SMALL_ROWS, : sums.shape[2]] = sums[h]
    keep[...] = scr[ids[2]]
    send[...] = scr[1 - ids[2]].astype(LOW)


def total_body(r1, r2, r3, own, out):
    out[...] = total_of(own, (r1, r2, r3)).astype(LOW)


def unpack_feed_body(ids, mine, other, first, second):
    for c, (a, b) in ((0, (mine, other)), (1, (other, mine))):

        @pl.when(ids[2] == c)
        def _(a=a, b=b):
            first[...] = a[...].astype(F32)
            second[...] = b[...].astype(F32)


def unpack_attend_body(ids, mine, other, dq, dk, dv, do, tail_a, tail_b):
    part = dq.shape[0]
    for c, (a, b) in ((0, (mine, other)), (1, (other, mine))):

        @pl.when(ids[2] == c)
        def _(a=a, b=b):
            dq[...] = a[:part, :].astype(F32)
            dk[...] = a[part : 2 * part, :].astype(F32)
            tail_a[...] = a[2 * part :, :].astype(F32)
            dv[...] = b[:part, :].astype(F32)
            do[...] = b[part : 2 * part, :].astype(F32)
            tail_b[...] = b[2 * part :, :].astype(F32)


def quarters_body(r1, r2, r3, own, n1, n2, n3, q0, q1, q2, q3):
    total = total_of(own, (r1, r2, r3)).astype(LOW)
    rows = q0.shape[0]
    q0[...] = total[:rows]
    for b, (q, n) in enumerate(((q1, n1), (q2, n2), (q3, n3)), 1):
        q[:rows, :] = total[b * rows : (b + 1) * rows]
        q[rows:, :] = n[...]


def join_body(ids, q0, q1, q2, q3, n0, joined, output):
    rows = q0.shape[0]
    for b, q in enumerate((q0, q1, q2, q3)):
        joined[b * rows : (b + 1) * rows, :] = q[:rows, :]
    output[ids[0]] = n0[...]
    for b, q in ((1, q1), (2, q2), (3, q3)):
        output[ids[0] ^ b] = q[rows:, :]


def place_body(ids, t0, t1, t2, t3, out):
    rows = out.shape[1] // 4
    for k, t in enumerate((t0, t1, t2, t3)):
        at = pl.ds(pl.multiple_of((ids[1] ^ k) * rows, rows), rows)
        for b in range(4):
            out[ids[0] ^ b, at, :] = t[b * rows : (b + 1) * rows, :].astype(out.dtype)


def dp_sum(values, dp_size):
    step = 2
    while step < dp_size:
        values = [
            (v.astype(F32) + swap(v, "dp", dp_size, step).astype(F32)).astype(v.dtype) for v in values
        ]
        step *= 2
    return values


def both_ways(along1, along2, size):
    return swap(along1, "seq", size, 1), swap(along2, "seq", size, 2)


def shards(
    inputs,
    lengths,
    query_weight,
    query_bias,
    key_weight,
    value_weight,
    value_bias,
    rel_weight,
    out_weight,
    out_bias,
    attn_gain,
    attn_shift,
    up_weight,
    up_bias,
    down_weight,
    down_bias,
    ffn_gain,
    ffn_shift,
    cotangent,
):
    seq_size, dp_size, mp_size = (lax.axis_size(a) for a in ("seq", "dp", "mp"))
    j, m, c = lax.axis_index("seq"), lax.axis_index("mp"), lax.axis_index("dp") % 2
    sentences, block_len, width = inputs.shape
    assert sentences == seq_size == mp_size == 4 and dp_size % 2 == 0
    half = block_len // 2
    full, slots = 4 * block_len, 4 * half
    heads = rel_weight.shape[0]
    part = query_weight.shape[1]
    head = part // heads
    hidden_here = up_weight.shape[1]
    assert hidden_here == width
    query_scale = head ** (-0.5)
    row = lambda v: v.reshape(1, -1)
    column = lambda v: v.reshape(-1, 1)
    ids = jnp.stack([j, m, c, pick(lengths, j)]).astype(jnp.int32)
    wq, wk, wv = query_weight.T, key_weight.T, value_weight.T

    x = [pick(inputs, j)] + [swap(pick(inputs, j ^ k), "seq", seq_size, k) for k in range(1, 4)]
    bias = kernel(
        functools.partial(bias_body, heads, block_len, 32), f32(heads, full, slots), (ids, rel_weight), smem=2, micros=3.0
    )
    own, p1, p2, p3, probs, qt, kt, vt, ct, pooled_low, tokens = kernel(
        functools.partial(attend_body, heads, query_scale),
        [f32(half, width)]
        + [low(half, width)] * 3
        + [f32(heads, full, slots), low(part, slots), low(part, full), low(part, full), low(part, slots)]
        + [low(slots, width), low(full, width)],
        (ids, *x, wq, wk, wv, out_weight, column(query_bias), column(value_bias), row(out_bias), bias),
        smem=1,
        scratch=[
            pltpu.VMEM((4, half, width), F32),
            pltpu.VMEM((heads, full, slots), F32),
            pltpu.VMEM((part, slots), LOW),
            pltpu.VMEM((part, full), LOW),
            pltpu.VMEM((part, full), LOW),
            pltpu.VMEM((part, slots), LOW),
            pltpu.VMEM((slots, width), LOW),
            pltpu.SemaphoreType.DMA((9 + heads,)),
        ],
        micros=5.0,
        hbm=range(4, 11),
    )
    arrived = scatter_low((p1, p2, p3), "mp", mp_size)
    attended = kernel(total_body, low(half, width), (*arrived, own), micros=0.5)
    later = after(cotangent, attended)
    cots = [pick(later, j)] + [swap(pick(later, j ^ k), "seq", seq_size, k) for k in range(1, 4)]
    own, p1, p2, p3, hidden, slope, normed, unit, inv = kernel(
        feed_body,
        [f32(half, width)]
        + [low(half, width)] * 3
        + [low(slots, hidden_here), f32(slots, hidden_here), low(slots, width), f32(slots, width), f32(slots, 128)],
        (ids, attended, *gather_low(attended, "mp", mp_size), row(attn_gain), row(attn_shift), up_weight)
        + (row(up_bias), down_weight, row(down_bias)),
        smem=1,
        scratch=[pltpu.VMEM((4, half, width), F32)],
        micros=3.0,
    )
    p1, p2, p3 = after((p1, p2, p3), cots)
    mixed = kernel(total_body, low(half, width), (*scatter_low((p1, p2, p3), "mp", mp_size), own), micros=0.5)
    own, p1, p2, p3, *rest = kernel(
        feed_back_body,
        [f32(half, width)]
        + [low(half, width)] * 7
        + [low(slots, width), low(slots, hidden_here), f32(SMALL_ROWS, width)],
        (ids, mixed, *gather_low(mixed, "mp", mp_size), *cots, row(ffn_gain), row(ffn_shift), slope)
        + (down_weight, up_weight),
        smem=1,
        scratch=[pltpu.VMEM((4, half, width), F32), pltpu.VMEM((slots, width), LOW)],
        micros=3.0,
    )
    outputs, (grad_mixed, upward, small_feed) = rest[:4], rest[4:]
    operands = (hidden, grad_mixed, normed, upward)
    sides = [pltpu.VMEM((slots, width), LOW)] * 2
    feed_send = kernel(
        feed_send_body, low(width, width), (ids, *operands), smem=1, scratch=sides, micros=1.2
    )
    feed_arrived = swap(feed_send, "dp", dp_size, 1)
    arrived = scatter_low((p1, p2, p3), "mp", mp_size)
    grad_normed = kernel(total_body, low(half, width), (*arrived, after(own, feed_arrived)), micros=0.5)
    rows = width // 8
    feed_kept, along1, along2 = kernel(
        feed_keep_body,
        [f32(4 * rows, width)] + [low(2 * rows, width)] * 2,
        (ids, *operands, after(feed_arrived, grad_normed)),
        smem=1,
        scratch=sides + [pltpu.VMEM((width, width), F32)],
        micros=1.5,
    )
    s = gather_low(after(grad_normed, along1), "mp", mp_size)
    came = both_ways(along1, along2, seq_size)
    grad, grad_attended, small_attend = kernel(
        norm_back_body,
        [f32(4, half, width), low(slots, width), f32(SMALL_ROWS, width)],
        (ids, grad_normed, *s, unit, inv, row(attn_gain)),
        smem=1,
        micros=6.5,
    )
    feed_own, along1, along2 = kernel(
        feed_second_body, [f32(2 * rows, width)] + [low(rows, width)] * 2, (feed_kept, came[0], after(came[1], grad_attended)), micros=0.2
    )
    came = both_ways(along1, along2, seq_size)
    own_input, o1, o2, o3, scores, stack, sums = kernel(
        functools.partial(attend_back_body, heads, query_scale),
        [f32(block_len, width)]
        + [low(block_len, width)] * 3
        + [f32(heads, full, slots), low(3 * part, full), f32(heads, 16, head)],
        (ids, grad, grad_attended, wq, wk, wv, out_weight, probs, qt, kt, after(vt, along1)),
        smem=1,
        scratch=[
            pltpu.VMEM((3 * part, width), LOW),
            pltpu.VMEM((part, slots), LOW),
            pltpu.VMEM((part, full), LOW),
            pltpu.VMEM((full, width), F32),
        ],
        micros=6.0,
    )
    rel = kernel(
        functools.partial(rel_body, heads, block_len, 32),
        f32(32, 128),
        (ids, scores),
        smem=1,
        scratch=[pltpu.VMEM((heads * BASES, 8, slots), F32)],
        micros=0.1,
    )
    half_rows = 2 * part + 128
    attend_keep, attend_send = kernel(
        attend_weights_body,
        [f32(half_rows, width), low(half_rows, width)],
        (ids, after(tokens, came), grad_attended, pooled_low, stack, ct, small_feed, small_attend, sums),
        smem=1,
        scratch=[pltpu.VMEM((2, half_rows, width), F32)],
        micros=1.5,
    )
    landed = scatter_low((o1, o2, o3), "mp", mp_size)
    attend_arrived = swap(attend_send, "dp", dp_size, 1)
    few = half_rows // 8
    attend_kept, sent1, sent2 = kernel(
        attend_first_body,
        [f32(4 * few, width)] + [low(2 * few + 2 * rows, width)] * 2,
        (ids, attend_keep, attend_arrived, rel, feed_own, *came),
        smem=1,
        scratch=[pltpu.VMEM((half_rows, width), F32)],
        micros=0.1,
    )
    early = both_ways(sent1, sent2, seq_size)
    quarter = block_len // 4
    q0, *q = kernel(
        quarters_body,
        [low(quarter, width)] + [low(quarter + half, width)] * 3,
        (*landed, own_input, *outputs[1:]),
        micros=8.0,
    )
    attend_own, along1, along2 = kernel(
        attend_second_body,
        [f32(2 * few, width)] + [low(rows + few, width)] * 2,
        (attend_kept, early[0], after(early[1], q0)),
        micros=0.2,
    )
    q = deep(scatter_low(q, "seq", seq_size))
    came = both_ways(along1, along2, seq_size)
    joined, output_all = kernel(
        join_body,
        [low(block_len, width), low(4, half, width)],
        (ids, q0, *q, outputs[0]),
        smem=1,
        micros=2.8,
    )
    spread = gather_low(joined, "mp", mp_size)
    feed_mine, along1, along2 = dp_sum(
        kernel(
            third_body,
            [low(width, width)] + [low(few, width)] * 2,
            (ids, after(attend_own, joined), sent1, sent2, *early, *came),
            smem=1,
            micros=0.2,
        ),
        dp_size,
    )
    feed_other = swap(feed_mine, "dp", dp_size, 1)
    sent = (after(along1, feed_other), along2)
    down_grad, up_grad = kernel(
        unpack_feed_body, [f32(width, width)] * 2, (ids, feed_mine, feed_other), smem=1, micros=0.1
    )
    along1, along2 = kernel(
        fourth_body, [low(2 * few, width)] * 2, (*sent, *after(both_ways(*sent, seq_size), down_grad)), micros=0.1
    )
    came = both_ways(along1, along2, seq_size)
    input_all = kernel(
        place_body, f32(4, block_len, width), (ids, joined, *spread), smem=1, micros=3.0
    )
    attend_mine = kernel(
        attend_join_body,
        low(half_rows, width),
        (ids, along1, along2, came[0], after(came[1], input_all)),
        smem=1,
        micros=0.2,
    )
    attend_other = swap(attend_mine, "dp", dp_size, 1)
    tail_rows = half_rows - 2 * part
    dq, dk, dv, do, tail_a, tail_b = kernel(
        unpack_attend_body,
        [f32(part, width)] * 4 + [f32(tail_rows, width)] * 2,
        (ids, attend_mine, attend_other),
        smem=1,
        micros=1.5,
    )
    bias_sums = tail_b[: heads * SMALL_ROWS, :head].reshape(heads, SMALL_ROWS, head)
    rel_sums = (tail_a + tail_b)[tail_rows - 32 : tail_rows - 32 + heads * BASES, 0].reshape(heads, BASES)
    first = SMALL_ROWS
    return (
        output_all,
        input_all,
        dq.T,
        bias_sums[:, 0].reshape(-1),
        dk.T,
        dv.T,
        bias_sums[:, 8].reshape(-1),
        rel_sums,
        do,
        tail_a[first + 2],
        tail_a[first],
        tail_a[first + 1],
        up_grad,
        tail_a[3],
        down_grad,
        tail_a[2],
        tail_a[0],
        tail_a[1],
    )


def solution(mesh):
    return jax.shard_map(
        shards,
        mesh=mesh,
        in_specs=(
            P("dp", "seq", None),
            P("dp"),
            P(None, "mp"),
            P("mp"),
            P(None, "mp"),
            P(None, "mp"),
            P("mp"),
            P("mp", None),
            P("mp", None),
            P(),
            P(),
            P(),
            P(None, "mp"),
            P("mp"),
            P("mp", None),
            P(),
            P(),
            P(),
            P("dp", "seq", None),
        ),
        out_specs=(
            P("dp", "seq", None),
            P("dp", "seq", None),
            P(None, "mp"),
            P("mp"),
            P(None, "mp"),
            P(None, "mp"),
            P("mp"),
            P("mp", None),
            P("mp", None),
            P(),
            P(),
            P(),
            P(None, "mp"),
            P("mp"),
            P("mp", None),
            P(),
            P(),
            P(),
        ),
        check_vma=False,
    )
```

```python
import functools

import jax
import jax.numpy as jnp
from jax import lax
from jax.experimental import pallas as pl
from jax.experimental.pallas import tpu as pltpu
from jax.sharding import PartitionSpec as P

BASES = 8
EPSILON = 1e-05
MASKED_SCORE = -1e30
F32 = jnp.float32
LOW = jnp.bfloat16
SMALL_ROWS = 16
MIB = 1024 * 1024
DEPTH = 2


def f32(*shape):
    return jax.ShapeDtypeStruct(shape, F32)


def low(*shape):
    return jax.ShapeDtypeStruct(shape, LOW)


def kernel(body, outs, args, smem=0, scratch=(), micros=1.0, limit=16, hbm=(), reused=0):
    in_specs = [pl.BlockSpec(memory_space=pltpu.SMEM)] * smem
    in_specs += [pl.BlockSpec(memory_space=pltpu.VMEM)] * (len(args) - smem - reused)
    in_specs += [pl.BlockSpec(memory_space=pltpu.HBM)] * reused
    whole = pl.BlockSpec(memory_space=pltpu.VMEM)
    if isinstance(outs, list):
        out_specs = [pl.BlockSpec(memory_space=pltpu.HBM) if n in hbm else whole for n in range(len(outs))]
    else:
        out_specs = whole
    return pl.pallas_call(
        body,
        out_shape=outs,
        in_specs=in_specs,
        out_specs=out_specs,
        scratch_shapes=list(scratch),
        input_output_aliases={len(args) - reused + n: n for n in range(reused)},
        compiler_params=pltpu.CompilerParams(vmem_limit_bytes=limit * MIB),
        cost_estimate=pl.CostEstimate(
            flops=int(micros * 4e8), bytes_accessed=int(micros * 3e6), transcendentals=0
        ),
    )(*args)


def after(value, *events):
    return lax.optimization_barrier((value, events))[0]


def dot_of(dims, a, b):
    return lax.dot_general(a, b, (dims, ((), ())), preferred_element_type=F32)


mm = functools.partial(dot_of, ((1,), (0,)))
mm_nt = functools.partial(dot_of, ((1,), (1,)))
mm_tn = functools.partial(dot_of, ((0,), (0,)))


def swap(block, axis, size, k):
    return lax.ppermute(block, axis, [(s, s ^ k) for s in range(size)])


def deep(values):
    for _ in range(DEPTH):
        values = lax.optimization_barrier(values)
    return values


def gather_low(block, axis, size):
    landed = [swap(block, axis, size, k) for k in range(1, size)]
    return deep(landed) if axis == "mp" else landed


def scatter_low(blocks, axis, size):
    landed = [swap(blocks[k - 1], axis, size, k) for k in range(1, size)]
    return deep(landed) if axis == "mp" else landed


def pick(stacked, index):
    return lax.dynamic_index_in_dim(stacked, index, 0, keepdims=False)


def norm_stats(rows):
    center = rows - jnp.mean(rows, axis=-1, keepdims=True)
    scale_inv = lax.rsqrt(jnp.mean(center * center, axis=-1, keepdims=True) + EPSILON)
    return center * scale_inv, scale_inv


def norm_back(grad_out, normed, scale_inv, gain):
    grad_normed = grad_out * gain
    centered = grad_normed - jnp.mean(grad_normed, axis=-1, keepdims=True)
    return scale_inv * (centered - normed * jnp.mean(grad_normed * normed, axis=-1, keepdims=True))


def total_of(own_ref, arrived_refs):
    total = own_ref[...]
    for ref in arrived_refs:
        total = total + ref[...].astype(F32)
    return total


def pair_matrix(rows, cols, tall):
    r = lax.broadcasted_iota(jnp.int32, (rows, cols), 0)
    c = lax.broadcasted_iota(jnp.int32, (rows, cols), 1)
    hit = (r >> 1) == c if tall else r == (c >> 1)
    return jnp.where(hit, 0.5, 0.0).astype(LOW)


def distances(ids, chunk, rows, block_len, slots):
    j = ids[0]
    start = chunk * rows
    token = (j ^ (start // block_len)) * block_len + start % block_len
    token = token + lax.broadcasted_iota(jnp.int32, (rows, slots), 0)
    s = lax.broadcasted_iota(jnp.int32, (rows, slots), 1)
    half = block_len // 2
    slot = (j ^ (s // half)) * half + s % half
    return token, (token - 2 * slot).astype(F32)


def basis_of(distance, index, span):
    degree = index % (BASES // 2)
    inverse = 64.0 / (span * 4.0**degree)
    if index < BASES // 2:
        return jnp.exp(jnp.abs(distance) * (-inverse))
    return jnp.tanh(distance * inverse)


def bias_body(heads, block_len, rows, ids, rel, out):
    full, slots = out.shape[1:]

    def step(chunk, carry):
        token, distance = distances(ids, chunk, rows, block_len, slots)
        sums = [jnp.zeros((rows, slots), F32)] * heads
        for index in range(BASES):
            base = basis_of(distance, index, full)
            sums = [sums[h] + rel[h, index] * base for h in range(heads)]
        valid = token < ids[3]
        for h in range(heads):
            out[h, pl.ds(pl.multiple_of(chunk * rows, rows), rows), :] = jnp.where(valid, sums[h], MASKED_SCORE)
        return carry

    lax.fori_loop(0, full // rows, step, 0)


def rel_body(heads, block_len, rows, ids, scores_ref, out, acc):
    full, slots = scores_ref.shape[1:]
    acc[...] = jnp.zeros_like(acc)

    def step(chunk, carry):
        _, distance = distances(ids, chunk, rows, block_len, slots)
        at = pl.ds(pl.multiple_of(chunk * rows, rows), rows)
        grads = [scores_ref[h, at, :] for h in range(heads)]
        for index in range(BASES):
            base = basis_of(distance, index, full)
            for h in range(heads):
                acc[h * BASES + index] += jnp.sum((grads[h] * base).reshape(rows // 8, 8, slots), axis=0)
        return carry

    lax.fori_loop(0, full // rows, step, 0)
    for row in range(heads * BASES):
        col = jnp.sum(jnp.sum(acc[row], axis=0, keepdims=True), axis=1, keepdims=True)
        out[row : row + 1, :] = jnp.broadcast_to(col, (1, out.shape[1]))


def attend_body(heads, query_scale, ids, *refs):
    x = refs[:4]
    wq, wk, wv, wo, qb, vb, ob, bias, own_out, p1, p2, p3 = refs[4:16]
    hbm = refs[16:23]
    scr, probs_ref, qt, kt, vt, ct, pooled_low, sem = refs[23:]
    probs_hbm, qt_hbm, kt_hbm, vt_hbm, ct_hbm, pooled_hbm, x_hbm = hbm
    block_len = x[0].shape[0]
    half = block_len // 2
    head = wq.shape[0] // heads
    copies = []

    def send(source, target):
        copy = pltpu.make_async_copy(source, target, sem.at[len(copies)])
        copy.start()
        copies.append(copy)

    for b in range(4):
        send(x[b], x_hbm.at[pl.ds(b * block_len, block_len), :])
    pairs = pair_matrix(half, block_len, False)
    for b in range(4):
        span = slice(b * block_len, (b + 1) * block_len)
        kt[:, span] = mm_nt(wk[...], x[b][...]).astype(LOW)
        vt[:, span] = (mm_nt(wv[...], x[b][...]) + vb[...]).astype(LOW)
        pooled = mm(pairs, x[b][...])
        scr[b] = pooled
        pooled_low[b * half : (b + 1) * half, :] = pooled.astype(LOW)
    turn = ids[0] ^ ids[1]
    own_out[...] = scr[turn] + ob[...]
    qt[...] = ((mm_nt(wq[...], pooled_low[...]) + qb[...]) * query_scale).astype(LOW)
    send(kt, kt_hbm)
    send(vt, vt_hbm)
    send(qt, qt_hbm)
    send(pooled_low, pooled_hbm)
    for h in range(heads):
        at = slice(h * head, (h + 1) * head)
        scores = mm_tn(kt[at, :], qt[at, :]) + bias[h]
        grown = jnp.exp(scores - jnp.max(scores, axis=0, keepdims=True))
        probs = grown * (1.0 / jnp.sum(grown, axis=0, keepdims=True))
        probs_ref[h] = probs
        send(probs_ref.at[h], probs_hbm.at[h])
        ct[at, :] = mm(vt[at, :], probs.astype(LOW)).astype(LOW)
    send(ct, ct_hbm)
    result = mm_tn(ct[...], wo[...])
    for b in range(4):
        scr[b] = result[b * half : (b + 1) * half, :]
    own_out[...] += scr[turn]
    for k, out in ((1, p1), (2, p2), (3, p3)):
        out[...] = scr[turn ^ k].astype(LOW)
    for copy in copies:
        copy.wait()


def feed_body(ids, a0, a1, a2, a3, gain, shift, wu, ub, wd, db, own, p1, p2, p3, *refs):
    hidden_out, slope_out, normed_out, unit_out, inv_out, scr = refs
    rows, width = a0.shape
    turn = ids[0] ^ ids[1]
    for k, a in enumerate((a0, a1, a2, a3)):
        scr[turn ^ k] = a[...].astype(F32)
    unit, inv = norm_stats(scr[...].reshape(4 * rows, width))
    normed = unit * gain[...] + shift[...]
    unit_out[...] = unit
    inv_out[...] = jnp.broadcast_to(inv, inv_out.shape)
    normed_low = normed.astype(LOW)
    normed_out[...] = normed_low
    scr[...] = normed.reshape(scr.shape)
    own[...] = scr[turn] + db[...]
    up = mm(normed_low, wu[...]) + ub[...]
    phi = 0.5 * (1.0 + lax.erf(up * (0.5**0.5)))
    density = jnp.exp(up * up * -0.5) * 0.3989422804014327
    hidden = (up * phi).astype(LOW)
    hidden_out[...] = hidden
    slope_out[...] = phi + up * density
    scr[...] = mm(hidden, wd[...]).reshape(scr.shape)
    own[...] += scr[turn]
    for k, out in ((1, p1), (2, p2), (3, p3)):
        out[...] = scr[turn ^ k].astype(LOW)


def small_rows(*sums):
    return jnp.concatenate(list(sums) + [jnp.zeros((SMALL_ROWS - len(sums), sums[0].shape[1]), F32)])


def feed_back_body(ids, *refs):
    pieces, cots = refs[:4], refs[4:8]
    gain, shift, slope, wd, wu, own, p1, p2, p3 = refs[8:17]
    outs = refs[17:21]
    grad_out, upward_out, small_out, scr, low_scr = refs[21:]
    rows, width = own.shape
    slots = 4 * rows
    turn = ids[0] ^ ids[1]
    for k, piece in enumerate(pieces):
        scr[turn ^ k] = piece[...].astype(F32)
    unit, inv = norm_stats(scr[...].reshape(slots, width))
    s = lax.broadcasted_iota(jnp.int32, (slots, 1), 0)
    slot = (ids[0] ^ (s // rows)) * rows + s % rows
    valid = jnp.where(2 * slot < ids[3], 1.0, 0.0)
    output = ((unit * gain[...] + shift[...]) * valid).astype(LOW)
    for b in range(4):
        outs[b][...] = output[b * rows : (b + 1) * rows, :]
        low_scr[b * rows : (b + 1) * rows, :] = cots[b][...]
    top = low_scr[...].astype(F32) * valid
    grad = norm_back(top, unit, inv, gain[...])
    grad_low = grad.astype(LOW)
    grad_out[...] = grad_low
    scr[...] = grad.reshape(scr.shape)
    own[...] = scr[turn]
    hidden = mm_nt(grad_low, wd[...]).astype(LOW).astype(F32)
    upward = hidden * slope[...]
    upward_low = upward.astype(LOW)
    upward_out[...] = upward_low
    total = lambda a: jnp.sum(a, axis=0, keepdims=True)
    small_out[...] = small_rows(total(top * unit), total(top), total(grad), total(upward))
    scr[...] = mm_nt(upward_low, wu[...]).reshape(scr.shape)
    own[...] += scr[turn]
    for k, out in ((1, p1), (2, p2), (3, p3)):
        out[...] = scr[turn ^ k].astype(LOW)


def feed_product(which, hidden, grad, normed, upward, left, right, put):
    @pl.when(which == 0)
    def _():
        left[...] = hidden[...]
        right[...] = grad[...]

    @pl.when(which != 0)
    def _():
        left[...] = normed[...]
        right[...] = upward[...]

    step = 256
    for at in range(0, left.shape[1], step):
        put(slice(at, at + step), mm_tn(left[:, at : at + step], right[...]))


def first_step(base, total, kept, along1, along2):
    rows = along1[0] // 2
    block = lambda half, k: total(pl.ds(pl.multiple_of((4 * half + (base ^ k)) * rows, rows), rows))
    for n, (half, k) in enumerate(((0, 0), (0, 2), (1, 0), (1, 1))):
        kept[n * rows : (n + 1) * rows, :] = block(half, k)
    for (_, out), picks in ((along1, ((0, 1), (0, 3))), (along2, ((1, 2), (1, 3)))):
        for n, (half, k) in enumerate(picks):
            out[n * rows : (n + 1) * rows, :] = block(half, k).astype(LOW)


def second_step(kept, came1, came2, own, along1, along2):
    rows = along1.shape[0]
    part = lambda n: kept[n * rows : (n + 1) * rows, :]
    came = lambda ref, n: ref[n * rows : (n + 1) * rows, :].astype(F32)
    own[:rows, :] = part(0) + came(came1, 0)
    own[rows:, :] = part(2) + came(came2, 0)
    along2[...] = (part(1) + came(came1, 1)).astype(LOW)
    along1[...] = (part(3) + came(came2, 1)).astype(LOW)


def last_sums(own, came1, came2):
    rows = came1.shape[0]
    upper = own[:rows, :] + came2[...].astype(F32)
    lower = own[rows:, :] + came1[...].astype(F32)
    return upper.astype(LOW), lower.astype(LOW)


def join_half(base, mine1, mine2, came1, came2, out):
    rows = out.shape[0] // 8
    order = ((mine1, 0, (0, 2)), (came1, 0, (1, 3)), (mine2, 1, (0, 1)), (came2, 1, (2, 3)))
    for ref, half, ks in order:
        for n, k in enumerate(ks):
            at = pl.ds(pl.multiple_of((4 * half + (base ^ k)) * rows, rows), rows)
            out[at, :] = ref[n * rows : (n + 1) * rows, :]


def feed_send_body(ids, hidden, grad, normed, upward, out, left, right):
    def put(at, value):
        out[at, :] = value.astype(LOW)

    feed_product(1 - ids[2], hidden, grad, normed, upward, left, right, put)


def feed_keep_body(ids, hidden, grad, normed, upward, arrived, kept, along1, along2, left, right, scr):
    def put(at, value):
        scr[at, :] = value + arrived[at, :].astype(F32)

    feed_product(ids[2], hidden, grad, normed, upward, left, right, put)
    rows = along1.shape[0]
    first_step(ids[0], lambda at: scr[at, :], kept, (rows, along1), (rows, along2))


def step_a_body(ids, keep, arrived, rel, feed_kept, came1, came2, kept, feed_own, along1, along2, scr):
    rows = keep.shape[0] // 4
    scr[...] = keep[...] + arrived[...].astype(F32)
    scr[-rel.shape[0] :, : rel.shape[1]] = rel[...]
    first_step(ids[0], lambda at: scr[at, :], kept, (rows, along1), (rows, along2))
    second_step(feed_kept, came1, came2, feed_own, along1.at[rows:, :], along2.at[rows:, :])


def step_b_body(kept, feed_own, came1, came2, own, along1, along2):
    few = own.shape[0] // 2
    skip = 2 * few
    first = slice(0, skip)
    second_step(
        kept, came1.at[first, :], came2.at[first, :], own, along1.at[slice(0, few), :], along2.at[slice(0, few), :]
    )
    upper, lower = last_sums(feed_own, came1.at[skip:, :], came2.at[skip:, :])
    for out, parts in ((along1, (lower, upper)), (along2, (upper, lower))):
        for n, part in enumerate(parts):
            out[few + n * part.shape[0] : few + (n + 1) * part.shape[0], :] = part


def step_c_body(own, came1, came2, along1, along2):
    first = slice(0, along1.shape[0])
    along2[...], along1[...] = last_sums(own, came1.at[first, :], came2.at[first, :])


def step_d_body(mid1, mid2, came1, came2, near1, near2, along1, along2):
    few = mid1.shape[0]
    done = along1.shape[0] - 2 * few
    for out, own, came, near in ((along1, mid2, came2, near2), (along2, mid1, came1, near1)):
        out[:few, :] = own[...]
        out[few : 2 * few, :] = came[...]
        out[2 * few :, :] = near[few : few + done, :]


def feed_join_body(ids, sent1, sent2, near1, near2, came1, came2, out):
    rows = out.shape[0] // 8
    few = sent1.shape[0] - 2 * rows
    skip = came1.shape[0] - rows
    first, second, last = slice(few, few + rows), slice(few + rows, few + 2 * rows), slice(skip, skip + rows)
    upper = ((sent2, first), (near1, second), (near2, first), (came1, last))
    lower = ((sent1, first), (near1, first), (near2, second), (came2, last))
    for half, blocks in enumerate((upper, lower)):
        for k, (ref, at) in enumerate(blocks):
            to = pl.multiple_of((4 * half + (ids[0] ^ k)) * rows, rows)
            out[pl.ds(to, rows), :] = ref[at, :]


def attend_join_body(ids, sent1, sent2, came1, came2, seen, out):
    join_half(ids[0], sent1, sent2, came1, came2, out)


def norm_back_body(ids, *refs):
    pieces, (unit, inv, gain, grad_out, low_out, small_out) = refs[:4], refs[4:]
    turn = ids[0] ^ ids[1]
    for k, piece in enumerate(pieces):
        grad_out[turn ^ k] = piece[...].astype(F32)
    grad_normed = grad_out[...].reshape(unit.shape)
    grad = norm_back(grad_normed, unit[...], inv[:, :1], gain[...])
    grad_out[...] = grad.reshape(grad_out.shape)
    low_out[...] = grad.astype(LOW)
    total = lambda a: jnp.sum(a, axis=0, keepdims=True)
    small_out[...] = small_rows(total(grad_normed * unit[...]), total(grad_normed), total(grad))


def row_sums(rows):
    high = rows.astype(LOW)
    rest = (rows - high.astype(F32)).astype(LOW)
    ones = jnp.ones((8, rows.shape[1]), LOW)
    return mm_nt(ones, high) + mm_nt(ones, rest)


def attend_back_body(heads, query_scale, ids, *refs):
    grad, grad_low, wq, wk, wv, wo, probs_ref, qt, kt, vt = refs[:10]
    o = refs[10:14]
    scores_out, stack, sums_out, weights, dct, repeated, result = refs[14:]
    part = wq.shape[0]
    head = part // heads
    slots, full = qt.shape[1], kt.shape[1]
    half, block_len = slots // 4, full // 4
    quarter = block_len // 4
    weights[:part, :] = wk[...]
    weights[part : 2 * part, :] = wv[...]
    weights[2 * part :, :] = wq[...]
    dct[...] = mm_nt(wo[...], grad_low[...]).astype(LOW)
    for h in range(heads):
        at = slice(h * head, (h + 1) * head)
        probs = probs_ref[h]
        grad_probs = mm_tn(vt[at, :], dct[at, :])
        grad_values = mm_nt(dct[at, :], probs.astype(LOW))
        scores = probs * (grad_probs - jnp.sum(probs * grad_probs, axis=0, keepdims=True))
        scores_out[h] = scores
        scores_low = scores.astype(LOW)
        grad_queries = mm(kt[at, :], scores_low) * query_scale
        stack[at, :] = mm_nt(qt[at, :], scores_low).astype(LOW)
        stack[part + h * head : part + (h + 1) * head, :] = grad_values.astype(LOW)
        stack[2 * part + h * head : 2 * part + (h + 1) * head, :slots] = grad_queries.astype(LOW)
        sums_out[h, :8, :] = row_sums(grad_queries)
        sums_out[h, 8:, :] = row_sums(grad_values)
    pairs = pair_matrix(half, block_len, False)
    for b in range(4):
        repeated[:, b * block_len : (b + 1) * block_len] = mm(
            stack[2 * part :, b * half : (b + 1) * half], pairs
        ).astype(LOW)
    result[...] = mm_tn(stack[: 2 * part, :], weights[: 2 * part, :]) + mm_tn(repeated[...], weights[2 * part :, :])
    spread = pair_matrix(quarter, quarter // 2, True)
    for b in range(4):
        to = slice(b * quarter, (b + 1) * quarter)
        rows = lambda k: pl.ds(pl.multiple_of(b * block_len + (ids[1] ^ k) * quarter, quarter), quarter)
        residual = grad[b, pl.ds(pl.multiple_of(ids[1] * (quarter // 2), quarter // 2), quarter // 2), :]
        high = residual.astype(LOW)
        rest = (residual - high.astype(F32)).astype(LOW)
        o[0][to, :] = result[rows(0), :] + (mm(spread, high) + mm(spread, rest))
        for k in range(1, 4):
            o[k][to, :] = result[rows(k), :].astype(LOW)


def attend_weights_body(ids, x, grad, pooled_low, stack, ct, small_feed, small_attend, sums, keep, send, scr):
    part, slots = ct.shape
    heads = sums.shape[0]
    scr[0, :part, :] = mm(stack[2 * part :, :slots], pooled_low[...])
    scr[0, part : 2 * part, :] = mm(stack[:part, :], x[...])
    scr[1, :part, :] = mm(stack[part : 2 * part, :], x[...])
    scr[1, part : 2 * part, :] = mm(ct[...], grad[...])
    scr[:, 2 * part :, :] = jnp.zeros((2, scr.shape[1] - 2 * part, scr.shape[2]), F32)
    scr[0, 2 * part : 2 * part + SMALL_ROWS, :] = small_feed[...]
    scr[0, 2 * part + SMALL_ROWS : 2 * part + 2 * SMALL_ROWS, :] = small_attend[...]
    for h in range(heads):
        scr[1, 2 * part + h * SMALL_ROWS : 2 * part + (h + 1) * SMALL_ROWS, : sums.shape[2]] = sums[h]
    keep[...] = scr[ids[2]]
    send[...] = scr[1 - ids[2]].astype(LOW)


def total_body(r1, r2, r3, own, out):
    out[...] = total_of(own, (r1, r2, r3)).astype(LOW)


def widen_body(flip, ids, rows, *refs):
    first, second, scr, sem = refs[-4:]
    step = rows.shape[0] // 4
    for c, out in ((0, first), (1, second)):

        @pl.when((ids[2] ^ flip) == c)
        def _(out=out):
            copies = []
            for n in range(4):
                span = pl.ds(n * step, step)
                scr[span, :] = rows[span, :].astype(F32)
                copies.append(pltpu.make_async_copy(scr.at[span, :], out.at[span, :], sem.at[n]))
                copies[-1].start()
            for copy in copies:
                copy.wait()


def output_body(ids, n0, q1, q2, q3, output):
    rows = n0.shape[0]
    output[ids[0]] = n0[...]
    for b, q in ((1, q1), (2, q2), (3, q3)):
        output[ids[0] ^ b] = q[q.shape[0] - rows :, :]


def unpack_attend_body(ids, mine, other, dq, dk, dv, do, *rest):
    *rows_out, query_out, value_out, rel_out = rest
    part = dq.shape[0]
    heads = rel_out.shape[0]
    head = part // heads
    for c, (a, b) in ((0, (mine, other)), (1, (other, mine))):

        @pl.when(ids[2] == c)
        def _(a=a, b=b):
            dq[...] = a[:part, :].astype(F32)
            dk[...] = a[part : 2 * part, :].astype(F32)
            dv[...] = b[:part, :].astype(F32)
            do[...] = b[part : 2 * part, :].astype(F32)
            small_a = a[2 * part :, :].astype(F32)
            small_b = b[2 * part :, :].astype(F32)
            for n, out in enumerate(rows_out):
                row = n if n < 4 else SMALL_ROWS + n - 4
                out[...] = small_a[row, :]
            for out, row in ((query_out, 0), (value_out, 8)):
                out[...] = jnp.concatenate(
                    [small_b[h * SMALL_ROWS + row : h * SMALL_ROWS + row + 1, :head] for h in range(heads)], axis=1
                )[0]
            last = small_a.shape[0] - 32
            table = small_a[last:, :128] + small_b[last:, :128]
            for h in range(heads):
                for index in range(BASES):
                    at = h * BASES + index
                    rel_out[h : h + 1, index : index + 1] = table[at : at + 1, :1]


def quarters_body(met, r1, r2, r3, own, n1, n2, n3, q0, q1, q2, q3):
    total = total_of(own, (r1, r2, r3)).astype(LOW)
    rows = q0.shape[0]
    q0[...] = total[:rows]
    for b, (q, n) in enumerate(((q1, n1), (q2, n2), (q3, n3)), 1):
        q[:rows, :] = total[b * rows : (b + 1) * rows]
        q[rows:, :] = n[...]


def join_body(q0, q1, q2, q3, joined):
    rows = q0.shape[0]
    for b, q in enumerate((q0, q1, q2, q3)):
        joined[b * rows : (b + 1) * rows, :] = q[:rows, :]


def touch_body(t1, t2, t3, out):
    rows = out.shape[0]
    out[...] = t1[:rows, :] + t2[:rows, :] + t3[:rows, :]


def place_body(ids, t0, t1, t2, t3, out):
    rows = out.shape[1] // 4
    for k, t in enumerate((t0, t1, t2, t3)):
        at = pl.ds(pl.multiple_of((ids[1] ^ k) * rows, rows), rows)
        for b in range(4):
            out[ids[0] ^ b, at, :] = t[b * rows : (b + 1) * rows, :].astype(out.dtype)


def dp_sum(values, dp_size):
    step = 2
    while step < dp_size:
        values = [
            (v.astype(F32) + swap(v, "dp", dp_size, step).astype(F32)).astype(v.dtype) for v in values
        ]
        step *= 2
    return values


def both_ways(along1, along2, size):
    return swap(along1, "seq", size, 1), swap(along2, "seq", size, 2)


def shards(
    inputs,
    lengths,
    query_weight,
    query_bias,
    key_weight,
    value_weight,
    value_bias,
    rel_weight,
    out_weight,
    out_bias,
    attn_gain,
    attn_shift,
    up_weight,
    up_bias,
    down_weight,
    down_bias,
    ffn_gain,
    ffn_shift,
    cotangent,
):
    seq_size, dp_size, mp_size = (lax.axis_size(a) for a in ("seq", "dp", "mp"))
    j, m, c = lax.axis_index("seq"), lax.axis_index("mp"), lax.axis_index("dp") % 2
    sentences, block_len, width = inputs.shape
    assert sentences == seq_size == mp_size == 4 and dp_size % 2 == 0
    half = block_len // 2
    full, slots = 4 * block_len, 4 * half
    heads = rel_weight.shape[0]
    part = query_weight.shape[1]
    head = part // heads
    hidden_here = up_weight.shape[1]
    assert hidden_here == width
    query_scale = head ** (-0.5)
    row = lambda v: v.reshape(1, -1)
    column = lambda v: v.reshape(-1, 1)
    ids = jnp.stack([j, m, c, pick(lengths, j)]).astype(jnp.int32)
    wq, wk, wv = query_weight.T, key_weight.T, value_weight.T

    x = [pick(inputs, j)] + [swap(pick(inputs, j ^ k), "seq", seq_size, k) for k in range(1, 4)]
    bias = kernel(
        functools.partial(bias_body, heads, block_len, 32), f32(heads, full, slots), (ids, rel_weight), smem=2, micros=3.0
    )
    own, p1, p2, p3, probs, qt, kt, vt, ct, pooled_low, tokens = kernel(
        functools.partial(attend_body, heads, query_scale),
        [f32(half, width)]
        + [low(half, width)] * 3
        + [f32(heads, full, slots), low(part, slots), low(part, full), low(part, full), low(part, slots)]
        + [low(slots, width), low(full, width)],
        (ids, *x, wq, wk, wv, out_weight, column(query_bias), column(value_bias), row(out_bias), bias),
        smem=1,
        scratch=[
            pltpu.VMEM((4, half, width), F32),
            pltpu.VMEM((heads, full, slots), F32),
            pltpu.VMEM((part, slots), LOW),
            pltpu.VMEM((part, full), LOW),
            pltpu.VMEM((part, full), LOW),
            pltpu.VMEM((part, slots), LOW),
            pltpu.VMEM((slots, width), LOW),
            pltpu.SemaphoreType.DMA((9 + heads,)),
        ],
        micros=5.0,
        hbm=range(4, 11),
    )
    arrived = scatter_low((p1, p2, p3), "mp", mp_size)
    attended = kernel(total_body, low(half, width), (*arrived, own), micros=0.5)
    later = after(cotangent, attended)
    cots = [pick(later, j)] + [swap(pick(later, j ^ k), "seq", seq_size, k) for k in range(1, 4)]
    own, p1, p2, p3, hidden, slope, normed, unit, inv = kernel(
        feed_body,
        [f32(half, width)]
        + [low(half, width)] * 3
        + [low(slots, hidden_here), f32(slots, hidden_here), low(slots, width), f32(slots, width), f32(slots, 128)],
        (ids, attended, *gather_low(attended, "mp", mp_size), row(attn_gain), row(attn_shift), up_weight)
        + (row(up_bias), down_weight, row(down_bias)),
        smem=1,
        scratch=[pltpu.VMEM((4, half, width), F32)],
        micros=3.0,
    )
    p1, p2, p3 = after((p1, p2, p3), cots)
    mixed = kernel(total_body, low(half, width), (*scatter_low((p1, p2, p3), "mp", mp_size), own), micros=0.5)
    own, p1, p2, p3, *rest = kernel(
        feed_back_body,
        [f32(half, width)]
        + [low(half, width)] * 7
        + [low(slots, width), low(slots, hidden_here), f32(SMALL_ROWS, width)],
        (ids, mixed, *gather_low(mixed, "mp", mp_size), *cots, row(ffn_gain), row(ffn_shift), slope)
        + (down_weight, up_weight),
        smem=1,
        scratch=[pltpu.VMEM((4, half, width), F32), pltpu.VMEM((slots, width), LOW)],
        micros=3.0,
    )
    outputs, (grad_mixed, upward, small_feed) = rest[:4], rest[4:]
    operands = (hidden, grad_mixed, normed, upward)
    sides = [pltpu.VMEM((slots, width), LOW)] * 2
    feed_send = kernel(
        feed_send_body, low(width, width), (ids, *operands), smem=1, scratch=sides, micros=0.1
    )
    feed_arrived = swap(feed_send, "dp", dp_size, 1)
    arrived = scatter_low((p1, p2, p3), "mp", mp_size)
    grad_normed = kernel(total_body, low(half, width), (*arrived, own), micros=40.0)
    rows = width // 8
    feed_kept, along1, along2 = kernel(
        feed_keep_body,
        [f32(4 * rows, width)] + [low(2 * rows, width)] * 2,
        (ids, *operands, after(feed_arrived, grad_normed)),
        smem=1,
        scratch=sides + [pltpu.VMEM((width, width), F32)],
        micros=0.1,
    )
    s = gather_low(grad_normed, "mp", mp_size)
    came = both_ways(along1, along2, seq_size)
    grad, grad_attended, small_attend = kernel(
        norm_back_body,
        [f32(4, half, width), low(slots, width), f32(SMALL_ROWS, width)],
        (ids, grad_normed, *s, unit, inv, row(attn_gain)),
        smem=1,
        micros=6.5,
    )
    own_input, o1, o2, o3, scores, stack, sums = kernel(
        functools.partial(attend_back_body, heads, query_scale),
        [f32(block_len, width)]
        + [low(block_len, width)] * 3
        + [f32(heads, full, slots), low(3 * part, full), f32(heads, 16, head)],
        (ids, grad, grad_attended, wq, wk, wv, out_weight, probs, qt, kt, vt),
        smem=1,
        scratch=[
            pltpu.VMEM((3 * part, width), LOW),
            pltpu.VMEM((part, slots), LOW),
            pltpu.VMEM((part, full), LOW),
            pltpu.VMEM((full, width), F32),
        ],
        micros=0.1,
    )
    rel = kernel(
        functools.partial(rel_body, heads, block_len, 32),
        f32(32, 128),
        (ids, scores),
        smem=1,
        scratch=[pltpu.VMEM((heads * BASES, 8, slots), F32)],
        micros=0.1,
    )
    half_rows = 2 * part + 128
    attend_keep, attend_send = kernel(
        attend_weights_body,
        [f32(half_rows, width), low(half_rows, width)],
        (ids, after(tokens, came), grad_attended, pooled_low, stack, ct, small_feed, small_attend, sums),
        smem=1,
        scratch=[pltpu.VMEM((2, half_rows, width), F32)],
        micros=0.1,
    )
    landed = scatter_low((o1, o2, o3), "mp", mp_size)
    attend_arrived = swap(attend_send, "dp", dp_size, 1)
    few = half_rows // 8
    attend_kept, feed_own, along1, along2 = kernel(
        step_a_body,
        [f32(4 * few, width), f32(2 * rows, width)] + [low(2 * few + rows, width)] * 2,
        (ids, attend_keep, attend_arrived, rel, feed_kept, *came),
        smem=1,
        scratch=[pltpu.VMEM((half_rows, width), F32)],
        micros=0.1,
    )
    met = kernel(touch_body, low(SMALL_ROWS, width), tuple(landed), micros=6.0)
    quarter = block_len // 4
    q0, *q = kernel(
        quarters_body,
        [low(quarter, width)] + [low(quarter + half, width)] * 3,
        (met, *landed, own_input, *outputs[1:]),
        micros=0.5,
    )
    attend_own, sent1, sent2 = kernel(
        step_b_body,
        [f32(2 * few, width)] + [low(few + 2 * rows, width)] * 2,
        (attend_kept, after(feed_own, q0), *both_ways(along1, along2, seq_size)),
        micros=0.1,
    )
    near = both_ways(sent1, sent2, seq_size)
    q = deep(scatter_low(q, "seq", seq_size))
    joined = kernel(join_body, low(block_len, width), (q0, *q), micros=8.0)
    spread = gather_low(joined, "mp", mp_size)
    mid = kernel(
        step_c_body, [low(few, width)] * 2, (after(attend_own, joined), *near), micros=0.1
    )
    output_all = kernel(output_body, low(4, half, width), (ids, outputs[0], *q), smem=1, micros=0.1)
    along1, along2 = kernel(
        step_d_body,
        [low(2 * few + rows, width)] * 2,
        (after(mid[0], output_all), mid[1], *both_ways(*mid, seq_size), *near),
        micros=0.1,
    )
    came = both_ways(along1, along2, seq_size)
    seen = kernel(touch_body, low(SMALL_ROWS, width), tuple(spread), micros=8.0)
    attend_mine = kernel(
        attend_join_body,
        low(half_rows, width),
        (ids, along1, along2, *came, seen),
        smem=1,
        micros=0.2,
    )
    feed_mine = kernel(
        feed_join_body,
        low(width, width),
        (ids, sent1, sent2, *near, came[0], after(came[1], attend_mine)),
        smem=1,
        micros=0.1,
    )
    attend_mine, feed_mine = dp_sum((attend_mine, feed_mine), dp_size)
    attend_other = swap(attend_mine, "dp", dp_size, 1)
    feed_other = swap(feed_mine, "dp", dp_size, 1)
    widen = lambda flip, *args: kernel(
        functools.partial(widen_body, flip),
        [f32(width, width)] * 2,
        (ids, *args),
        smem=1,
        scratch=[pltpu.VMEM((width, width), F32), pltpu.SemaphoreType.DMA((4,))],
        micros=0.1,
        hbm=(0, 1),
        reused=len(args) - 1,
    )
    halves = widen(0, feed_mine)
    down_grad, up_grad = widen(1, feed_other, *halves)
    input_all = kernel(
        place_body, f32(4, block_len, width), (ids, joined, *spread), smem=1, micros=0.1
    )
    dq, dk, dv, do, *small, query_sum, value_sum, rel_sum = kernel(
        unpack_attend_body,
        [f32(part, width)] * 4 + [f32(width)] * 7 + [f32(part)] * 2 + [f32(heads, BASES)],
        (ids, after(attend_mine, halves), attend_other),
        smem=1,
        micros=1.5,
    )
    ffn_gain_sum, ffn_shift_sum, down_bias_sum, up_bias_sum, attn_gain_sum, attn_shift_sum, out_bias_sum = small
    return (
        output_all,
        input_all,
        dq.T,
        query_sum,
        dk.T,
        dv.T,
        value_sum,
        rel_sum,
        do,
        out_bias_sum,
        attn_gain_sum,
        attn_shift_sum,
        up_grad,
        up_bias_sum,
        down_grad,
        down_bias_sum,
        ffn_gain_sum,
        ffn_shift_sum,
    )


def solution(mesh):
    return jax.shard_map(
        shards,
        mesh=mesh,
        in_specs=(
            P("dp", "seq", None),
            P("dp"),
            P(None, "mp"),
            P("mp"),
            P(None, "mp"),
            P(None, "mp"),
            P("mp"),
            P("mp", None),
            P("mp", None),
            P(),
            P(),
            P(),
            P(None, "mp"),
            P("mp"),
            P("mp", None),
            P(),
            P(),
            P(),
            P("dp", "seq", None),
        ),
        out_specs=(
            P("dp", "seq", None),
            P("dp", "seq", None),
            P(None, "mp"),
            P("mp"),
            P(None, "mp"),
            P(None, "mp"),
            P("mp"),
            P("mp", None),
            P("mp", None),
            P(),
            P(),
            P(),
            P(None, "mp"),
            P("mp"),
            P("mp", None),
            P(),
            P(),
            P(),
        ),
        check_vma=False,
    )
```

```python
import functools

import jax
import jax.numpy as jnp
from jax import lax
from jax.experimental import pallas as pl
from jax.experimental.pallas import tpu as pltpu
from jax.sharding import PartitionSpec as P

BASES = 8
EPSILON = 1e-05
MASKED_SCORE = -1e30
F32 = jnp.float32
LOW = jnp.bfloat16
SMALL_ROWS = 16
MIB = 1024 * 1024
DEPTH = 2


def f32(*shape):
    return jax.ShapeDtypeStruct(shape, F32)


def low(*shape):
    return jax.ShapeDtypeStruct(shape, LOW)


def kernel(body, outs, args, smem=0, scratch=(), micros=1.0, limit=16, hbm=(), reused=0):
    in_specs = [pl.BlockSpec(memory_space=pltpu.SMEM)] * smem
    in_specs += [pl.BlockSpec(memory_space=pltpu.VMEM)] * (len(args) - smem - reused)
    in_specs += [pl.BlockSpec(memory_space=pltpu.HBM)] * reused
    whole = pl.BlockSpec(memory_space=pltpu.VMEM)
    if isinstance(outs, list):
        out_specs = [pl.BlockSpec(memory_space=pltpu.HBM) if n in hbm else whole for n in range(len(outs))]
    else:
        out_specs = whole
    return pl.pallas_call(
        body,
        out_shape=outs,
        in_specs=in_specs,
        out_specs=out_specs,
        scratch_shapes=list(scratch),
        input_output_aliases={len(args) - reused + n: n for n in range(reused)},
        compiler_params=pltpu.CompilerParams(vmem_limit_bytes=limit * MIB),
        cost_estimate=pl.CostEstimate(
            flops=int(micros * 4e8), bytes_accessed=int(micros * 3e6), transcendentals=0
        ),
    )(*args)


def after(value, *events):
    return lax.optimization_barrier((value, events))[0]


def dot_of(dims, a, b):
    return lax.dot_general(a, b, (dims, ((), ())), preferred_element_type=F32)


mm = functools.partial(dot_of, ((1,), (0,)))
mm_nt = functools.partial(dot_of, ((1,), (1,)))
mm_tn = functools.partial(dot_of, ((0,), (0,)))


def swap(block, axis, size, k):
    return lax.ppermute(block, axis, [(s, s ^ k) for s in range(size)])


def deep(values):
    for _ in range(DEPTH):
        values = lax.optimization_barrier(values)
    return values


def gather_low(block, axis, size):
    landed = [swap(block, axis, size, k) for k in range(1, size)]
    return deep(landed) if axis == "mp" else landed


def scatter_low(blocks, axis, size):
    landed = [swap(blocks[k - 1], axis, size, k) for k in range(1, size)]
    return deep(landed) if axis == "mp" else landed


def pick(stacked, index):
    return lax.dynamic_index_in_dim(stacked, index, 0, keepdims=False)


def norm_stats(rows):
    center = rows - jnp.mean(rows, axis=-1, keepdims=True)
    scale_inv = lax.rsqrt(jnp.mean(center * center, axis=-1, keepdims=True) + EPSILON)
    return center * scale_inv, scale_inv


def norm_back(grad_out, normed, scale_inv, gain):
    grad_normed = grad_out * gain
    centered = grad_normed - jnp.mean(grad_normed, axis=-1, keepdims=True)
    return scale_inv * (centered - normed * jnp.mean(grad_normed * normed, axis=-1, keepdims=True))


def total_of(own_ref, arrived_refs):
    total = own_ref[...]
    for ref in arrived_refs:
        total = total + ref[...].astype(F32)
    return total


def pair_matrix(rows, cols, tall):
    r = lax.broadcasted_iota(jnp.int32, (rows, cols), 0)
    c = lax.broadcasted_iota(jnp.int32, (rows, cols), 1)
    hit = (r >> 1) == c if tall else r == (c >> 1)
    return jnp.where(hit, 0.5, 0.0).astype(LOW)


def distances(ids, chunk, rows, block_len, slots):
    j = ids[0]
    start = chunk * rows
    token = (j ^ (start // block_len)) * block_len + start % block_len
    token = token + lax.broadcasted_iota(jnp.int32, (rows, slots), 0)
    s = lax.broadcasted_iota(jnp.int32, (rows, slots), 1)
    half = block_len // 2
    slot = (j ^ (s // half)) * half + s % half
    return token, (token - 2 * slot).astype(F32)


def basis_of(distance, index, span):
    degree = index % (BASES // 2)
    inverse = 64.0 / (span * 4.0**degree)
    if index < BASES // 2:
        return jnp.exp(jnp.abs(distance) * (-inverse))
    return jnp.tanh(distance * inverse)


def bias_body(heads, block_len, rows, ids, rel, out):
    full, slots = out.shape[1:]

    def step(chunk, carry):
        token, distance = distances(ids, chunk, rows, block_len, slots)
        sums = [jnp.zeros((rows, slots), F32)] * heads
        for index in range(BASES):
            base = basis_of(distance, index, full)
            sums = [sums[h] + rel[h, index] * base for h in range(heads)]
        valid = token < ids[3]
        for h in range(heads):
            out[h, pl.ds(pl.multiple_of(chunk * rows, rows), rows), :] = jnp.where(valid, sums[h], MASKED_SCORE)
        return carry

    lax.fori_loop(0, full // rows, step, 0)


def rel_body(heads, block_len, rows, ids, scores_ref, out, acc):
    full, slots = scores_ref.shape[1:]
    acc[...] = jnp.zeros_like(acc)

    def step(chunk, carry):
        _, distance = distances(ids, chunk, rows, block_len, slots)
        at = pl.ds(pl.multiple_of(chunk * rows, rows), rows)
        grads = [scores_ref[h, at, :] for h in range(heads)]
        for index in range(BASES):
            base = basis_of(distance, index, full)
            for h in range(heads):
                acc[h * BASES + index] += jnp.sum((grads[h] * base).reshape(rows // 8, 8, slots), axis=0)
        return carry

    lax.fori_loop(0, full // rows, step, 0)
    for row in range(heads * BASES):
        col = jnp.sum(jnp.sum(acc[row], axis=0, keepdims=True), axis=1, keepdims=True)
        out[row : row + 1, :] = jnp.broadcast_to(col, (1, out.shape[1]))


def attend_body(heads, query_scale, ids, *refs):
    x = refs[:4]
    wq, wk, wv, wo, qb, vb, ob, bias, own_out, p1, p2, p3 = refs[4:16]
    hbm = refs[16:23]
    scr, probs_ref, qt, kt, vt, ct, pooled_low, sem = refs[23:]
    probs_hbm, qt_hbm, kt_hbm, vt_hbm, ct_hbm, pooled_hbm, x_hbm = hbm
    block_len = x[0].shape[0]
    half = block_len // 2
    head = wq.shape[0] // heads
    copies = []

    def send(source, target):
        copy = pltpu.make_async_copy(source, target, sem.at[len(copies)])
        copy.start()
        copies.append(copy)

    for b in range(4):
        send(x[b], x_hbm.at[pl.ds(b * block_len, block_len), :])
    pairs = pair_matrix(half, block_len, False)
    for b in range(4):
        span = slice(b * block_len, (b + 1) * block_len)
        kt[:, span] = mm_nt(wk[...], x[b][...]).astype(LOW)
        vt[:, span] = (mm_nt(wv[...], x[b][...]) + vb[...]).astype(LOW)
        pooled = mm(pairs, x[b][...])
        scr[b] = pooled
        pooled_low[b * half : (b + 1) * half, :] = pooled.astype(LOW)
    turn = ids[0] ^ ids[1]
    own_out[...] = scr[turn] + ob[...]
    qt[...] = ((mm_nt(wq[...], pooled_low[...]) + qb[...]) * query_scale).astype(LOW)
    send(kt, kt_hbm)
    send(vt, vt_hbm)
    send(qt, qt_hbm)
    send(pooled_low, pooled_hbm)
    for h in range(heads):
        at = slice(h * head, (h + 1) * head)
        scores = mm_tn(kt[at, :], qt[at, :]) + bias[h]
        grown = jnp.exp(scores - jnp.max(scores, axis=0, keepdims=True))
        probs = grown * (1.0 / jnp.sum(grown, axis=0, keepdims=True))
        probs_ref[h] = probs
        send(probs_ref.at[h], probs_hbm.at[h])
        ct[at, :] = mm(vt[at, :], probs.astype(LOW)).astype(LOW)
    send(ct, ct_hbm)
    result = mm_tn(ct[...], wo[...])
    for b in range(4):
        scr[b] = result[b * half : (b + 1) * half, :]
    own_out[...] += scr[turn]
    for k, out in ((1, p1), (2, p2), (3, p3)):
        out[...] = scr[turn ^ k].astype(LOW)
    for copy in copies:
        copy.wait()


def feed_body(ids, a0, a1, a2, a3, gain, shift, wu, ub, wd, db, own, p1, p2, p3, *refs):
    hidden_out, slope_out, normed_out, unit_out, inv_out, scr = refs
    rows, width = a0.shape
    turn = ids[0] ^ ids[1]
    for k, a in enumerate((a0, a1, a2, a3)):
        scr[turn ^ k] = a[...].astype(F32)
    unit, inv = norm_stats(scr[...].reshape(4 * rows, width))
    normed = unit * gain[...] + shift[...]
    unit_out[...] = unit
    inv_out[...] = jnp.broadcast_to(inv, inv_out.shape)
    normed_low = normed.astype(LOW)
    normed_out[...] = normed_low
    scr[...] = normed.reshape(scr.shape)
    own[...] = scr[turn] + db[...]
    up = mm(normed_low, wu[...]) + ub[...]
    phi = 0.5 * (1.0 + lax.erf(up * (0.5**0.5)))
    density = jnp.exp(up * up * -0.5) * 0.3989422804014327
    hidden = (up * phi).astype(LOW)
    hidden_out[...] = hidden
    slope_out[...] = phi + up * density
    scr[...] = mm(hidden, wd[...]).reshape(scr.shape)
    own[...] += scr[turn]
    for k, out in ((1, p1), (2, p2), (3, p3)):
        out[...] = scr[turn ^ k].astype(LOW)


def small_rows(*sums):
    return jnp.concatenate(list(sums) + [jnp.zeros((SMALL_ROWS - len(sums), sums[0].shape[1]), F32)])


def feed_back_body(ids, *refs):
    pieces, cots = refs[:4], refs[4:8]
    gain, shift, slope, wd, wu, own, p1, p2, p3 = refs[8:17]
    outs = refs[17:21]
    grad_out, upward_out, small_out, scr, low_scr = refs[21:]
    rows, width = own.shape
    slots = 4 * rows
    turn = ids[0] ^ ids[1]
    for k, piece in enumerate(pieces):
        scr[turn ^ k] = piece[...].astype(F32)
    unit, inv = norm_stats(scr[...].reshape(slots, width))
    s = lax.broadcasted_iota(jnp.int32, (slots, 1), 0)
    slot = (ids[0] ^ (s // rows)) * rows + s % rows
    valid = jnp.where(2 * slot < ids[3], 1.0, 0.0)
    output = ((unit * gain[...] + shift[...]) * valid).astype(LOW)
    for b in range(4):
        outs[b][...] = output[b * rows : (b + 1) * rows, :]
        low_scr[b * rows : (b + 1) * rows, :] = cots[b][...]
    top = low_scr[...].astype(F32) * valid
    grad = norm_back(top, unit, inv, gain[...])
    grad_low = grad.astype(LOW)
    grad_out[...] = grad_low
    scr[...] = grad.reshape(scr.shape)
    own[...] = scr[turn]
    hidden = mm_nt(grad_low, wd[...]).astype(LOW).astype(F32)
    upward = hidden * slope[...]
    upward_low = upward.astype(LOW)
    upward_out[...] = upward_low
    total = lambda a: jnp.sum(a, axis=0, keepdims=True)
    small_out[...] = small_rows(total(top * unit), total(top), total(grad), total(upward))
    scr[...] = mm_nt(upward_low, wu[...]).reshape(scr.shape)
    own[...] += scr[turn]
    for k, out in ((1, p1), (2, p2), (3, p3)):
        out[...] = scr[turn ^ k].astype(LOW)


def feed_product(which, hidden, grad, normed, upward, left, right, put):
    @pl.when(which == 0)
    def _():
        left[...] = hidden[...]
        right[...] = grad[...]

    @pl.when(which != 0)
    def _():
        left[...] = normed[...]
        right[...] = upward[...]

    step = 256
    for at in range(0, left.shape[1], step):
        put(slice(at, at + step), mm_tn(left[:, at : at + step], right[...]))


def first_step(base, total, kept, along1, along2):
    rows = along1[0] // 2
    block = lambda half, k: total(pl.ds(pl.multiple_of((4 * half + (base ^ k)) * rows, rows), rows))
    for n, (half, k) in enumerate(((0, 0), (0, 2), (1, 0), (1, 1))):
        kept[n * rows : (n + 1) * rows, :] = block(half, k)
    for (_, out), picks in ((along1, ((0, 1), (0, 3))), (along2, ((1, 2), (1, 3)))):
        for n, (half, k) in enumerate(picks):
            out[n * rows : (n + 1) * rows, :] = block(half, k).astype(LOW)


def second_step(kept, came1, came2, own, along1, along2):
    rows = along1.shape[0]
    part = lambda n: kept[n * rows : (n + 1) * rows, :]
    came = lambda ref, n: ref[n * rows : (n + 1) * rows, :].astype(F32)
    own[:rows, :] = part(0) + came(came1, 0)
    own[rows:, :] = part(2) + came(came2, 0)
    along2[...] = (part(1) + came(came1, 1)).astype(LOW)
    along1[...] = (part(3) + came(came2, 1)).astype(LOW)


def last_sums(own, came1, came2):
    rows = came1.shape[0]
    upper = own[:rows, :] + came2[...].astype(F32)
    lower = own[rows:, :] + came1[...].astype(F32)
    return upper.astype(LOW), lower.astype(LOW)


def join_half(base, mine1, mine2, came1, came2, out):
    rows = out.shape[0] // 8
    order = ((mine1, 0, (0, 2)), (came1, 0, (1, 3)), (mine2, 1, (0, 1)), (came2, 1, (2, 3)))
    for ref, half, ks in order:
        for n, k in enumerate(ks):
            at = pl.ds(pl.multiple_of((4 * half + (base ^ k)) * rows, rows), rows)
            out[at, :] = ref[n * rows : (n + 1) * rows, :]


def feed_send_body(ids, hidden, grad, normed, upward, out, left, right):
    def put(at, value):
        out[at, :] = value.astype(LOW)

    feed_product(1 - ids[2], hidden, grad, normed, upward, left, right, put)


def feed_keep_body(ids, hidden, grad, normed, upward, arrived, kept, along1, along2, left, right, scr):
    def put(at, value):
        scr[at, :] = value + arrived[at, :].astype(F32)

    feed_product(ids[2], hidden, grad, normed, upward, left, right, put)
    rows = along1.shape[0]
    first_step(ids[0], lambda at: scr[at, :], kept, (rows, along1), (rows, along2))


def step_a_body(ids, keep, arrived, rel, feed_kept, came1, came2, kept, feed_own, along1, along2, scr):
    rows = keep.shape[0] // 4
    scr[...] = keep[...] + arrived[...].astype(F32)
    scr[-rel.shape[0] :, : rel.shape[1]] = rel[...]
    first_step(ids[0], lambda at: scr[at, :], kept, (rows, along1), (rows, along2))
    second_step(feed_kept, came1, came2, feed_own, along1.at[rows:, :], along2.at[rows:, :])


def step_b_body(kept, feed_own, came1, came2, own, along1, along2):
    few = own.shape[0] // 2
    skip = 2 * few
    first = slice(0, skip)
    second_step(
        kept, came1.at[first, :], came2.at[first, :], own, along1.at[slice(0, few), :], along2.at[slice(0, few), :]
    )
    upper, lower = last_sums(feed_own, came1.at[skip:, :], came2.at[skip:, :])
    for out, parts in ((along1, (lower, upper)), (along2, (upper, lower))):
        for n, part in enumerate(parts):
            out[few + n * part.shape[0] : few + (n + 1) * part.shape[0], :] = part


def step_c_body(own, came1, came2, along1, along2):
    first = slice(0, along1.shape[0])
    along2[...], along1[...] = last_sums(own, came1.at[first, :], came2.at[first, :])


def step_d_body(mid1, mid2, came1, came2, near1, near2, along1, along2):
    few = mid1.shape[0]
    done = along1.shape[0] - 2 * few
    for out, own, came, near in ((along1, mid2, came2, near2), (along2, mid1, came1, near1)):
        out[:few, :] = own[...]
        out[few : 2 * few, :] = came[...]
        out[2 * few :, :] = near[few : few + done, :]


def joins_body(ids, along1, along2, came1, came2, sent1, sent2, near1, near2, seen, attend_out, out):
    join_half(ids[0], along1, along2, came1, came2, attend_out)
    rows = out.shape[0] // 8
    few = sent1.shape[0] - 2 * rows
    skip = came1.shape[0] - rows
    first, second, last = slice(few, few + rows), slice(few + rows, few + 2 * rows), slice(skip, skip + rows)
    upper = ((sent2, first), (near1, second), (near2, first), (came1, last))
    lower = ((sent1, first), (near1, first), (near2, second), (came2, last))
    for half, blocks in enumerate((upper, lower)):
        for k, (ref, at) in enumerate(blocks):
            to = pl.multiple_of((4 * half + (ids[0] ^ k)) * rows, rows)
            out[pl.ds(to, rows), :] = ref[at, :]


def norm_back_body(ids, *refs):
    pieces, (unit, inv, gain, grad_out, low_out, small_out) = refs[:4], refs[4:]
    turn = ids[0] ^ ids[1]
    for k, piece in enumerate(pieces):
        grad_out[turn ^ k] = piece[...].astype(F32)
    grad_normed = grad_out[...].reshape(unit.shape)
    grad = norm_back(grad_normed, unit[...], inv[:, :1], gain[...])
    grad_out[...] = grad.reshape(grad_out.shape)
    low_out[...] = grad.astype(LOW)
    total = lambda a: jnp.sum(a, axis=0, keepdims=True)
    small_out[...] = small_rows(total(grad_normed * unit[...]), total(grad_normed), total(grad))


def row_sums(rows):
    high = rows.astype(LOW)
    rest = (rows - high.astype(F32)).astype(LOW)
    ones = jnp.ones((8, rows.shape[1]), LOW)
    return mm_nt(ones, high) + mm_nt(ones, rest)


def attend_back_body(heads, query_scale, ids, *refs):
    grad, grad_low, wq, wk, wv, wo, probs_ref, qt, kt, vt = refs[:10]
    o = refs[10:14]
    scores_out, stack, sums_out, weights, dct, repeated, result = refs[14:]
    part = wq.shape[0]
    head = part // heads
    slots, full = qt.shape[1], kt.shape[1]
    half, block_len = slots // 4, full // 4
    quarter = block_len // 4
    weights[:part, :] = wk[...]
    weights[part : 2 * part, :] = wv[...]
    weights[2 * part :, :] = wq[...]
    dct[...] = mm_nt(wo[...], grad_low[...]).astype(LOW)
    for h in range(heads):
        at = slice(h * head, (h + 1) * head)
        probs = probs_ref[h]
        grad_probs = mm_tn(vt[at, :], dct[at, :])
        grad_values = mm_nt(dct[at, :], probs.astype(LOW))
        scores = probs * (grad_probs - jnp.sum(probs * grad_probs, axis=0, keepdims=True))
        scores_out[h] = scores
        scores_low = scores.astype(LOW)
        grad_queries = mm(kt[at, :], scores_low) * query_scale
        stack[at, :] = mm_nt(qt[at, :], scores_low).astype(LOW)
        stack[part + h * head : part + (h + 1) * head, :] = grad_values.astype(LOW)
        stack[2 * part + h * head : 2 * part + (h + 1) * head, :slots] = grad_queries.astype(LOW)
        sums_out[h, :8, :] = row_sums(grad_queries)
        sums_out[h, 8:, :] = row_sums(grad_values)
    pairs = pair_matrix(half, block_len, False)
    for b in range(4):
        repeated[:, b * block_len : (b + 1) * block_len] = mm(
            stack[2 * part :, b * half : (b + 1) * half], pairs
        ).astype(LOW)
    result[...] = mm_tn(stack[: 2 * part, :], weights[: 2 * part, :]) + mm_tn(repeated[...], weights[2 * part :, :])
    spread = pair_matrix(quarter, quarter // 2, True)
    for b in range(4):
        to = slice(b * quarter, (b + 1) * quarter)
        rows = lambda k: pl.ds(pl.multiple_of(b * block_len + (ids[1] ^ k) * quarter, quarter), quarter)
        residual = grad[b, pl.ds(pl.multiple_of(ids[1] * (quarter // 2), quarter // 2), quarter // 2), :]
        high = residual.astype(LOW)
        rest = (residual - high.astype(F32)).astype(LOW)
        o[0][to, :] = result[rows(0), :] + (mm(spread, high) + mm(spread, rest))
        for k in range(1, 4):
            o[k][to, :] = result[rows(k), :].astype(LOW)


def attend_weights_body(ids, x, grad, pooled_low, stack, ct, small_feed, small_attend, sums, keep, send, scr):
    part, slots = ct.shape
    heads = sums.shape[0]
    scr[0, :part, :] = mm(stack[2 * part :, :slots], pooled_low[...])
    scr[0, part : 2 * part, :] = mm(stack[:part, :], x[...])
    scr[1, :part, :] = mm(stack[part : 2 * part, :], x[...])
    scr[1, part : 2 * part, :] = mm(ct[...], grad[...])
    scr[:, 2 * part :, :] = jnp.zeros((2, scr.shape[1] - 2 * part, scr.shape[2]), F32)
    scr[0, 2 * part : 2 * part + SMALL_ROWS, :] = small_feed[...]
    scr[0, 2 * part + SMALL_ROWS : 2 * part + 2 * SMALL_ROWS, :] = small_attend[...]
    for h in range(heads):
        scr[1, 2 * part + h * SMALL_ROWS : 2 * part + (h + 1) * SMALL_ROWS, : sums.shape[2]] = sums[h]
    keep[...] = scr[ids[2]]
    send[...] = scr[1 - ids[2]].astype(LOW)


def total_body(r1, r2, r3, own, out):
    out[...] = total_of(own, (r1, r2, r3)).astype(LOW)


def sender(sem):
    copies = []

    def send(source, target):
        copy = pltpu.make_async_copy(source, target, sem.at[len(copies)])
        copy.start()
        copies.append(copy)

    def wait():
        for copy in copies:
            copy.wait()

    return send, wait


def widen(which, rows, first, second, scr, sem):
    step = rows.shape[0] // 4
    for n in range(4):
        span = pl.ds(n * step, step)
        scr[span, :] = rows[span, :].astype(F32)
        for c, out in ((0, first), (1, second)):

            @pl.when(which == c)
            def _(out=out, n=n, span=span):
                copy = pltpu.make_async_copy(scr.at[span, :], out.at[span, :], sem.at[n])
                copy.start()


def widen_wait(which, first, second, scr, sem):
    step = scr.shape[0] // 4
    for n in range(4):
        span = pl.ds(n * step, step)
        for c, out in ((0, first), (1, second)):

            @pl.when(which == c)
            def _(out=out, n=n, span=span):
                pltpu.make_async_copy(scr.at[span, :], out.at[span, :], sem.at[n]).wait()


def output_body(ids, n0, q1, q2, q3, output):
    rows = n0.shape[0]
    output[ids[0]] = n0[...]
    for b, q in ((1, q1), (2, q2), (3, q3)):
        output[ids[0] ^ b] = q[q.shape[0] - rows :, :]


def unpack_body(ids, mine, other, feed_other, _first, _second, first, second, *rest):
    *rows_out, query_out, value_out, rel_out, dq, dk, dv, do, scr, wide, sem, wide_sem = rest
    widen(1 - ids[2], feed_other, first, second, wide, wide_sem)
    unpack_attend(ids, mine, other, rows_out, query_out, value_out, rel_out, (dq, dk, dv, do), scr, sem)
    widen_wait(1 - ids[2], first, second, wide, wide_sem)


def unpack_attend(ids, mine, other, rows_out, query_out, value_out, rel_out, larges, scr, sem):
    dq, dk, dv, do = larges
    send, wait = sender(sem)
    part = dq.shape[0]
    heads = rel_out.shape[0]
    head = part // heads
    for c, (a, b) in ((0, (mine, other)), (1, (other, mine))):

        @pl.when(ids[2] == c)
        def _(a=a, b=b):
            scr[0] = a[:part, :].astype(F32)
            scr[1] = a[part : 2 * part, :].astype(F32)
            scr[2] = b[:part, :].astype(F32)
            scr[3] = b[part : 2 * part, :].astype(F32)
            small_a = a[2 * part :, :].astype(F32)
            small_b = b[2 * part :, :].astype(F32)
            for n, out in enumerate(rows_out):
                row = n if n < 4 else SMALL_ROWS + n - 4
                out[...] = small_a[row, :]
            for out, row in ((query_out, 0), (value_out, 8)):
                out[...] = jnp.concatenate(
                    [small_b[h * SMALL_ROWS + row : h * SMALL_ROWS + row + 1, :head] for h in range(heads)], axis=1
                )[0]
            last = small_a.shape[0] - 32
            table = small_a[last:, :128] + small_b[last:, :128]
            for h in range(heads):
                for index in range(BASES):
                    at = h * BASES + index
                    rel_out[h : h + 1, index : index + 1] = table[at : at + 1, :1]

    for n, out in enumerate(larges):
        send(scr.at[n], out)
    wait()


def quarters_body(met, r1, r2, r3, own, n1, n2, n3, q0, q1, q2, q3):
    total = total_of(own, (r1, r2, r3)).astype(LOW)
    rows = q0.shape[0]
    q0[...] = total[:rows]
    for b, (q, n) in enumerate(((q1, n1), (q2, n2), (q3, n3)), 1):
        q[:rows, :] = total[b * rows : (b + 1) * rows]
        q[rows:, :] = n[...]


def join_body(q0, q1, q2, q3, joined):
    rows = q0.shape[0]
    for b, q in enumerate((q0, q1, q2, q3)):
        joined[b * rows : (b + 1) * rows, :] = q[:rows, :]


def touch_body(t1, t2, t3, out):
    rows = out.shape[0]
    out[...] = t1[:rows, :] + t2[:rows, :] + t3[:rows, :]


def place_body(ids, t0, t1, t2, t3, mine, out, first, second, scr, wide, sem, wide_sem):
    send, wait = sender(sem)
    rows = scr.shape[1] // 4
    for b in range(4):
        for k, t in enumerate((t0, t1, t2, t3)):
            at = pl.ds(pl.multiple_of((ids[1] ^ k) * rows, rows), rows)
            scr[b, at, :] = t[b * rows : (b + 1) * rows, :].astype(out.dtype)
        send(scr.at[b], out.at[ids[0] ^ b])
    widen(ids[2], mine, first, second, wide, wide_sem)
    wait()
    widen_wait(ids[2], first, second, wide, wide_sem)


def dp_sum(values, dp_size):
    step = 2
    while step < dp_size:
        values = [
            (v.astype(F32) + swap(v, "dp", dp_size, step).astype(F32)).astype(v.dtype) for v in values
        ]
        step *= 2
    return values


def both_ways(along1, along2, size):
    return swap(along1, "seq", size, 1), swap(along2, "seq", size, 2)


def shards(
    inputs,
    lengths,
    query_weight,
    query_bias,
    key_weight,
    value_weight,
    value_bias,
    rel_weight,
    out_weight,
    out_bias,
    attn_gain,
    attn_shift,
    up_weight,
    up_bias,
    down_weight,
    down_bias,
    ffn_gain,
    ffn_shift,
    cotangent,
):
    seq_size, dp_size, mp_size = (lax.axis_size(a) for a in ("seq", "dp", "mp"))
    j, m, c = lax.axis_index("seq"), lax.axis_index("mp"), lax.axis_index("dp") % 2
    sentences, block_len, width = inputs.shape
    assert sentences == seq_size == mp_size == 4 and dp_size % 2 == 0
    half = block_len // 2
    full, slots = 4 * block_len, 4 * half
    heads = rel_weight.shape[0]
    part = query_weight.shape[1]
    head = part // heads
    hidden_here = up_weight.shape[1]
    assert hidden_here == width
    query_scale = head ** (-0.5)
    row = lambda v: v.reshape(1, -1)
    column = lambda v: v.reshape(-1, 1)
    ids = jnp.stack([j, m, c, pick(lengths, j)]).astype(jnp.int32)
    wq, wk, wv = query_weight.T, key_weight.T, value_weight.T

    x = [pick(inputs, j)] + [swap(pick(inputs, j ^ k), "seq", seq_size, k) for k in range(1, 4)]
    bias = kernel(
        functools.partial(bias_body, heads, block_len, 32), f32(heads, full, slots), (ids, rel_weight), smem=2, micros=3.0
    )
    own, p1, p2, p3, probs, qt, kt, vt, ct, pooled_low, tokens = kernel(
        functools.partial(attend_body, heads, query_scale),
        [f32(half, width)]
        + [low(half, width)] * 3
        + [f32(heads, full, slots), low(part, slots), low(part, full), low(part, full), low(part, slots)]
        + [low(slots, width), low(full, width)],
        (ids, *x, wq, wk, wv, out_weight, column(query_bias), column(value_bias), row(out_bias), bias),
        smem=1,
        scratch=[
            pltpu.VMEM((4, half, width), F32),
            pltpu.VMEM((heads, full, slots), F32),
            pltpu.VMEM((part, slots), LOW),
            pltpu.VMEM((part, full), LOW),
            pltpu.VMEM((part, full), LOW),
            pltpu.VMEM((part, slots), LOW),
            pltpu.VMEM((slots, width), LOW),
            pltpu.SemaphoreType.DMA((9 + heads,)),
        ],
        micros=5.0,
        hbm=range(4, 11),
    )
    arrived = scatter_low((p1, p2, p3), "mp", mp_size)
    attended = kernel(total_body, low(half, width), (*arrived, own), micros=0.5)
    later = after(cotangent, attended)
    cots = [pick(later, j)] + [swap(pick(later, j ^ k), "seq", seq_size, k) for k in range(1, 4)]
    own, p1, p2, p3, hidden, slope, normed, unit, inv = kernel(
        feed_body,
        [f32(half, width)]
        + [low(half, width)] * 3
        + [low(slots, hidden_here), f32(slots, hidden_here), low(slots, width), f32(slots, width), f32(slots, 128)],
        (ids, attended, *gather_low(attended, "mp", mp_size), row(attn_gain), row(attn_shift), up_weight)
        + (row(up_bias), down_weight, row(down_bias)),
        smem=1,
        scratch=[pltpu.VMEM((4, half, width), F32)],
        micros=3.0,
    )
    p1, p2, p3 = after((p1, p2, p3), cots)
    mixed = kernel(total_body, low(half, width), (*scatter_low((p1, p2, p3), "mp", mp_size), own), micros=0.5)
    own, p1, p2, p3, *rest = kernel(
        feed_back_body,
        [f32(half, width)]
        + [low(half, width)] * 7
        + [low(slots, width), low(slots, hidden_here), f32(SMALL_ROWS, width)],
        (ids, mixed, *gather_low(mixed, "mp", mp_size), *cots, row(ffn_gain), row(ffn_shift), slope)
        + (down_weight, up_weight),
        smem=1,
        scratch=[pltpu.VMEM((4, half, width), F32), pltpu.VMEM((slots, width), LOW)],
        micros=3.0,
    )
    outputs, (grad_mixed, upward, small_feed) = rest[:4], rest[4:]
    operands = (hidden, grad_mixed, normed, upward)
    sides = [pltpu.VMEM((slots, width), LOW)] * 2
    feed_send = kernel(
        feed_send_body, low(width, width), (ids, *operands), smem=1, scratch=sides, micros=0.1
    )
    feed_arrived = swap(feed_send, "dp", dp_size, 1)
    arrived = scatter_low((p1, p2, p3), "mp", mp_size)
    grad_normed = kernel(total_body, low(half, width), (*arrived, own), micros=40.0)
    rows = width // 8
    feed_kept, along1, along2 = kernel(
        feed_keep_body,
        [f32(4 * rows, width)] + [low(2 * rows, width)] * 2,
        (ids, *operands, after(feed_arrived, grad_normed)),
        smem=1,
        scratch=sides + [pltpu.VMEM((width, width), F32)],
        micros=0.1,
    )
    s = gather_low(grad_normed, "mp", mp_size)
    came = both_ways(along1, along2, seq_size)
    grad, grad_attended, small_attend = kernel(
        norm_back_body,
        [f32(4, half, width), low(slots, width), f32(SMALL_ROWS, width)],
        (ids, grad_normed, *s, unit, inv, row(attn_gain)),
        smem=1,
        micros=6.5,
    )
    own_input, o1, o2, o3, scores, stack, sums = kernel(
        functools.partial(attend_back_body, heads, query_scale),
        [f32(block_len, width)]
        + [low(block_len, width)] * 3
        + [f32(heads, full, slots), low(3 * part, full), f32(heads, 16, head)],
        (ids, grad, grad_attended, wq, wk, wv, out_weight, probs, qt, kt, vt),
        smem=1,
        scratch=[
            pltpu.VMEM((3 * part, width), LOW),
            pltpu.VMEM((part, slots), LOW),
            pltpu.VMEM((part, full), LOW),
            pltpu.VMEM((full, width), F32),
        ],
        micros=0.1,
    )
    rel = kernel(
        functools.partial(rel_body, heads, block_len, 32),
        f32(32, 128),
        (ids, scores),
        smem=1,
        scratch=[pltpu.VMEM((heads * BASES, 8, slots), F32)],
        micros=0.1,
    )
    half_rows = 2 * part + 128
    attend_keep, attend_send = kernel(
        attend_weights_body,
        [f32(half_rows, width), low(half_rows, width)],
        (ids, after(tokens, came), grad_attended, pooled_low, stack, ct, small_feed, small_attend, sums),
        smem=1,
        scratch=[pltpu.VMEM((2, half_rows, width), F32)],
        micros=0.1,
    )
    landed = scatter_low((o1, o2, o3), "mp", mp_size)
    attend_arrived = swap(attend_send, "dp", dp_size, 1)
    few = half_rows // 8
    attend_kept, feed_own, along1, along2 = kernel(
        step_a_body,
        [f32(4 * few, width), f32(2 * rows, width)] + [low(2 * few + rows, width)] * 2,
        (ids, attend_keep, attend_arrived, rel, feed_kept, *came),
        smem=1,
        scratch=[pltpu.VMEM((half_rows, width), F32)],
        micros=0.1,
    )
    met = kernel(touch_body, low(SMALL_ROWS, width), tuple(landed), micros=6.0)
    quarter = block_len // 4
    q0, *q = kernel(
        quarters_body,
        [low(quarter, width)] + [low(quarter + half, width)] * 3,
        (met, *landed, own_input, *outputs[1:]),
        micros=0.5,
    )
    attend_own, sent1, sent2 = kernel(
        step_b_body,
        [f32(2 * few, width)] + [low(few + 2 * rows, width)] * 2,
        (attend_kept, after(feed_own, q0), *both_ways(along1, along2, seq_size)),
        micros=0.1,
    )
    near = both_ways(sent1, sent2, seq_size)
    q = deep(scatter_low(q, "seq", seq_size))
    joined = kernel(join_body, low(block_len, width), (q0, *q), micros=8.0)
    spread = gather_low(joined, "mp", mp_size)
    mid = kernel(
        step_c_body, [low(few, width)] * 2, (after(attend_own, joined), *near), micros=0.1
    )
    output_all = kernel(output_body, low(4, half, width), (ids, outputs[0], *q), smem=1, micros=0.1)
    along1, along2 = kernel(
        step_d_body,
        [low(2 * few + rows, width)] * 2,
        (after(mid[0], output_all), mid[1], *both_ways(*mid, seq_size), *near),
        micros=0.1,
    )
    came = both_ways(along1, along2, seq_size)
    seen = kernel(touch_body, low(SMALL_ROWS, width), tuple(spread), micros=8.0)
    attend_mine, feed_mine = kernel(
        joins_body,
        [low(half_rows, width), low(width, width)],
        (ids, along1, along2, *came, sent1, sent2, *near, seen),
        smem=1,
        micros=0.2,
    )
    attend_mine, feed_mine = dp_sum((attend_mine, feed_mine), dp_size)
    attend_other = swap(attend_mine, "dp", dp_size, 1)
    feed_other = swap(feed_mine, "dp", dp_size, 1)
    wide = pltpu.VMEM((width, width), F32)
    sems = pltpu.SemaphoreType.DMA((4,))
    input_all, *halves = kernel(
        place_body,
        [f32(4, block_len, width)] + [f32(width, width)] * 2,
        (ids, joined, *spread, feed_mine),
        smem=1,
        scratch=[pltpu.VMEM((4, block_len, width), F32), wide, sems, sems],
        micros=0.1,
        hbm=range(3),
    )
    down_grad, up_grad, *rest = kernel(
        unpack_body,
        [f32(width, width)] * 2
        + [f32(width)] * 7
        + [f32(part)] * 2
        + [f32(heads, BASES)]
        + [f32(part, width)] * 4,
        (ids, attend_mine, attend_other, feed_other, *halves),
        smem=1,
        scratch=[pltpu.VMEM((4, part, width), F32), wide, sems, sems],
        micros=0.1,
        hbm=(0, 1, 12, 13, 14, 15),
        reused=2,
    )
    *small, query_sum, value_sum, rel_sum, dq, dk, dv, do = rest
    ffn_gain_sum, ffn_shift_sum, down_bias_sum, up_bias_sum, attn_gain_sum, attn_shift_sum, out_bias_sum = small
    return (
        output_all,
        input_all,
        dq.T,
        query_sum,
        dk.T,
        dv.T,
        value_sum,
        rel_sum,
        do,
        out_bias_sum,
        attn_gain_sum,
        attn_shift_sum,
        up_grad,
        up_bias_sum,
        down_grad,
        down_bias_sum,
        ffn_gain_sum,
        ffn_shift_sum,
    )


def solution(mesh):
    return jax.shard_map(
        shards,
        mesh=mesh,
        in_specs=(
            P("dp", "seq", None),
            P("dp"),
            P(None, "mp"),
            P("mp"),
            P(None, "mp"),
            P(None, "mp"),
            P("mp"),
            P("mp", None),
            P("mp", None),
            P(),
            P(),
            P(),
            P(None, "mp"),
            P("mp"),
            P("mp", None),
            P(),
            P(),
            P(),
            P("dp", "seq", None),
        ),
        out_specs=(
            P("dp", "seq", None),
            P("dp", "seq", None),
            P(None, "mp"),
            P("mp"),
            P(None, "mp"),
            P(None, "mp"),
            P("mp"),
            P("mp", None),
            P("mp", None),
            P(),
            P(),
            P(),
            P(None, "mp"),
            P("mp"),
            P("mp", None),
            P(),
            P(),
            P(),
        ),
        check_vma=False,
    )
```

```python
import functools

import jax
import jax.numpy as jnp
from jax import lax
from jax.experimental import pallas as pl
from jax.experimental.pallas import tpu as pltpu
from jax.sharding import PartitionSpec as P

BASES = 8
EPSILON = 1e-05
MASKED_SCORE = -1e30
F32 = jnp.float32
LOW = jnp.bfloat16
SMALL_ROWS = 16
MIB = 1024 * 1024
DEPTH = 2


def f32(*shape):
    return jax.ShapeDtypeStruct(shape, F32)


def low(*shape):
    return jax.ShapeDtypeStruct(shape, LOW)


def kernel(body, outs, args, smem=0, scratch=(), micros=1.0, limit=16, hbm=(), reused=0):
    in_specs = [pl.BlockSpec(memory_space=pltpu.SMEM)] * smem
    in_specs += [pl.BlockSpec(memory_space=pltpu.VMEM)] * (len(args) - smem - reused)
    in_specs += [pl.BlockSpec(memory_space=pltpu.HBM)] * reused
    whole = pl.BlockSpec(memory_space=pltpu.VMEM)
    if isinstance(outs, list):
        out_specs = [pl.BlockSpec(memory_space=pltpu.HBM) if n in hbm else whole for n in range(len(outs))]
    else:
        out_specs = whole
    return pl.pallas_call(
        body,
        out_shape=outs,
        in_specs=in_specs,
        out_specs=out_specs,
        scratch_shapes=list(scratch),
        input_output_aliases={len(args) - reused + n: n for n in range(reused)},
        compiler_params=pltpu.CompilerParams(vmem_limit_bytes=limit * MIB),
        cost_estimate=pl.CostEstimate(
            flops=int(micros * 4e8), bytes_accessed=int(micros * 3e6), transcendentals=0
        ),
    )(*args)


def after(value, *events):
    return lax.optimization_barrier((value, events))[0]


def dot_of(dims, a, b):
    return lax.dot_general(a, b, (dims, ((), ())), preferred_element_type=F32)


mm = functools.partial(dot_of, ((1,), (0,)))
mm_nt = functools.partial(dot_of, ((1,), (1,)))
mm_tn = functools.partial(dot_of, ((0,), (0,)))


def swap(block, axis, size, k):
    return lax.ppermute(block, axis, [(s, s ^ k) for s in range(size)])


def deep(values):
    for _ in range(DEPTH):
        values = lax.optimization_barrier(values)
    return values


def ordered(blocks, axis, size, order):
    landed = [swap(blocks[k - 1], axis, size, k) for k in order]
    landed = deep(landed) if axis == "mp" else landed
    return [landed[order.index(k)] for k in range(1, size)]


def gather_low(block, axis, size):
    return ordered([block] * (size - 1), axis, size, [1, 3, 2])


def scatter_low(blocks, axis, size):
    return ordered(blocks, axis, size, [2, 1, 3])


def pick(stacked, index):
    return lax.dynamic_index_in_dim(stacked, index, 0, keepdims=False)


def norm_stats(rows):
    center = rows - jnp.mean(rows, axis=-1, keepdims=True)
    scale_inv = lax.rsqrt(jnp.mean(center * center, axis=-1, keepdims=True) + EPSILON)
    return center * scale_inv, scale_inv


def norm_back(grad_out, normed, scale_inv, gain):
    grad_normed = grad_out * gain
    centered = grad_normed - jnp.mean(grad_normed, axis=-1, keepdims=True)
    return scale_inv * (centered - normed * jnp.mean(grad_normed * normed, axis=-1, keepdims=True))


def total_of(own_ref, arrived_refs):
    total = own_ref[...]
    for ref in arrived_refs:
        total = total + ref[...].astype(F32)
    return total


def pair_matrix(rows, cols, tall):
    r = lax.broadcasted_iota(jnp.int32, (rows, cols), 0)
    c = lax.broadcasted_iota(jnp.int32, (rows, cols), 1)
    hit = (r >> 1) == c if tall else r == (c >> 1)
    return jnp.where(hit, 0.5, 0.0).astype(LOW)


def distances(ids, chunk, rows, block_len, slots):
    j = ids[0]
    start = chunk * rows
    token = (j ^ (start // block_len)) * block_len + start % block_len
    token = token + lax.broadcasted_iota(jnp.int32, (rows, slots), 0)
    s = lax.broadcasted_iota(jnp.int32, (rows, slots), 1)
    half = block_len // 2
    slot = (j ^ (s // half)) * half + s % half
    return token, (token - 2 * slot).astype(F32)


def basis_of(distance, index, span):
    degree = index % (BASES // 2)
    inverse = 64.0 / (span * 4.0**degree)
    if index < BASES // 2:
        return jnp.exp(jnp.abs(distance) * (-inverse))
    return jnp.tanh(distance * inverse)


def bias_body(heads, block_len, rows, ids, rel, out):
    full, slots = out.shape[1:]

    def step(chunk, carry):
        token, distance = distances(ids, chunk, rows, block_len, slots)
        sums = [jnp.zeros((rows, slots), F32)] * heads
        for index in range(BASES):
            base = basis_of(distance, index, full)
            sums = [sums[h] + rel[h, index] * base for h in range(heads)]
        valid = token < ids[3]
        for h in range(heads):
            out[h, pl.ds(pl.multiple_of(chunk * rows, rows), rows), :] = jnp.where(valid, sums[h], MASKED_SCORE)
        return carry

    lax.fori_loop(0, full // rows, step, 0)


def rel_body(heads, block_len, rows, ids, scores_ref, out, acc):
    full, slots = scores_ref.shape[1:]
    acc[...] = jnp.zeros_like(acc)

    def step(chunk, carry):
        _, distance = distances(ids, chunk, rows, block_len, slots)
        at = pl.ds(pl.multiple_of(chunk * rows, rows), rows)
        grads = [scores_ref[h, at, :] for h in range(heads)]
        for index in range(BASES):
            base = basis_of(distance, index, full)
            for h in range(heads):
                acc[h * BASES + index] += jnp.sum((grads[h] * base).reshape(rows // 8, 8, slots), axis=0)
        return carry

    lax.fori_loop(0, full // rows, step, 0)
    for row in range(heads * BASES):
        col = jnp.sum(jnp.sum(acc[row], axis=0, keepdims=True), axis=1, keepdims=True)
        out[row : row + 1, :] = jnp.broadcast_to(col, (1, out.shape[1]))


def attend_body(heads, query_scale, ids, *refs):
    x = refs[:4]
    wq, wk, wv, wo, qb, vb, ob, bias, own_out, p1, p2, p3 = refs[4:16]
    probs_hbm, qt_hbm, kt_hbm, vt_hbm, ct_hbm, x_hbm = refs[16:22]
    scr, probs_ref, qt, kt, vt, ct, tokens, weights, sem = refs[22:]
    block_len = x[0].shape[0]
    half = block_len // 2
    part = wq.shape[0]
    head = part // heads
    copies = []

    def send(source, target):
        copy = pltpu.make_async_copy(source, target, sem.at[len(copies)])
        copy.start()
        copies.append(copy)

    for b in range(4):
        tokens[b * block_len : (b + 1) * block_len, :] = x[b][...]
    send(tokens, x_hbm)
    for n, w in enumerate((wk, wv, wq)):
        weights[n * part : (n + 1) * part, :] = w[...]
    product = mm_nt(weights[...], tokens[...])
    kt[...] = product[:part, :].astype(LOW)
    vt[...] = (product[part : 2 * part, :] + vb[...]).astype(LOW)
    pairs = pair_matrix(4 * block_len, 4 * half, True)
    projected = product[2 * part :, :]
    high = projected.astype(LOW)
    pooled = mm(high, pairs) + mm((projected - high.astype(F32)).astype(LOW), pairs)
    qt[...] = ((pooled + qb[...]) * query_scale).astype(LOW)
    send(kt, kt_hbm)
    send(vt, vt_hbm)
    send(qt, qt_hbm)
    for h in range(heads):
        at = slice(h * head, (h + 1) * head)
        scores = mm_tn(kt[at, :], qt[at, :]) + bias[h]
        grown = jnp.exp(scores - jnp.max(scores, axis=0, keepdims=True))
        probs = grown * (1.0 / jnp.sum(grown, axis=0, keepdims=True))
        probs_ref[h] = probs
        send(probs_ref.at[h], probs_hbm.at[h])
        ct[at, :] = mm(vt[at, :], probs.astype(LOW)).astype(LOW)
    send(ct, ct_hbm)
    turn = ids[0] ^ ids[1]
    mine = tokens[pl.ds(pl.multiple_of(turn * block_len, block_len), block_len), :]
    own_pooled = mm(pair_matrix(half, block_len, False), mine)
    result = mm_tn(ct[...], wo[...])
    scr[...] = result.reshape(scr.shape)
    own_out[...] = own_pooled + ob[...] + scr[turn]
    for k, out in ((1, p1), (2, p2), (3, p3)):
        out[...] = scr[turn ^ k].astype(LOW)
    for copy in copies:
        copy.wait()


def feed_body(ids, a0, a1, a2, a3, gain, shift, wu, ub, wd, db, own, p1, p2, p3, *refs):
    hidden_out, slope_out, normed_out, unit_out, inv_out, scr = refs
    rows, width = a0.shape
    turn = ids[0] ^ ids[1]
    for k, a in enumerate((a0, a1, a2, a3)):
        scr[turn ^ k] = a[...].astype(F32)
    unit, inv = norm_stats(scr[...].reshape(4 * rows, width))
    normed = unit * gain[...] + shift[...]
    unit_out[...] = unit
    inv_out[...] = jnp.broadcast_to(inv, inv_out.shape)
    normed_low = normed.astype(LOW)
    normed_out[...] = normed_low
    scr[...] = normed.reshape(scr.shape)
    own[...] = scr[turn] + db[...]
    up = mm(normed_low, wu[...]) + ub[...]
    phi = 0.5 * (1.0 + lax.erf(up * (0.5**0.5)))
    density = jnp.exp(up * up * -0.5) * 0.3989422804014327
    hidden = (up * phi).astype(LOW)
    hidden_out[...] = hidden
    slope_out[...] = phi + up * density
    scr[...] = mm(hidden, wd[...]).reshape(scr.shape)
    own[...] += scr[turn]
    for k, out in ((1, p1), (2, p2), (3, p3)):
        out[...] = scr[turn ^ k].astype(LOW)


def small_rows(*sums):
    return jnp.concatenate(list(sums) + [jnp.zeros((SMALL_ROWS - len(sums), sums[0].shape[1]), F32)])


def feed_back_body(ids, *refs):
    pieces, cots = refs[:4], refs[4:8]
    gain, shift, slope, wd, wu, own, p1, p2, p3 = refs[8:17]
    outs = refs[17:21]
    grad_out, upward_out, small_out, scr, low_scr = refs[21:]
    rows, width = own.shape
    slots = 4 * rows
    turn = ids[0] ^ ids[1]
    for k, piece in enumerate(pieces):
        scr[turn ^ k] = piece[...].astype(F32)
    unit, inv = norm_stats(scr[...].reshape(slots, width))
    s = lax.broadcasted_iota(jnp.int32, (slots, 1), 0)
    slot = (ids[0] ^ (s // rows)) * rows + s % rows
    valid = jnp.where(2 * slot < ids[3], 1.0, 0.0)
    output = ((unit * gain[...] + shift[...]) * valid).astype(LOW)
    for b in range(4):
        outs[b][...] = output[b * rows : (b + 1) * rows, :]
        low_scr[b * rows : (b + 1) * rows, :] = cots[b][...]
    top = low_scr[...].astype(F32) * valid
    grad = norm_back(top, unit, inv, gain[...])
    grad_low = grad.astype(LOW)
    grad_out[...] = grad_low
    scr[...] = grad.reshape(scr.shape)
    own[...] = scr[turn]
    hidden = mm_nt(grad_low, wd[...]).astype(LOW).astype(F32)
    upward = hidden * slope[...]
    upward_low = upward.astype(LOW)
    upward_out[...] = upward_low
    total = lambda a: jnp.sum(a, axis=0, keepdims=True)
    small_out[...] = small_rows(total(top * unit), total(top), total(grad), total(upward))
    scr[...] = mm_nt(upward_low, wu[...]).reshape(scr.shape)
    own[...] += scr[turn]
    for k, out in ((1, p1), (2, p2), (3, p3)):
        out[...] = scr[turn ^ k].astype(LOW)


def feed_product(which, hidden, grad, normed, upward, left, right, put):
    @pl.when(which == 0)
    def _():
        left[...] = hidden[...]
        right[...] = grad[...]

    @pl.when(which != 0)
    def _():
        left[...] = normed[...]
        right[...] = upward[...]

    step = 256
    for at in range(0, left.shape[1], step):
        put(slice(at, at + step), mm_tn(left[:, at : at + step], right[...]))


def first_step(base, total, kept, along1, along2):
    rows = along1[0] // 2
    block = lambda half, k: total(pl.ds(pl.multiple_of((4 * half + (base ^ k)) * rows, rows), rows))
    for n, (half, k) in enumerate(((0, 0), (0, 2), (1, 0), (1, 1))):
        kept[n * rows : (n + 1) * rows, :] = block(half, k)
    for (_, out), picks in ((along1, ((0, 1), (0, 3))), (along2, ((1, 2), (1, 3)))):
        for n, (half, k) in enumerate(picks):
            out[n * rows : (n + 1) * rows, :] = block(half, k).astype(LOW)


def second_step(kept, came1, came2, own, along1, along2):
    rows = along1.shape[0]
    part = lambda n: kept[n * rows : (n + 1) * rows, :]
    came = lambda ref, n: ref[n * rows : (n + 1) * rows, :].astype(F32)
    own[:rows, :] = part(0) + came(came1, 0)
    own[rows:, :] = part(2) + came(came2, 0)
    along2[...] = (part(1) + came(came1, 1)).astype(LOW)
    along1[...] = (part(3) + came(came2, 1)).astype(LOW)


def last_sums(own, came1, came2):
    rows = came1.shape[0]
    upper = own[:rows, :] + came2[...].astype(F32)
    lower = own[rows:, :] + came1[...].astype(F32)
    return upper.astype(LOW), lower.astype(LOW)


def join_half(base, mine1, mine2, came1, came2, out):
    rows = out.shape[0] // 8
    order = ((mine1, 0, (0, 2)), (came1, 0, (1, 3)), (mine2, 1, (0, 1)), (came2, 1, (2, 3)))
    for ref, half, ks in order:
        for n, k in enumerate(ks):
            at = pl.ds(pl.multiple_of((4 * half + (base ^ k)) * rows, rows), rows)
            out[at, :] = ref[n * rows : (n + 1) * rows, :]


def feed_send_body(ids, hidden, grad, normed, upward, out, left, right):
    def put(at, value):
        out[at, :] = value.astype(LOW)

    feed_product(1 - ids[2], hidden, grad, normed, upward, left, right, put)


def feed_keep_body(ids, hidden, grad, normed, upward, arrived, kept, along1, along2, left, right, scr):
    def put(at, value):
        scr[at, :] = value + arrived[at, :].astype(F32)

    feed_product(ids[2], hidden, grad, normed, upward, left, right, put)
    rows = along1.shape[0]
    first_step(ids[0], lambda at: scr[at, :], kept, (rows, along1), (rows, along2))


def step_a_body(ids, keep, arrived, rel, feed_kept, came1, came2, kept, feed_own, along1, along2, scr):
    rows = keep.shape[0] // 4
    scr[...] = keep[...] + arrived[...].astype(F32)
    scr[-rel.shape[0] :, : rel.shape[1]] = rel[...]
    first_step(ids[0], lambda at: scr[at, :], kept, (rows, along1), (rows, along2))
    second_step(feed_kept, came1, came2, feed_own, along1.at[rows:, :], along2.at[rows:, :])


def step_b_body(kept, feed_own, came1, came2, own, along1, along2):
    few = own.shape[0] // 2
    skip = 2 * few
    first = slice(0, skip)
    second_step(
        kept, came1.at[first, :], came2.at[first, :], own, along1.at[slice(0, few), :], along2.at[slice(0, few), :]
    )
    upper, lower = last_sums(feed_own, came1.at[skip:, :], came2.at[skip:, :])
    for out, parts in ((along1, (lower, upper)), (along2, (upper, lower))):
        for n, part in enumerate(parts):
            out[few + n * part.shape[0] : few + (n + 1) * part.shape[0], :] = part


def step_c_body(own, came1, came2, along1, along2):
    first = slice(0, along1.shape[0])
    along2[...], along1[...] = last_sums(own, came1.at[first, :], came2.at[first, :])


def step_d_body(mid1, mid2, came1, came2, near1, near2, along1, along2):
    few = mid1.shape[0]
    done = along1.shape[0] - 2 * few
    for out, own, came, near in ((along1, mid2, came2, near2), (along2, mid1, came1, near1)):
        out[:few, :] = own[...]
        out[few : 2 * few, :] = came[...]
        out[2 * few :, :] = near[few : few + done, :]


def joins_body(ids, along1, along2, came1, came2, sent1, sent2, near1, near2, seen, attend_out, out):
    join_half(ids[0], along1, along2, came1, came2, attend_out)
    rows = out.shape[0] // 8
    few = sent1.shape[0] - 2 * rows
    skip = came1.shape[0] - rows
    first, second, last = slice(few, few + rows), slice(few + rows, few + 2 * rows), slice(skip, skip + rows)
    upper = ((sent2, first), (near1, second), (near2, first), (came1, last))
    lower = ((sent1, first), (near1, first), (near2, second), (came2, last))
    for half, blocks in enumerate((upper, lower)):
        for k, (ref, at) in enumerate(blocks):
            to = pl.multiple_of((4 * half + (ids[0] ^ k)) * rows, rows)
            out[pl.ds(to, rows), :] = ref[at, :]


def norm_back_body(ids, *refs):
    pieces, (unit, inv, gain, grad_out, low_out, small_out) = refs[:4], refs[4:]
    turn = ids[0] ^ ids[1]
    for k, piece in enumerate(pieces):
        grad_out[turn ^ k] = piece[...].astype(F32)
    grad_normed = grad_out[...].reshape(unit.shape)
    grad = norm_back(grad_normed, unit[...], inv[:, :1], gain[...])
    grad_out[...] = grad.reshape(grad_out.shape)
    low_out[...] = grad.astype(LOW)
    total = lambda a: jnp.sum(a, axis=0, keepdims=True)
    small_out[...] = small_rows(total(grad_normed * unit[...]), total(grad_normed), total(grad))


def row_sums(rows):
    high = rows.astype(LOW)
    rest = (rows - high.astype(F32)).astype(LOW)
    ones = jnp.ones((8, rows.shape[1]), LOW)
    return mm_nt(ones, high) + mm_nt(ones, rest)


def attend_back_body(heads, query_scale, ids, *refs):
    grad, grad_low, wq, wk, wv, wo, probs_ref, qt, kt, vt = refs[:10]
    o = refs[10:14]
    scores_out, stack, sums_out, weights, dct, grad_q, result = refs[14:]
    part = wq.shape[0]
    head = part // heads
    slots, full = qt.shape[1], kt.shape[1]
    half, block_len = slots // 4, full // 4
    quarter = block_len // 4
    weights[:part, :] = wk[...]
    weights[part : 2 * part, :] = wv[...]
    weights[2 * part :, :] = wq[...]
    dct[...] = mm_nt(wo[...], grad_low[...]).astype(LOW)
    for h in range(heads):
        at = slice(h * head, (h + 1) * head)
        probs = probs_ref[h]
        grad_probs = mm_tn(vt[at, :], dct[at, :])
        grad_values = mm_nt(dct[at, :], probs.astype(LOW))
        scores = probs * (grad_probs - jnp.sum(probs * grad_probs, axis=0, keepdims=True))
        scores_out[h] = scores
        scores_low = scores.astype(LOW)
        grad_queries = mm(kt[at, :], scores_low) * query_scale
        stack[at, :] = mm_nt(qt[at, :], scores_low).astype(LOW)
        stack[part + h * head : part + (h + 1) * head, :] = grad_values.astype(LOW)
        grad_q[at, :] = grad_queries.astype(LOW)
        sums_out[h, :8, :] = row_sums(grad_queries)
        sums_out[h, 8:, :] = row_sums(grad_values)
    stack[2 * part :, :] = mm(grad_q[...], pair_matrix(slots, full, False)).astype(LOW)
    result[...] = mm_tn(stack[...], weights[...])
    spread = pair_matrix(quarter, quarter // 2, True)
    for b in range(4):
        to = slice(b * quarter, (b + 1) * quarter)
        rows = lambda k: pl.ds(pl.multiple_of(b * block_len + (ids[1] ^ k) * quarter, quarter), quarter)
        residual = grad[b, pl.ds(pl.multiple_of(ids[1] * (quarter // 2), quarter // 2), quarter // 2), :]
        high = residual.astype(LOW)
        rest = (residual - high.astype(F32)).astype(LOW)
        o[0][to, :] = result[rows(0), :] + (mm(spread, high) + mm(spread, rest))
        for k in range(1, 4):
            o[k][to, :] = result[rows(k), :].astype(LOW)


def attend_weights_body(ids, x, grad, stack, ct, small_feed, small_attend, sums, keep, send, scr):
    part = ct.shape[0]
    heads = sums.shape[0]
    product = mm(stack[...], x[...])
    scr[0, part : 2 * part, :] = product[:part]
    scr[1, :part, :] = product[part : 2 * part]
    scr[0, :part, :] = product[2 * part :]
    scr[1, part : 2 * part, :] = mm(ct[...], grad[...])
    scr[:, 2 * part :, :] = jnp.zeros((2, scr.shape[1] - 2 * part, scr.shape[2]), F32)
    scr[0, 2 * part : 2 * part + SMALL_ROWS, :] = small_feed[...]
    scr[0, 2 * part + SMALL_ROWS : 2 * part + 2 * SMALL_ROWS, :] = small_attend[...]
    for h in range(heads):
        scr[1, 2 * part + h * SMALL_ROWS : 2 * part + (h + 1) * SMALL_ROWS, : sums.shape[2]] = sums[h]
    keep[...] = scr[ids[2]]
    send[...] = scr[1 - ids[2]].astype(LOW)


def total_body(r1, r2, r3, own, out):
    out[...] = total_of(own, (r1, r2, r3)).astype(LOW)


def sender(sem):
    copies = []

    def send(source, target):
        copy = pltpu.make_async_copy(source, target, sem.at[len(copies)])
        copy.start()
        copies.append(copy)

    def wait():
        for copy in copies:
            copy.wait()

    return send, wait


def widen(which, rows, first, second, scr, sem):
    step = rows.shape[0] // 4
    for n in range(4):
        span = pl.ds(n * step, step)
        scr[span, :] = rows[span, :].astype(F32)
        for c, out in ((0, first), (1, second)):

            @pl.when(which == c)
            def _(out=out, n=n, span=span):
                copy = pltpu.make_async_copy(scr.at[span, :], out.at[span, :], sem.at[n])
                copy.start()


def widen_wait(which, first, second, scr, sem):
    step = scr.shape[0] // 4
    for n in range(4):
        span = pl.ds(n * step, step)
        for c, out in ((0, first), (1, second)):

            @pl.when(which == c)
            def _(out=out, n=n, span=span):
                pltpu.make_async_copy(scr.at[span, :], out.at[span, :], sem.at[n]).wait()


def output_body(ids, n0, q1, q2, q3, output):
    rows = n0.shape[0]
    output[ids[0]] = n0[...]
    for b, q in ((1, q1), (2, q2), (3, q3)):
        output[ids[0] ^ b] = q[q.shape[0] - rows :, :]


def unpack_body(ids, mine, other, feed_other, _first, _second, first, second, *rest):
    *rows_out, query_out, value_out, rel_out, dq, dk, dv, do, scr, wide, sem, wide_sem = rest
    widen(1 - ids[2], feed_other, first, second, wide, wide_sem)
    unpack_attend(ids, mine, other, rows_out, query_out, value_out, rel_out, (dq, dk, dv, do), scr, sem)
    widen_wait(1 - ids[2], first, second, wide, wide_sem)


def unpack_attend(ids, mine, other, rows_out, query_out, value_out, rel_out, larges, scr, sem):
    part = larges[0].shape[0]
    heads = rel_out.shape[0]
    head = part // heads
    send, wait = sender(sem)
    for c, (a, b) in ((0, (mine, other)), (1, (other, mine))):

        @pl.when(ids[2] == c)
        def _(a=a, b=b):
            for n, half in enumerate((a, a, b, b)):
                scr[n] = half[n % 2 * part : (n % 2 + 1) * part, :].astype(F32)

    for n, out in enumerate(larges):
        send(scr.at[n], out)
    for c, (a, b) in ((0, (mine, other)), (1, (other, mine))):

        @pl.when(ids[2] == c)
        def _(a=a, b=b):
            small_a = a[2 * part :, :].astype(F32)
            small_b = b[2 * part :, :].astype(F32)
            for n, out in enumerate(rows_out):
                row = n if n < 4 else SMALL_ROWS + n - 4
                out[...] = small_a[row, :]
            for out, row in ((query_out, 0), (value_out, 8)):
                out[...] = jnp.concatenate(
                    [small_b[h * SMALL_ROWS + row : h * SMALL_ROWS + row + 1, :head] for h in range(heads)], axis=1
                )[0]
            last = small_a.shape[0] - 32
            table = small_a[last:, :128] + small_b[last:, :128]
            for h in range(heads):
                for index in range(BASES):
                    at = h * BASES + index
                    rel_out[h : h + 1, index : index + 1] = table[at : at + 1, :1]

    wait()


def quarters_body(met, r1, r2, r3, own, n1, n2, n3, q0, q1, q2, q3):
    total = total_of(own, (r1, r2, r3)).astype(LOW)
    rows = q0.shape[0]
    q0[...] = total[:rows]
    for b, (q, n) in enumerate(((q1, n1), (q2, n2), (q3, n3)), 1):
        q[:rows, :] = total[b * rows : (b + 1) * rows]
        q[rows:, :] = n[...]


def join_body(q0, q1, q2, q3, joined):
    rows = q0.shape[0]
    for b, q in enumerate((q0, q1, q2, q3)):
        joined[b * rows : (b + 1) * rows, :] = q[:rows, :]


def touch_body(t1, t2, t3, out):
    rows = out.shape[0]
    out[...] = t1[:rows, :] + t2[:rows, :] + t3[:rows, :]


def place_body(ids, t0, t1, t2, t3, mine, out, first, second, scr, wide, sem, wide_sem):
    send, wait = sender(sem)
    rows = scr.shape[1] // 4
    for b in range(4):
        for k, t in enumerate((t0, t1, t2, t3)):
            at = pl.ds(pl.multiple_of((ids[1] ^ k) * rows, rows), rows)
            scr[b, at, :] = t[b * rows : (b + 1) * rows, :].astype(out.dtype)
        send(scr.at[b], out.at[ids[0] ^ b])
    widen(ids[2], mine, first, second, wide, wide_sem)
    wait()
    widen_wait(ids[2], first, second, wide, wide_sem)


def dp_sum(values, dp_size):
    step = 2
    while step < dp_size:
        values = [
            (v.astype(F32) + swap(v, "dp", dp_size, step).astype(F32)).astype(v.dtype) for v in values
        ]
        step *= 2
    return values


def both_ways(along1, along2, size):
    return swap(along1, "seq", size, 1), swap(along2, "seq", size, 2)


def shards(
    inputs,
    lengths,
    query_weight,
    query_bias,
    key_weight,
    value_weight,
    value_bias,
    rel_weight,
    out_weight,
    out_bias,
    attn_gain,
    attn_shift,
    up_weight,
    up_bias,
    down_weight,
    down_bias,
    ffn_gain,
    ffn_shift,
    cotangent,
):
    seq_size, dp_size, mp_size = (lax.axis_size(a) for a in ("seq", "dp", "mp"))
    j, m, c = lax.axis_index("seq"), lax.axis_index("mp"), lax.axis_index("dp") % 2
    sentences, block_len, width = inputs.shape
    assert sentences == seq_size == mp_size == 4 and dp_size % 2 == 0
    half = block_len // 2
    full, slots = 4 * block_len, 4 * half
    heads = rel_weight.shape[0]
    part = query_weight.shape[1]
    head = part // heads
    hidden_here = up_weight.shape[1]
    assert hidden_here == width
    query_scale = head ** (-0.5)
    row = lambda v: v.reshape(1, -1)
    column = lambda v: v.reshape(-1, 1)
    ids = jnp.stack([j, m, c, pick(lengths, j)]).astype(jnp.int32)
    wq, wk, wv = query_weight.T, key_weight.T, value_weight.T

    x = [pick(inputs, j)] + [swap(pick(inputs, j ^ k), "seq", seq_size, k) for k in range(1, 4)]
    bias = kernel(
        functools.partial(bias_body, heads, block_len, 32), f32(heads, full, slots), (ids, rel_weight), smem=2, micros=3.0
    )
    own, p1, p2, p3, probs, qt, kt, vt, ct, tokens = kernel(
        functools.partial(attend_body, heads, query_scale),
        [f32(half, width)]
        + [low(half, width)] * 3
        + [f32(heads, full, slots), low(part, slots), low(part, full), low(part, full), low(part, slots)]
        + [low(full, width)],
        (ids, *x, wq, wk, wv, out_weight, column(query_bias), column(value_bias), row(out_bias), bias),
        smem=1,
        scratch=[
            pltpu.VMEM((4, half, width), F32),
            pltpu.VMEM((heads, full, slots), F32),
            pltpu.VMEM((part, slots), LOW),
            pltpu.VMEM((part, full), LOW),
            pltpu.VMEM((part, full), LOW),
            pltpu.VMEM((part, slots), LOW),
            pltpu.VMEM((full, width), LOW),
            pltpu.VMEM((3 * part, width), LOW),
            pltpu.SemaphoreType.DMA((5 + heads,)),
        ],
        micros=5.0,
        hbm=range(4, 10),
    )
    arrived = scatter_low((p1, p2, p3), "mp", mp_size)
    attended = kernel(total_body, low(half, width), (*arrived, own), micros=0.5)
    later = after(cotangent, attended)
    cots = [pick(later, j)] + [swap(pick(later, j ^ k), "seq", seq_size, k) for k in range(1, 4)]
    own, p1, p2, p3, hidden, slope, normed, unit, inv = kernel(
        feed_body,
        [f32(half, width)]
        + [low(half, width)] * 3
        + [low(slots, hidden_here), f32(slots, hidden_here), low(slots, width), f32(slots, width), f32(slots, 128)],
        (ids, attended, *gather_low(attended, "mp", mp_size), row(attn_gain), row(attn_shift), up_weight)
        + (row(up_bias), down_weight, row(down_bias)),
        smem=1,
        scratch=[pltpu.VMEM((4, half, width), F32)],
        micros=3.0,
    )
    p1, p2, p3 = after((p1, p2, p3), cots)
    mixed = kernel(total_body, low(half, width), (*scatter_low((p1, p2, p3), "mp", mp_size), own), micros=0.5)
    own, p1, p2, p3, *rest = kernel(
        feed_back_body,
        [f32(half, width)]
        + [low(half, width)] * 7
        + [low(slots, width), low(slots, hidden_here), f32(SMALL_ROWS, width)],
        (ids, mixed, *gather_low(mixed, "mp", mp_size), *cots, row(ffn_gain), row(ffn_shift), slope)
        + (down_weight, up_weight),
        smem=1,
        scratch=[pltpu.VMEM((4, half, width), F32), pltpu.VMEM((slots, width), LOW)],
        micros=3.0,
    )
    outputs, (grad_mixed, upward, small_feed) = rest[:4], rest[4:]
    operands = (hidden, grad_mixed, normed, upward)
    sides = [pltpu.VMEM((slots, width), LOW)] * 2
    feed_send = kernel(
        feed_send_body, low(width, width), (ids, *operands), smem=1, scratch=sides, micros=0.1
    )
    feed_arrived = swap(feed_send, "dp", dp_size, 1)
    arrived = scatter_low((p1, p2, p3), "mp", mp_size)
    grad_normed = kernel(total_body, low(half, width), (*arrived, own), micros=40.0)
    rows = width // 8
    feed_kept, along1, along2 = kernel(
        feed_keep_body,
        [f32(4 * rows, width)] + [low(2 * rows, width)] * 2,
        (ids, *operands, after(feed_arrived, grad_normed)),
        smem=1,
        scratch=sides + [pltpu.VMEM((width, width), F32)],
        micros=0.1,
    )
    s = gather_low(grad_normed, "mp", mp_size)
    came = both_ways(along1, along2, seq_size)
    grad, grad_attended, small_attend = kernel(
        norm_back_body,
        [f32(4, half, width), low(slots, width), f32(SMALL_ROWS, width)],
        (ids, grad_normed, *s, unit, inv, row(attn_gain)),
        smem=1,
        micros=6.5,
    )
    own_input, o1, o2, o3, scores, stack, sums = kernel(
        functools.partial(attend_back_body, heads, query_scale),
        [f32(block_len, width)]
        + [low(block_len, width)] * 3
        + [f32(heads, full, slots), low(3 * part, full), f32(heads, 16, head)],
        (ids, grad, grad_attended, wq, wk, wv, out_weight, probs, qt, kt, vt),
        smem=1,
        scratch=[
            pltpu.VMEM((3 * part, width), LOW),
            pltpu.VMEM((part, slots), LOW),
            pltpu.VMEM((part, slots), LOW),
            pltpu.VMEM((full, width), F32),
        ],
        micros=0.1,
    )
    rel = kernel(
        functools.partial(rel_body, heads, block_len, 32),
        f32(32, 128),
        (ids, scores),
        smem=1,
        scratch=[pltpu.VMEM((heads * BASES, 8, slots), F32)],
        micros=0.1,
    )
    half_rows = 2 * part + 128
    attend_keep, attend_send = kernel(
        attend_weights_body,
        [f32(half_rows, width), low(half_rows, width)],
        (ids, after(tokens, came), grad_attended, stack, ct, small_feed, small_attend, sums),
        smem=1,
        scratch=[pltpu.VMEM((2, half_rows, width), F32)],
        micros=0.1,
    )
    landed = scatter_low((o1, o2, o3), "mp", mp_size)
    attend_arrived = swap(attend_send, "dp", dp_size, 1)
    few = half_rows // 8
    attend_kept, feed_own, along1, along2 = kernel(
        step_a_body,
        [f32(4 * few, width), f32(2 * rows, width)] + [low(2 * few + rows, width)] * 2,
        (ids, attend_keep, attend_arrived, rel, feed_kept, *came),
        smem=1,
        scratch=[pltpu.VMEM((half_rows, width), F32)],
        micros=0.1,
    )
    met = kernel(touch_body, low(SMALL_ROWS, width), tuple(landed), micros=6.0)
    quarter = block_len // 4
    q0, *q = kernel(
        quarters_body,
        [low(quarter, width)] + [low(quarter + half, width)] * 3,
        (met, *landed, own_input, *outputs[1:]),
        micros=0.5,
    )
    attend_own, sent1, sent2 = kernel(
        step_b_body,
        [f32(2 * few, width)] + [low(few + 2 * rows, width)] * 2,
        (attend_kept, after(feed_own, q0), *both_ways(along1, along2, seq_size)),
        micros=0.1,
    )
    near = both_ways(sent1, sent2, seq_size)
    q = [swap(q[k - 1], "seq", seq_size, k) for k in [2, 1, 3]]
    q = deep(q)
    q = [q[[2, 1, 3].index(k)] for k in range(1, 4)]
    joined = kernel(join_body, low(block_len, width), (q0, *q), micros=8.0)
    spread = gather_low(joined, "mp", mp_size)
    mid = kernel(
        step_c_body, [low(few, width)] * 2, (after(attend_own, joined), *near), micros=0.1
    )
    output_all = kernel(output_body, low(4, half, width), (ids, outputs[0], *q), smem=1, micros=0.1)
    along1, along2 = kernel(
        step_d_body,
        [low(2 * few + rows, width)] * 2,
        (after(mid[0], output_all), mid[1], *both_ways(*mid, seq_size), *near),
        micros=0.1,
    )
    came = both_ways(along1, along2, seq_size)
    seen = kernel(touch_body, low(SMALL_ROWS, width), tuple(spread), micros=8.0)
    attend_mine, feed_mine = kernel(
        joins_body,
        [low(half_rows, width), low(width, width)],
        (ids, along1, along2, *came, sent1, sent2, *near, seen),
        smem=1,
        micros=0.2,
    )
    attend_mine, feed_mine = dp_sum((attend_mine, feed_mine), dp_size)
    attend_other = swap(attend_mine, "dp", dp_size, 1)
    feed_other = swap(feed_mine, "dp", dp_size, 1)
    wide = pltpu.VMEM((width, width), F32)
    sems = pltpu.SemaphoreType.DMA((4,))
    input_all, *halves = kernel(
        place_body,
        [f32(4, block_len, width)] + [f32(width, width)] * 2,
        (ids, joined, *spread, feed_mine),
        smem=1,
        scratch=[pltpu.VMEM((4, block_len, width), F32), wide, sems, sems],
        micros=0.1,
        hbm=range(3),
    )
    down_grad, up_grad, *rest = kernel(
        unpack_body,
        [f32(width, width)] * 2
        + [f32(width)] * 7
        + [f32(part)] * 2
        + [f32(heads, BASES)]
        + [f32(part, width)] * 4,
        (ids, attend_mine, attend_other, feed_other, *halves),
        smem=1,
        scratch=[pltpu.VMEM((4, part, width), F32), wide, sems, sems],
        micros=0.1,
        hbm=(0, 1, 12, 13, 14, 15),
        reused=2,
    )
    *small, query_sum, value_sum, rel_sum, dq, dk, dv, do = rest
    ffn_gain_sum, ffn_shift_sum, down_bias_sum, up_bias_sum, attn_gain_sum, attn_shift_sum, out_bias_sum = small
    return (
        output_all,
        input_all,
        dq.T,
        query_sum,
        dk.T,
        dv.T,
        value_sum,
        rel_sum,
        do,
        out_bias_sum,
        attn_gain_sum,
        attn_shift_sum,
        up_grad,
        up_bias_sum,
        down_grad,
        down_bias_sum,
        ffn_gain_sum,
        ffn_shift_sum,
    )


def solution(mesh):
    return jax.shard_map(
        shards,
        mesh=mesh,
        in_specs=(
            P("dp", "seq", None),
            P("dp"),
            P(None, "mp"),
            P("mp"),
            P(None, "mp"),
            P(None, "mp"),
            P("mp"),
            P("mp", None),
            P("mp", None),
            P(),
            P(),
            P(),
            P(None, "mp"),
            P("mp"),
            P("mp", None),
            P(),
            P(),
            P(),
            P("dp", "seq", None),
        ),
        out_specs=(
            P("dp", "seq", None),
            P("dp", "seq", None),
            P(None, "mp"),
            P("mp"),
            P(None, "mp"),
            P(None, "mp"),
            P("mp"),
            P("mp", None),
            P("mp", None),
            P(),
            P(),
            P(),
            P(None, "mp"),
            P("mp"),
            P("mp", None),
            P(),
            P(),
            P(),
        ),
        check_vma=False,
    )
```

```python
import functools

import jax
import jax.numpy as jnp
from jax import lax
from jax.experimental import pallas as pl
from jax.experimental.pallas import tpu as pltpu
from jax.sharding import PartitionSpec as P

BASES = 8
EPSILON = 1e-05
MASKED_SCORE = -1e30
F32 = jnp.float32
LOW = jnp.bfloat16
SMALL_ROWS = 16
MIB = 1024 * 1024
DEPTH = 2


def f32(*shape):
    return jax.ShapeDtypeStruct(shape, F32)


def low(*shape):
    return jax.ShapeDtypeStruct(shape, LOW)


def kernel(body, outs, args, smem=0, scratch=(), micros=1.0, limit=16, hbm=(), reused=0):
    in_specs = [pl.BlockSpec(memory_space=pltpu.SMEM)] * smem
    in_specs += [pl.BlockSpec(memory_space=pltpu.VMEM)] * (len(args) - smem - reused)
    in_specs += [pl.BlockSpec(memory_space=pltpu.HBM)] * reused
    whole = pl.BlockSpec(memory_space=pltpu.VMEM)
    if isinstance(outs, list):
        out_specs = [pl.BlockSpec(memory_space=pltpu.HBM) if n in hbm else whole for n in range(len(outs))]
    else:
        out_specs = whole
    return pl.pallas_call(
        body,
        out_shape=outs,
        in_specs=in_specs,
        out_specs=out_specs,
        scratch_shapes=list(scratch),
        input_output_aliases={len(args) - reused + n: n for n in range(reused)},
        compiler_params=pltpu.CompilerParams(vmem_limit_bytes=limit * MIB),
        cost_estimate=pl.CostEstimate(
            flops=int(micros * 4e8), bytes_accessed=int(micros * 3e6), transcendentals=0
        ),
    )(*args)


def after(value, *events):
    return lax.optimization_barrier((value, events))[0]


def dot_of(dims, a, b):
    return lax.dot_general(a, b, (dims, ((), ())), preferred_element_type=F32)


mm = functools.partial(dot_of, ((1,), (0,)))
mm_nt = functools.partial(dot_of, ((1,), (1,)))
mm_tn = functools.partial(dot_of, ((0,), (0,)))


def swap(block, axis, size, k):
    return lax.ppermute(block, axis, [(s, s ^ k) for s in range(size)])


def deep(values):
    for _ in range(DEPTH):
        values = lax.optimization_barrier(values)
    return values


def ordered(blocks, axis, size, order):
    landed = [swap(blocks[k - 1], axis, size, k) for k in order]
    landed = deep(landed) if axis == "mp" else landed
    return [landed[order.index(k)] for k in range(1, size)]


def gather_low(block, axis, size):
    return ordered([block] * (size - 1), axis, size, [1, 3, 2])


def scatter_low(blocks, axis, size):
    return ordered(blocks, axis, size, [2, 1, 3])


def pick(stacked, index):
    return lax.dynamic_index_in_dim(stacked, index, 0, keepdims=False)


def norm_stats(rows):
    center = rows - jnp.mean(rows, axis=-1, keepdims=True)
    scale_inv = lax.rsqrt(jnp.mean(center * center, axis=-1, keepdims=True) + EPSILON)
    return center * scale_inv, scale_inv


def norm_back(grad_out, normed, scale_inv, gain):
    grad_normed = grad_out * gain
    centered = grad_normed - jnp.mean(grad_normed, axis=-1, keepdims=True)
    return scale_inv * (centered - normed * jnp.mean(grad_normed * normed, axis=-1, keepdims=True))


def total_of(own_ref, arrived_refs):
    total = own_ref[...]
    for ref in arrived_refs:
        total = total + ref[...].astype(F32)
    return total


def pair_matrix(rows, cols, tall):
    r = lax.broadcasted_iota(jnp.int32, (rows, cols), 0)
    c = lax.broadcasted_iota(jnp.int32, (rows, cols), 1)
    hit = (r >> 1) == c if tall else r == (c >> 1)
    return jnp.where(hit, 0.5, 0.0).astype(LOW)


def distances(ids, chunk, rows, block_len, slots):
    j = ids[0]
    start = chunk * rows
    token = (j ^ (start // block_len)) * block_len + start % block_len
    token = token + lax.broadcasted_iota(jnp.int32, (rows, slots), 0)
    s = lax.broadcasted_iota(jnp.int32, (rows, slots), 1)
    half = block_len // 2
    slot = (j ^ (s // half)) * half + s % half
    return token, (token - 2 * slot).astype(F32)


def basis_of(distance, index, span):
    degree = index % (BASES // 2)
    inverse = 64.0 / (span * 4.0**degree)
    if index < BASES // 2:
        return jnp.exp(jnp.abs(distance) * (-inverse))
    return jnp.tanh(distance * inverse)


def bias_body(heads, block_len, rows, ids, rel, out):
    full, slots = out.shape[1:]

    def step(chunk, carry):
        token, distance = distances(ids, chunk, rows, block_len, slots)
        sums = [jnp.zeros((rows, slots), F32)] * heads
        for index in range(BASES):
            base = basis_of(distance, index, full)
            sums = [sums[h] + rel[h, index] * base for h in range(heads)]
        valid = token < ids[3]
        for h in range(heads):
            out[h, pl.ds(pl.multiple_of(chunk * rows, rows), rows), :] = jnp.where(valid, sums[h], MASKED_SCORE)
        return carry

    lax.fori_loop(0, full // rows, step, 0)


def rel_body(heads, block_len, rows, ids, scores_ref, out, acc):
    full, slots = scores_ref.shape[1:]
    acc[...] = jnp.zeros_like(acc)

    def step(chunk, carry):
        _, distance = distances(ids, chunk, rows, block_len, slots)
        at = pl.ds(pl.multiple_of(chunk * rows, rows), rows)
        grads = [scores_ref[h, at, :] for h in range(heads)]
        for index in range(BASES):
            base = basis_of(distance, index, full)
            for h in range(heads):
                acc[h * BASES + index] += jnp.sum((grads[h] * base).reshape(rows // 8, 8, slots), axis=0)
        return carry

    lax.fori_loop(0, full // rows, step, 0)
    lane = lax.broadcasted_iota(jnp.int32, (1, out.shape[1]), 1)
    line = jnp.zeros((1, out.shape[1]), F32)
    for row in range(heads * BASES):
        col = jnp.sum(jnp.sum(acc[row], axis=0, keepdims=True), axis=1, keepdims=True)
        line = jnp.where(lane == row, col, line)
    out[...] = jnp.broadcast_to(line, out.shape)


def attend_body(heads, query_scale, ids, *refs):
    x = refs[:4]
    wq, wk, wv, wo, qb, vb, ob, bias, own_out, p1, p2, p3 = refs[4:16]
    probs_hbm, qt_hbm, kt_hbm, vt_hbm, ct_hbm, x_hbm = refs[16:22]
    scr, probs_ref, qt, kt, vt, ct, tokens, weights, sem = refs[22:]
    block_len = x[0].shape[0]
    half = block_len // 2
    part = wq.shape[0]
    head = part // heads
    copies = []

    def send(source, target):
        copy = pltpu.make_async_copy(source, target, sem.at[len(copies)])
        copy.start()
        copies.append(copy)

    for b in range(4):
        tokens[b * block_len : (b + 1) * block_len, :] = x[b][...]
    send(tokens, x_hbm)
    for n, w in enumerate((wk, wv, wq)):
        weights[n * part : (n + 1) * part, :] = w[...]
    product = mm_nt(weights[...], tokens[...])
    kt[...] = product[:part, :].astype(LOW)
    vt[...] = (product[part : 2 * part, :] + vb[...]).astype(LOW)
    pairs = pair_matrix(4 * block_len, 4 * half, True)
    projected = product[2 * part :, :]
    high = projected.astype(LOW)
    pooled = mm(high, pairs) + mm((projected - high.astype(F32)).astype(LOW), pairs)
    qt[...] = ((pooled + qb[...]) * query_scale).astype(LOW)
    send(kt, kt_hbm)
    send(vt, vt_hbm)
    send(qt, qt_hbm)
    for h in range(heads):
        at = slice(h * head, (h + 1) * head)
        scores = mm_tn(kt[at, :], qt[at, :]) + bias[h]
        grown = jnp.exp(scores - jnp.max(scores, axis=0, keepdims=True))
        probs = grown * (1.0 / jnp.sum(grown, axis=0, keepdims=True))
        probs_ref[h] = probs
        send(probs_ref.at[h], probs_hbm.at[h])
        ct[at, :] = mm(vt[at, :], probs.astype(LOW)).astype(LOW)
    send(ct, ct_hbm)
    turn = ids[0] ^ ids[1]
    mine = tokens[pl.ds(pl.multiple_of(turn * block_len, block_len), block_len), :]
    own_pooled = mm(pair_matrix(half, block_len, False), mine)
    result = mm_tn(ct[...], wo[...])
    scr[...] = result.reshape(scr.shape)
    own_out[...] = own_pooled + ob[...] + scr[turn]
    for k, out in ((1, p1), (2, p2), (3, p3)):
        out[...] = scr[turn ^ k].astype(LOW)
    for copy in copies:
        copy.wait()


def feed_body(ids, a0, a1, a2, a3, gain, shift, wu, ub, wd, db, own, p1, p2, p3, *refs):
    hidden_out, slope_out, normed_out, unit_out, inv_out, scr = refs
    rows, width = a0.shape
    turn = ids[0] ^ ids[1]
    for k, a in enumerate((a0, a1, a2, a3)):
        scr[turn ^ k] = a[...].astype(F32)
    unit, inv = norm_stats(scr[...].reshape(4 * rows, width))
    normed = unit * gain[...] + shift[...]
    unit_out[...] = unit
    inv_out[...] = jnp.broadcast_to(inv, inv_out.shape)
    normed_low = normed.astype(LOW)
    normed_out[...] = normed_low
    scr[...] = normed.reshape(scr.shape)
    own[...] = scr[turn] + db[...]
    up = mm(normed_low, wu[...]) + ub[...]
    phi = 0.5 * (1.0 + lax.erf(up * (0.5**0.5)))
    density = jnp.exp(up * up * -0.5) * 0.3989422804014327
    hidden = (up * phi).astype(LOW)
    hidden_out[...] = hidden
    slope_out[...] = phi + up * density
    scr[...] = mm(hidden, wd[...]).reshape(scr.shape)
    own[...] += scr[turn]
    for k, out in ((1, p1), (2, p2), (3, p3)):
        out[...] = scr[turn ^ k].astype(LOW)


def small_rows(*sums):
    return jnp.concatenate(list(sums) + [jnp.zeros((SMALL_ROWS - len(sums), sums[0].shape[1]), F32)])


def feed_back_body(ids, *refs):
    pieces, cots = refs[:4], refs[4:8]
    gain, shift, slope, wd, wu, own, p1, p2, p3 = refs[8:17]
    outs = refs[17:21]
    grad_out, upward_out, small_out, scr, low_scr = refs[21:]
    rows, width = own.shape
    slots = 4 * rows
    turn = ids[0] ^ ids[1]
    for k, piece in enumerate(pieces):
        scr[turn ^ k] = piece[...].astype(F32)
    unit, inv = norm_stats(scr[...].reshape(slots, width))
    s = lax.broadcasted_iota(jnp.int32, (slots, 1), 0)
    slot = (ids[0] ^ (s // rows)) * rows + s % rows
    valid = jnp.where(2 * slot < ids[3], 1.0, 0.0)
    output = ((unit * gain[...] + shift[...]) * valid).astype(LOW)
    for b in range(4):
        outs[b][...] = output[b * rows : (b + 1) * rows, :]
        low_scr[b * rows : (b + 1) * rows, :] = cots[b][...]
    top = low_scr[...].astype(F32) * valid
    grad = norm_back(top, unit, inv, gain[...])
    grad_low = grad.astype(LOW)
    grad_out[...] = grad_low
    scr[...] = grad.reshape(scr.shape)
    own[...] = scr[turn]
    hidden = mm_nt(grad_low, wd[...]).astype(LOW).astype(F32)
    upward = hidden * slope[...]
    upward_low = upward.astype(LOW)
    upward_out[...] = upward_low
    total = lambda a: jnp.sum(a, axis=0, keepdims=True)
    small_out[...] = small_rows(total(top * unit), total(top), total(grad), total(upward))
    scr[...] = mm_nt(upward_low, wu[...]).reshape(scr.shape)
    own[...] += scr[turn]
    for k, out in ((1, p1), (2, p2), (3, p3)):
        out[...] = scr[turn ^ k].astype(LOW)


def feed_product(which, hidden, grad, normed, upward, left, right, put):
    @pl.when(which == 0)
    def _():
        left[...] = hidden[...]
        right[...] = grad[...]

    @pl.when(which != 0)
    def _():
        left[...] = normed[...]
        right[...] = upward[...]

    step = 256
    for at in range(0, left.shape[1], step):
        put(slice(at, at + step), mm_tn(left[:, at : at + step], right[...]))


def first_step(base, total, kept, along1, along2):
    rows = along1[0] // 2
    block = lambda half, k: total(pl.ds(pl.multiple_of((4 * half + (base ^ k)) * rows, rows), rows))
    for n, (half, k) in enumerate(((0, 0), (0, 2), (1, 0), (1, 1))):
        kept[n * rows : (n + 1) * rows, :] = block(half, k)
    for (_, out), picks in ((along1, ((0, 1), (0, 3))), (along2, ((1, 2), (1, 3)))):
        for n, (half, k) in enumerate(picks):
            out[n * rows : (n + 1) * rows, :] = block(half, k).astype(LOW)


def second_step(kept, came1, came2, own, along1, along2):
    rows = along1.shape[0]
    part = lambda n: kept[n * rows : (n + 1) * rows, :]
    came = lambda ref, n: ref[n * rows : (n + 1) * rows, :].astype(F32)
    own[:rows, :] = part(0) + came(came1, 0)
    own[rows:, :] = part(2) + came(came2, 0)
    along2[...] = (part(1) + came(came1, 1)).astype(LOW)
    along1[...] = (part(3) + came(came2, 1)).astype(LOW)


def last_sums(own, came1, came2):
    rows = came1.shape[0]
    upper = own[:rows, :] + came2[...].astype(F32)
    lower = own[rows:, :] + came1[...].astype(F32)
    return upper.astype(LOW), lower.astype(LOW)


def join_half(base, mine1, mine2, came1, came2, out):
    rows = out.shape[0] // 8
    order = ((mine1, 0, (0, 2)), (came1, 0, (1, 3)), (mine2, 1, (0, 1)), (came2, 1, (2, 3)))
    for ref, half, ks in order:
        for n, k in enumerate(ks):
            at = pl.ds(pl.multiple_of((4 * half + (base ^ k)) * rows, rows), rows)
            out[at, :] = ref[n * rows : (n + 1) * rows, :]


def feed_send_body(ids, hidden, grad, normed, upward, out, left, right):
    def put(at, value):
        out[at, :] = value.astype(LOW)

    feed_product(1 - ids[2], hidden, grad, normed, upward, left, right, put)


def feed_keep_body(ids, hidden, grad, normed, upward, arrived, kept, along1, along2, left, right, scr):
    def put(at, value):
        scr[at, :] = value + arrived[at, :].astype(F32)

    feed_product(ids[2], hidden, grad, normed, upward, left, right, put)
    rows = along1.shape[0]
    first_step(ids[0], lambda at: scr[at, :], kept, (rows, along1), (rows, along2))


def low_sum(a, b):
    return a.astype(F32) + b.astype(F32)


def step_a_body(
    ids, keep, arrived, small, rel, feed_kept, came1, came2, kept, feed_own, along1, along2, scr, small_scr
):
    size = keep.shape[0]
    few = size // 8
    scr[...] = keep[...] + arrived[:size, :].astype(F32)
    first_step(ids[0], lambda at: scr[at, :], kept, (2 * few, along1), (2 * few, along2))
    at = slice(2 * few, 2 * few + feed_own.shape[0] // 2)
    second_step(feed_kept, came1, came2, feed_own, along1.at[at, :], along2.at[at, :])
    small_scr[...] = low_sum(small[...].astype(LOW), arrived[size:, :])
    small_scr[8:9, : rel.shape[1]] = rel[:1, :]
    along1[at.stop :, :] = small_scr[...].astype(LOW)


def step_b_body(kept, feed_own, sent1, came1, came2, own, along1, along2):
    few = own.shape[0] // 2
    rows = feed_own.shape[0] // 2
    first, at, last = slice(0, 2 * few), slice(2 * few, 2 * few + rows), slice(2 * few + rows, None)
    head = slice(0, few)
    second_step(kept, came1.at[first, :], came2.at[first, :], own, along1.at[head, :], along2.at[head, :])
    upper, lower = last_sums(feed_own, came1.at[at, :], came2.at[at, :])
    for out, parts in ((along1, (lower, upper)), (along2, (upper, lower))):
        for n, part in enumerate(parts):
            out[few + n * rows : few + (n + 1) * rows, :] = part
    along2[few + 2 * rows :, :] = low_sum(sent1[last, :], came1[last, :]).astype(LOW)


def step_c_body(own, sent2, came1, came2, along1, along2, small_out):
    few = along1.shape[0]
    head = slice(0, few)
    last = slice(came1.shape[0], None)
    along2[...], along1[...] = last_sums(own, came1.at[head, :], came2.at[head, :])
    small_out[...] = low_sum(sent2[last, :], came2[last, :]).astype(LOW)


def step_d_body(mid1, mid2, came1, came2, near1, near2, along1, along2):
    few = mid1.shape[0]
    done = along1.shape[0] - 2 * few
    for out, own, came, near in ((along1, mid2, came2, near2), (along2, mid1, came1, near1)):
        out[:few, :] = own[...]
        out[few : 2 * few, :] = came[...]
        out[2 * few :, :] = near[few : few + done, :]


def joins_body(ids, along1, along2, came1, came2, sent1, sent2, near1, near2, small, seen, attend_out, out):
    size = attend_out.shape[0] - small.shape[0]
    join_half(ids[0], along1, along2, came1, came2, attend_out.at[:size, :])
    attend_out[size:, :] = small[...]
    rows = out.shape[0] // 8
    few = sent1.shape[0] - 2 * rows
    skip = came1.shape[0] - rows
    first, second, last = slice(few, few + rows), slice(few + rows, few + 2 * rows), slice(skip, skip + rows)
    upper = ((sent2, first), (near1, second), (near2, first), (came1, last))
    lower = ((sent1, first), (near1, first), (near2, second), (came2, last))
    for half, blocks in enumerate((upper, lower)):
        for k, (ref, at) in enumerate(blocks):
            to = pl.multiple_of((4 * half + (ids[0] ^ k)) * rows, rows)
            out[pl.ds(to, rows), :] = ref[at, :]


def norm_back_body(ids, *refs):
    pieces, (unit, inv, gain, grad_out, low_out, small_out) = refs[:4], refs[4:]
    turn = ids[0] ^ ids[1]
    for k, piece in enumerate(pieces):
        grad_out[turn ^ k] = piece[...].astype(F32)
    grad_normed = grad_out[...].reshape(unit.shape)
    grad = norm_back(grad_normed, unit[...], inv[:, :1], gain[...])
    grad_out[...] = grad.reshape(grad_out.shape)
    low_out[...] = grad.astype(LOW)
    total = lambda a: jnp.sum(a, axis=0, keepdims=True)
    small_out[...] = small_rows(total(grad_normed * unit[...]), total(grad_normed), total(grad))


def row_sums(rows):
    high = rows.astype(LOW)
    rest = (rows - high.astype(F32)).astype(LOW)
    ones = jnp.ones((8, rows.shape[1]), LOW)
    return mm_nt(ones, high) + mm_nt(ones, rest)


def attend_back_body(heads, query_scale, ids, *refs):
    grad, grad_low, wq, wk, wv, wo, probs_ref, qt, kt, vt = refs[:10]
    o = refs[10:14]
    scores_out, stack, sums_out, weights, dct, grad_q, result = refs[14:]
    part = wq.shape[0]
    head = part // heads
    slots, full = qt.shape[1], kt.shape[1]
    half, block_len = slots // 4, full // 4
    quarter = block_len // 4
    weights[:part, :] = wk[...]
    weights[part : 2 * part, :] = wv[...]
    weights[2 * part :, :] = wq[...]
    dct[...] = mm_nt(wo[...], grad_low[...]).astype(LOW)
    for h in range(heads):
        at = slice(h * head, (h + 1) * head)
        probs = probs_ref[h]
        grad_probs = mm_tn(vt[at, :], dct[at, :])
        grad_values = mm_nt(dct[at, :], probs.astype(LOW))
        scores = probs * (grad_probs - jnp.sum(probs * grad_probs, axis=0, keepdims=True))
        scores_out[h] = scores
        scores_low = scores.astype(LOW)
        grad_queries = mm(kt[at, :], scores_low) * query_scale
        stack[at, :] = mm_nt(qt[at, :], scores_low).astype(LOW)
        stack[part + h * head : part + (h + 1) * head, :] = grad_values.astype(LOW)
        grad_q[at, :] = grad_queries.astype(LOW)
        sums_out[h, :8, :] = row_sums(grad_queries)
        sums_out[h, 8:, :] = row_sums(grad_values)
    stack[2 * part :, :] = mm(grad_q[...], pair_matrix(slots, full, False)).astype(LOW)
    result[...] = mm_tn(stack[...], weights[...])
    spread = pair_matrix(quarter, quarter // 2, True)
    for b in range(4):
        to = slice(b * quarter, (b + 1) * quarter)
        rows = lambda k: pl.ds(pl.multiple_of(b * block_len + (ids[1] ^ k) * quarter, quarter), quarter)
        residual = grad[b, pl.ds(pl.multiple_of(ids[1] * (quarter // 2), quarter // 2), quarter // 2), :]
        high = residual.astype(LOW)
        rest = (residual - high.astype(F32)).astype(LOW)
        o[0][to, :] = result[rows(0), :] + (mm(spread, high) + mm(spread, rest))
        for k in range(1, 4):
            o[k][to, :] = result[rows(k), :].astype(LOW)


def attend_weights_body(ids, x, grad, stack, ct, small_feed, small_attend, sums, keep, send, small_out):
    part = ct.shape[0]
    heads = sums.shape[0]
    product = mm(stack[...], x[...])
    outer = mm(ct[...], grad[...])
    rows = (product[2 * part :], product[:part], product[part : 2 * part], outer)
    for half in (0, 1):
        for c, out in ((half, keep), (1 - half, send)):

            @pl.when(ids[2] == c)
            def _(half=half, out=out):
                for n in (0, 1):
                    out[n * part : (n + 1) * part, :] = rows[2 * half + n].astype(out.dtype)

    small_out[...] = jnp.zeros_like(small_out)
    small_out[:4, :] = small_feed[:4, :]
    small_out[4:7, :] = small_attend[:3, :]
    line = [sums[h, at : at + 1, :] for at in (0, 8) for h in range(heads)]
    small_out[7:8, : 2 * part] = jnp.concatenate(line, axis=1)
    send[2 * part :, :] = small_out[...].astype(LOW)


def total_body(r1, r2, r3, own, out):
    out[...] = total_of(own, (r1, r2, r3)).astype(LOW)


def sender(sem):
    copies = []

    def send(source, target):
        copy = pltpu.make_async_copy(source, target, sem.at[len(copies)])
        copy.start()
        copies.append(copy)

    def wait():
        for copy in copies:
            copy.wait()

    return send, wait


def widen(which, rows, first, second, scr, sem):
    step = rows.shape[0] // 4
    for n in range(4):
        span = pl.ds(n * step, step)
        scr[span, :] = rows[span, :].astype(F32)
        for c, out in ((0, first), (1, second)):

            @pl.when(which == c)
            def _(out=out, n=n, span=span):
                copy = pltpu.make_async_copy(scr.at[span, :], out.at[span, :], sem.at[n])
                copy.start()


def widen_wait(which, first, second, scr, sem):
    step = scr.shape[0] // 4
    for n in range(4):
        span = pl.ds(n * step, step)
        for c, out in ((0, first), (1, second)):

            @pl.when(which == c)
            def _(out=out, n=n, span=span):
                pltpu.make_async_copy(scr.at[span, :], out.at[span, :], sem.at[n]).wait()


def output_body(ids, n0, q1, q2, q3, output):
    rows = n0.shape[0]
    output[ids[0]] = n0[...]
    for b, q in ((1, q1), (2, q2), (3, q3)):
        output[ids[0] ^ b] = q[q.shape[0] - rows :, :]


def unpack_body(ids, mine, other, feed_other, _first, _second, first, second, *rest):
    *rows_out, query_out, value_out, rel_out, dq, dk, dv, do, scr, wide, sem, wide_sem = rest
    widen(1 - ids[2], feed_other, first, second, wide, wide_sem)
    unpack_attend(ids, mine, other, rows_out, query_out, value_out, rel_out, (dq, dk, dv, do), scr, sem)
    widen_wait(1 - ids[2], first, second, wide, wide_sem)


def unpack_attend(ids, mine, other, rows_out, query_out, value_out, rel_out, larges, scr, sem):
    part = larges[0].shape[0]
    heads = rel_out.shape[0]
    send, wait = sender(sem)
    for c, (a, b) in ((0, (mine, other)), (1, (other, mine))):

        @pl.when(ids[2] == c)
        def _(a=a, b=b):
            for n, half in enumerate((a, a, b, b)):
                scr[n] = half[n % 2 * part : (n % 2 + 1) * part, :].astype(F32)

    for n, out in enumerate(larges):
        send(scr.at[n], out)
    last = slice(2 * part, None)
    small = mine[last, :].astype(F32)
    for row, out in enumerate(rows_out):
        out[...] = small[row, :]
    query_out[...] = small[7, :part]
    value_out[...] = small[7, part : 2 * part]
    line = small[8:9, :128] + other[last, :128].astype(F32)[8:9, :]
    for h in range(heads):
        rel_out[h : h + 1, :] = line[:, h * BASES : (h + 1) * BASES]
    wait()


def quarters_body(met, r1, r2, r3, own, n1, n2, n3, q0, q1, q2, q3):
    total = total_of(own, (r1, r2, r3)).astype(LOW)
    rows = q0.shape[0]
    q0[...] = total[:rows]
    for b, (q, n) in enumerate(((q1, n1), (q2, n2), (q3, n3)), 1):
        q[:rows, :] = total[b * rows : (b + 1) * rows]
        q[rows:, :] = n[...]


def join_body(q0, q1, q2, q3, joined):
    rows = q0.shape[0]
    for b, q in enumerate((q0, q1, q2, q3)):
        joined[b * rows : (b + 1) * rows, :] = q[:rows, :]


def touch_body(t1, t2, t3, out):
    rows = out.shape[0]
    out[...] = t1[:rows, :] + t2[:rows, :] + t3[:rows, :]


def place_body(ids, t0, t1, t2, t3, mine, out, first, second, scr, wide, sem, wide_sem):
    send, wait = sender(sem)
    rows = scr.shape[1] // 4
    for b in range(4):
        for k, t in enumerate((t0, t1, t2, t3)):
            at = pl.ds(pl.multiple_of((ids[1] ^ k) * rows, rows), rows)
            scr[b, at, :] = t[b * rows : (b + 1) * rows, :].astype(out.dtype)
        send(scr.at[b], out.at[ids[0] ^ b])
    widen(ids[2], mine, first, second, wide, wide_sem)
    wait()
    widen_wait(ids[2], first, second, wide, wide_sem)


def dp_sum(values, dp_size):
    step = 2
    while step < dp_size:
        values = [
            (v.astype(F32) + swap(v, "dp", dp_size, step).astype(F32)).astype(v.dtype) for v in values
        ]
        step *= 2
    return values


def both_ways(along1, along2, size):
    return swap(along1, "seq", size, 1), swap(along2, "seq", size, 2)


def shards(
    inputs,
    lengths,
    query_weight,
    query_bias,
    key_weight,
    value_weight,
    value_bias,
    rel_weight,
    out_weight,
    out_bias,
    attn_gain,
    attn_shift,
    up_weight,
    up_bias,
    down_weight,
    down_bias,
    ffn_gain,
    ffn_shift,
    cotangent,
):
    seq_size, dp_size, mp_size = (lax.axis_size(a) for a in ("seq", "dp", "mp"))
    j, m, c = lax.axis_index("seq"), lax.axis_index("mp"), lax.axis_index("dp") % 2
    sentences, block_len, width = inputs.shape
    assert sentences == seq_size == mp_size == 4 and dp_size % 2 == 0
    half = block_len // 2
    full, slots = 4 * block_len, 4 * half
    heads = rel_weight.shape[0]
    part = query_weight.shape[1]
    head = part // heads
    hidden_here = up_weight.shape[1]
    assert hidden_here == width
    query_scale = head ** (-0.5)
    row = lambda v: v.reshape(1, -1)
    column = lambda v: v.reshape(-1, 1)
    ids = jnp.stack([j, m, c, pick(lengths, j)]).astype(jnp.int32)
    wq, wk, wv = query_weight.T, key_weight.T, value_weight.T

    x = [pick(inputs, j)] + [swap(pick(inputs, j ^ k), "seq", seq_size, k) for k in range(1, 4)]
    bias = kernel(
        functools.partial(bias_body, heads, block_len, 32), f32(heads, full, slots), (ids, rel_weight), smem=2, micros=3.0
    )
    own, p1, p2, p3, probs, qt, kt, vt, ct, tokens = kernel(
        functools.partial(attend_body, heads, query_scale),
        [f32(half, width)]
        + [low(half, width)] * 3
        + [f32(heads, full, slots), low(part, slots), low(part, full), low(part, full), low(part, slots)]
        + [low(full, width)],
        (ids, *x, wq, wk, wv, out_weight, column(query_bias), column(value_bias), row(out_bias), bias),
        smem=1,
        scratch=[
            pltpu.VMEM((4, half, width), F32),
            pltpu.VMEM((heads, full, slots), F32),
            pltpu.VMEM((part, slots), LOW),
            pltpu.VMEM((part, full), LOW),
            pltpu.VMEM((part, full), LOW),
            pltpu.VMEM((part, slots), LOW),
            pltpu.VMEM((full, width), LOW),
            pltpu.VMEM((3 * part, width), LOW),
            pltpu.SemaphoreType.DMA((5 + heads,)),
        ],
        micros=5.0,
        hbm=range(4, 10),
    )
    arrived = scatter_low((p1, p2, p3), "mp", mp_size)
    attended = kernel(total_body, low(half, width), (*arrived, own), micros=0.5)
    later = after(cotangent, attended)
    cots = [pick(later, j)] + [swap(pick(later, j ^ k), "seq", seq_size, k) for k in range(1, 4)]
    own, p1, p2, p3, hidden, slope, normed, unit, inv = kernel(
        feed_body,
        [f32(half, width)]
        + [low(half, width)] * 3
        + [low(slots, hidden_here), f32(slots, hidden_here), low(slots, width), f32(slots, width), f32(slots, 128)],
        (ids, attended, *gather_low(attended, "mp", mp_size), row(attn_gain), row(attn_shift), up_weight)
        + (row(up_bias), down_weight, row(down_bias)),
        smem=1,
        scratch=[pltpu.VMEM((4, half, width), F32)],
        micros=3.0,
    )
    p1, p2, p3 = after((p1, p2, p3), cots)
    mixed = kernel(total_body, low(half, width), (*scatter_low((p1, p2, p3), "mp", mp_size), own), micros=0.5)
    own, p1, p2, p3, *rest = kernel(
        feed_back_body,
        [f32(half, width)]
        + [low(half, width)] * 7
        + [low(slots, width), low(slots, hidden_here), f32(SMALL_ROWS, width)],
        (ids, mixed, *gather_low(mixed, "mp", mp_size), *cots, row(ffn_gain), row(ffn_shift), slope)
        + (down_weight, up_weight),
        smem=1,
        scratch=[pltpu.VMEM((4, half, width), F32), pltpu.VMEM((slots, width), LOW)],
        micros=3.0,
    )
    outputs, (grad_mixed, upward, small_feed) = rest[:4], rest[4:]
    operands = (hidden, grad_mixed, normed, upward)
    sides = [pltpu.VMEM((slots, width), LOW)] * 2
    feed_send = kernel(
        feed_send_body, low(width, width), (ids, *operands), smem=1, scratch=sides, micros=0.1
    )
    feed_arrived = swap(feed_send, "dp", dp_size, 1)
    arrived = scatter_low((p1, p2, p3), "mp", mp_size)
    grad_normed = kernel(total_body, low(half, width), (*arrived, own), micros=40.0)
    rows = width // 8
    feed_kept, along1, along2 = kernel(
        feed_keep_body,
        [f32(4 * rows, width)] + [low(2 * rows, width)] * 2,
        (ids, *operands, after(feed_arrived, grad_normed)),
        smem=1,
        scratch=sides + [pltpu.VMEM((width, width), F32)],
        micros=0.1,
    )
    s = gather_low(grad_normed, "mp", mp_size)
    came = both_ways(along1, along2, seq_size)
    grad, grad_attended, small_attend = kernel(
        norm_back_body,
        [f32(4, half, width), low(slots, width), f32(SMALL_ROWS, width)],
        (ids, grad_normed, *s, unit, inv, row(attn_gain)),
        smem=1,
        micros=6.5,
    )
    own_input, o1, o2, o3, scores, stack, sums = kernel(
        functools.partial(attend_back_body, heads, query_scale),
        [f32(block_len, width)]
        + [low(block_len, width)] * 3
        + [f32(heads, full, slots), low(3 * part, full), f32(heads, 16, head)],
        (ids, grad, grad_attended, wq, wk, wv, out_weight, probs, qt, kt, vt),
        smem=1,
        scratch=[
            pltpu.VMEM((3 * part, width), LOW),
            pltpu.VMEM((part, slots), LOW),
            pltpu.VMEM((part, slots), LOW),
            pltpu.VMEM((full, width), F32),
        ],
        micros=0.1,
    )
    rel = kernel(
        functools.partial(rel_body, heads, block_len, 32),
        f32(8, 128),
        (ids, scores),
        smem=1,
        scratch=[pltpu.VMEM((heads * BASES, 8, slots), F32)],
        micros=0.1,
    )
    half_rows = 2 * part
    attend_keep, attend_send, small = kernel(
        attend_weights_body,
        [f32(half_rows, width), low(half_rows + SMALL_ROWS, width), f32(SMALL_ROWS, width)],
        (ids, after(tokens, came), grad_attended, stack, ct, small_feed, small_attend, sums),
        smem=1,
        micros=0.1,
    )
    landed = ordered((o1, o2, o3), "mp", mp_size, [1, 2, 3])
    attend_arrived = swap(attend_send, "dp", dp_size, 1)
    few = half_rows // 8
    attend_kept, feed_own, along1, along2 = kernel(
        step_a_body,
        [f32(4 * few, width), f32(2 * rows, width)]
        + [low(2 * few + rows + SMALL_ROWS, width), low(2 * few + rows, width)],
        (ids, attend_keep, attend_arrived, small, rel, feed_kept, *came),
        smem=1,
        scratch=[pltpu.VMEM((half_rows, width), F32), pltpu.VMEM((SMALL_ROWS, width), F32)],
        micros=0.1,
    )
    met = kernel(touch_body, low(SMALL_ROWS, width), tuple(landed), micros=4.2)
    quarter = block_len // 4
    q0, *q = kernel(
        quarters_body,
        [low(quarter, width)] + [low(quarter + half, width)] * 3,
        (met, *landed, own_input, *outputs[1:]),
        micros=0.5,
    )
    attend_own, sent1, sent2 = kernel(
        step_b_body,
        [f32(2 * few, width), low(few + 2 * rows, width), low(few + 2 * rows + SMALL_ROWS, width)],
        (attend_kept, after(feed_own, q0), along1, *both_ways(along1, along2, seq_size)),
        micros=0.1,
    )
    near = both_ways(sent1, sent2, seq_size)
    q = [swap(q[k - 1], "seq", seq_size, k) for k in [2, 1, 3]]
    q = deep(q)
    q = [q[[2, 1, 3].index(k)] for k in range(1, 4)]
    joined = kernel(join_body, low(block_len, width), (q0, *q), micros=6.8)
    spread = gather_low(joined, "mp", mp_size)
    *mid, small = kernel(
        step_c_body,
        [low(few, width)] * 2 + [low(SMALL_ROWS, width)],
        (after(attend_own, joined), sent2, *near),
        micros=0.1,
    )
    output_all = kernel(output_body, low(4, half, width), (ids, outputs[0], *q), smem=1, micros=0.1)
    along1, along2 = kernel(
        step_d_body,
        [low(2 * few + rows, width)] * 2,
        (after(mid[0], output_all), mid[1], *both_ways(*mid, seq_size), *near),
        micros=0.1,
    )
    came = both_ways(along1, along2, seq_size)
    seen = kernel(touch_body, low(SMALL_ROWS, width), tuple(spread), micros=7.0)
    attend_mine, feed_mine = kernel(
        joins_body,
        [low(half_rows + SMALL_ROWS, width), low(width, width)],
        (ids, along1, along2, *came, sent1, sent2, *near, small, seen),
        smem=1,
        micros=0.2,
    )
    attend_mine, feed_mine = dp_sum((attend_mine, feed_mine), dp_size)
    attend_other = swap(attend_mine, "dp", dp_size, 1)
    feed_other = swap(feed_mine, "dp", dp_size, 1)
    wide = pltpu.VMEM((width, width), F32)
    sems = pltpu.SemaphoreType.DMA((4,))
    input_all, *halves = kernel(
        place_body,
        [f32(4, block_len, width)] + [f32(width, width)] * 2,
        (ids, joined, *spread, feed_mine),
        smem=1,
        scratch=[pltpu.VMEM((4, block_len, width), F32), wide, sems, sems],
        micros=0.1,
        hbm=range(3),
    )
    down_grad, up_grad, *rest = kernel(
        unpack_body,
        [f32(width, width)] * 2
        + [f32(width)] * 7
        + [f32(part)] * 2
        + [f32(heads, BASES)]
        + [f32(part, width)] * 4,
        (ids, attend_mine, attend_other, feed_other, *halves),
        smem=1,
        scratch=[pltpu.VMEM((4, part, width), F32), wide, sems, sems],
        micros=0.1,
        hbm=(0, 1, 12, 13, 14, 15),
        reused=2,
    )
    *small, query_sum, value_sum, rel_sum, dq, dk, dv, do = rest
    ffn_gain_sum, ffn_shift_sum, down_bias_sum, up_bias_sum, attn_gain_sum, attn_shift_sum, out_bias_sum = small
    return (
        output_all,
        input_all,
        dq.T,
        query_sum,
        dk.T,
        dv.T,
        value_sum,
        rel_sum,
        do,
        out_bias_sum,
        attn_gain_sum,
        attn_shift_sum,
        up_grad,
        up_bias_sum,
        down_grad,
        down_bias_sum,
        ffn_gain_sum,
        ffn_shift_sum,
    )


def solution(mesh):
    return jax.shard_map(
        shards,
        mesh=mesh,
        in_specs=(
            P("dp", "seq", None),
            P("dp"),
            P(None, "mp"),
            P("mp"),
            P(None, "mp"),
            P(None, "mp"),
            P("mp"),
            P("mp", None),
            P("mp", None),
            P(),
            P(),
            P(),
            P(None, "mp"),
            P("mp"),
            P("mp", None),
            P(),
            P(),
            P(),
            P("dp", "seq", None),
        ),
        out_specs=(
            P("dp", "seq", None),
            P("dp", "seq", None),
            P(None, "mp"),
            P("mp"),
            P(None, "mp"),
            P(None, "mp"),
            P("mp"),
            P("mp", None),
            P("mp", None),
            P(),
            P(),
            P(),
            P(None, "mp"),
            P("mp"),
            P("mp", None),
            P(),
            P(),
            P(),
        ),
        check_vma=False,
    )
```

```python
import functools

import jax
import jax.numpy as jnp
from jax import lax
from jax.experimental import pallas as pl
from jax.experimental.pallas import tpu as pltpu
from jax.sharding import PartitionSpec as P

BASES = 8
EPSILON = 1e-05
MASKED_SCORE = -1e30
F32 = jnp.float32
LOW = jnp.bfloat16
SMALL_ROWS = 16
MIB = 1024 * 1024
DEPTH = 2


def f32(*shape):
    return jax.ShapeDtypeStruct(shape, F32)


def low(*shape):
    return jax.ShapeDtypeStruct(shape, LOW)


def kernel(body, outs, args, smem=0, scratch=(), micros=1.0, limit=16, hbm=(), reused=0):
    in_specs = [pl.BlockSpec(memory_space=pltpu.SMEM)] * smem
    in_specs += [pl.BlockSpec(memory_space=pltpu.VMEM)] * (len(args) - smem - reused)
    in_specs += [pl.BlockSpec(memory_space=pltpu.HBM)] * reused
    whole = pl.BlockSpec(memory_space=pltpu.VMEM)
    if isinstance(outs, list):
        out_specs = [pl.BlockSpec(memory_space=pltpu.HBM) if n in hbm else whole for n in range(len(outs))]
    else:
        out_specs = whole
    return pl.pallas_call(
        body,
        out_shape=outs,
        in_specs=in_specs,
        out_specs=out_specs,
        scratch_shapes=list(scratch),
        input_output_aliases={len(args) - reused + n: n for n in range(reused)},
        compiler_params=pltpu.CompilerParams(vmem_limit_bytes=limit * MIB),
        cost_estimate=pl.CostEstimate(
            flops=int(micros * 4e8), bytes_accessed=int(micros * 3e6), transcendentals=0
        ),
    )(*args)


def after(value, *events):
    return lax.optimization_barrier((value, events))[0]


def dot_of(dims, a, b):
    return lax.dot_general(a, b, (dims, ((), ())), preferred_element_type=F32)


mm = functools.partial(dot_of, ((1,), (0,)))
mm_nt = functools.partial(dot_of, ((1,), (1,)))
mm_tn = functools.partial(dot_of, ((0,), (0,)))


def swap(block, axis, size, k):
    return lax.ppermute(block, axis, [(s, s ^ k) for s in range(size)])


def deep(values):
    for _ in range(DEPTH):
        values = lax.optimization_barrier(values)
    return values


def ordered(blocks, axis, size, order):
    landed = [swap(blocks[k - 1], axis, size, k) for k in order]
    landed = deep(landed) if axis == "mp" else landed
    return [landed[order.index(k)] for k in range(1, size)]


def gather_low(block, axis, size, order=(1, 3, 2)):
    return ordered([block] * (size - 1), axis, size, order)


def scatter_low(blocks, axis, size):
    return ordered(blocks, axis, size, [2, 1, 3])


def pick(stacked, index):
    return lax.dynamic_index_in_dim(stacked, index, 0, keepdims=False)


def norm_stats(rows):
    center = rows - jnp.mean(rows, axis=-1, keepdims=True)
    scale_inv = lax.rsqrt(jnp.mean(center * center, axis=-1, keepdims=True) + EPSILON)
    return center * scale_inv, scale_inv


def norm_back(grad_out, normed, scale_inv, gain):
    grad_normed = grad_out * gain
    centered = grad_normed - jnp.mean(grad_normed, axis=-1, keepdims=True)
    return scale_inv * (centered - normed * jnp.mean(grad_normed * normed, axis=-1, keepdims=True))


def total_of(own_ref, arrived_refs):
    total = own_ref[...]
    for ref in arrived_refs:
        total = total + ref[...].astype(F32)
    return total


def pair_matrix(rows, cols, tall):
    r = lax.broadcasted_iota(jnp.int32, (rows, cols), 0)
    c = lax.broadcasted_iota(jnp.int32, (rows, cols), 1)
    hit = (r >> 1) == c if tall else r == (c >> 1)
    return jnp.where(hit, 0.5, 0.0).astype(LOW)


def distances(ids, chunk, rows, block_len, slots):
    j = ids[0]
    start = chunk * rows
    token = (j ^ (start // block_len)) * block_len + start % block_len
    token = token + lax.broadcasted_iota(jnp.int32, (rows, slots), 0)
    s = lax.broadcasted_iota(jnp.int32, (rows, slots), 1)
    half = block_len // 2
    slot = (j ^ (s // half)) * half + s % half
    return token, (token - 2 * slot).astype(F32)


def basis_of(distance, index, span):
    degree = index % (BASES // 2)
    inverse = 64.0 / (span * 4.0**degree)
    if index < BASES // 2:
        return jnp.exp(jnp.abs(distance) * (-inverse))
    return jnp.tanh(distance * inverse)


def bias_body(heads, block_len, rows, ids, rel, out):
    full, slots = out.shape[1:]

    def step(chunk, carry):
        token, distance = distances(ids, chunk, rows, block_len, slots)
        sums = [jnp.zeros((rows, slots), F32)] * heads
        for index in range(BASES):
            base = basis_of(distance, index, full)
            sums = [sums[h] + rel[h, index] * base for h in range(heads)]
        valid = token < ids[3]
        for h in range(heads):
            out[h, pl.ds(pl.multiple_of(chunk * rows, rows), rows), :] = jnp.where(valid, sums[h], MASKED_SCORE)
        return carry

    lax.fori_loop(0, full // rows, step, 0)


def rel_body(heads, block_len, rows, ids, scores_ref, out, acc):
    full, slots = scores_ref.shape[1:]
    acc[...] = jnp.zeros_like(acc)

    def step(chunk, carry):
        _, distance = distances(ids, chunk, rows, block_len, slots)
        at = pl.ds(pl.multiple_of(chunk * rows, rows), rows)
        grads = [scores_ref[h, at, :] for h in range(heads)]
        for index in range(BASES):
            base = basis_of(distance, index, full)
            for h in range(heads):
                acc[h * BASES + index] += jnp.sum((grads[h] * base).reshape(rows // 8, 8, slots), axis=0)
        return carry

    lax.fori_loop(0, full // rows, step, 0)
    lane = lax.broadcasted_iota(jnp.int32, (1, out.shape[1]), 1)
    line = jnp.zeros((1, out.shape[1]), F32)
    for row in range(heads * BASES):
        col = jnp.sum(jnp.sum(acc[row], axis=0, keepdims=True), axis=1, keepdims=True)
        line = jnp.where(lane == row, col, line)
    out[...] = jnp.broadcast_to(line, out.shape)


def attend_body(heads, query_scale, ids, *refs):
    x = refs[:4]
    wq, wk, wv, wo, qb, vb, ob, bias, own_out, p1, p2, p3 = refs[4:16]
    probs_hbm, qt_hbm, kt_hbm, vt_hbm, ct_hbm, x_hbm = refs[16:22]
    scr, probs_ref, qt, kt, vt, ct, tokens, weights, sem = refs[22:]
    block_len = x[0].shape[0]
    half = block_len // 2
    part = wq.shape[0]
    head = part // heads
    copies = []

    def send(source, target):
        copy = pltpu.make_async_copy(source, target, sem.at[len(copies)])
        copy.start()
        copies.append(copy)

    for b in range(4):
        tokens[b * block_len : (b + 1) * block_len, :] = x[b][...]
    send(tokens, x_hbm)
    for n, w in enumerate((wk, wv, wq)):
        weights[n * part : (n + 1) * part, :] = w[...]
    product = mm_nt(weights[...], tokens[...])
    kt[...] = product[:part, :].astype(LOW)
    vt[...] = (product[part : 2 * part, :] + vb[...]).astype(LOW)
    pairs = pair_matrix(4 * block_len, 4 * half, True)
    projected = product[2 * part :, :]
    high = projected.astype(LOW)
    pooled = mm(high, pairs) + mm((projected - high.astype(F32)).astype(LOW), pairs)
    qt[...] = ((pooled + qb[...]) * query_scale).astype(LOW)
    send(kt, kt_hbm)
    send(vt, vt_hbm)
    send(qt, qt_hbm)
    for h in range(heads):
        at = slice(h * head, (h + 1) * head)
        scores = mm_tn(kt[at, :], qt[at, :]) + bias[h]
        grown = jnp.exp(scores - jnp.max(scores, axis=0, keepdims=True))
        probs = grown * (1.0 / jnp.sum(grown, axis=0, keepdims=True))
        probs_ref[h] = probs
        send(probs_ref.at[h], probs_hbm.at[h])
        ct[at, :] = mm(vt[at, :], probs.astype(LOW)).astype(LOW)
    send(ct, ct_hbm)
    turn = ids[0] ^ ids[1]
    mine = tokens[pl.ds(pl.multiple_of(turn * block_len, block_len), block_len), :]
    own_pooled = mm(pair_matrix(half, block_len, False), mine)
    result = mm_tn(ct[...], wo[...])
    scr[...] = result.reshape(scr.shape)
    own_out[...] = own_pooled + ob[...] + scr[turn]
    for k, out in ((1, p1), (2, p2), (3, p3)):
        out[...] = scr[turn ^ k].astype(LOW)
    for copy in copies:
        copy.wait()


def feed_body(ids, a0, a1, a2, a3, gain, shift, wu, ub, wd, db, own, p1, p2, p3, *refs):
    hidden_out, slope_out, normed_out, unit_out, inv_out, scr = refs
    rows, width = a0.shape
    turn = ids[0] ^ ids[1]
    for k, a in enumerate((a0, a1, a2, a3)):
        scr[turn ^ k] = a[...].astype(F32)
    unit, inv = norm_stats(scr[...].reshape(4 * rows, width))
    normed = unit * gain[...] + shift[...]
    unit_out[...] = unit
    inv_out[...] = jnp.broadcast_to(inv, inv_out.shape)
    normed_low = normed.astype(LOW)
    normed_out[...] = normed_low
    scr[...] = normed.reshape(scr.shape)
    own[...] = scr[turn] + db[...]
    up = mm(normed_low, wu[...]) + ub[...]
    phi = 0.5 * (1.0 + lax.erf(up * (0.5**0.5)))
    density = jnp.exp(up * up * -0.5) * 0.3989422804014327
    hidden = (up * phi).astype(LOW)
    hidden_out[...] = hidden
    slope_out[...] = phi + up * density
    scr[...] = mm(hidden, wd[...]).reshape(scr.shape)
    own[...] += scr[turn]
    for k, out in ((1, p1), (2, p2), (3, p3)):
        out[...] = scr[turn ^ k].astype(LOW)


def small_rows(*sums):
    return jnp.concatenate(list(sums) + [jnp.zeros((SMALL_ROWS - len(sums), sums[0].shape[1]), F32)])


def feed_back_body(ids, *refs):
    pieces, cots = refs[:4], refs[4:8]
    gain, shift, slope, wd, wu, own, p1, p2, p3 = refs[8:17]
    outs = refs[17:21]
    grad_out, upward_out, small_out, scr, low_scr = refs[21:]
    rows, width = own.shape
    slots = 4 * rows
    turn = ids[0] ^ ids[1]
    for k, piece in enumerate(pieces):
        scr[turn ^ k] = piece[...].astype(F32)
    unit, inv = norm_stats(scr[...].reshape(slots, width))
    s = lax.broadcasted_iota(jnp.int32, (slots, 1), 0)
    slot = (ids[0] ^ (s // rows)) * rows + s % rows
    valid = jnp.where(2 * slot < ids[3], 1.0, 0.0)
    output = ((unit * gain[...] + shift[...]) * valid).astype(LOW)
    for b in range(4):
        outs[b][...] = output[b * rows : (b + 1) * rows, :]
        low_scr[b * rows : (b + 1) * rows, :] = cots[b][...]
    top = low_scr[...].astype(F32) * valid
    grad = norm_back(top, unit, inv, gain[...])
    grad_low = grad.astype(LOW)
    grad_out[...] = grad_low
    scr[...] = grad.reshape(scr.shape)
    own[...] = scr[turn]
    hidden = mm_nt(grad_low, wd[...]).astype(LOW).astype(F32)
    upward = hidden * slope[...]
    upward_low = upward.astype(LOW)
    upward_out[...] = upward_low
    total = lambda a: jnp.sum(a, axis=0, keepdims=True)
    small_out[...] = small_rows(total(top * unit), total(top), total(grad), total(upward))
    scr[...] = mm_nt(upward_low, wu[...]).reshape(scr.shape)
    own[...] += scr[turn]
    for k, out in ((1, p1), (2, p2), (3, p3)):
        out[...] = scr[turn ^ k].astype(LOW)


def feed_product(which, hidden, grad, normed, upward, left, right, put):
    @pl.when(which == 0)
    def _():
        left[...] = hidden[...]
        right[...] = grad[...]

    @pl.when(which != 0)
    def _():
        left[...] = normed[...]
        right[...] = upward[...]

    step = 256
    for at in range(0, left.shape[1], step):
        put(slice(at, at + step), mm_tn(left[:, at : at + step], right[...]))


def first_step(base, total, kept, along1, along2):
    rows = along1[0] // 2
    block = lambda half, k: total(pl.ds(pl.multiple_of((4 * half + (base ^ k)) * rows, rows), rows))
    for n, (half, k) in enumerate(((0, 0), (0, 2), (1, 0), (1, 1))):
        kept[n * rows : (n + 1) * rows, :] = block(half, k)
    for (_, out), picks in ((along1, ((0, 1), (0, 3))), (along2, ((1, 2), (1, 3)))):
        for n, (half, k) in enumerate(picks):
            out[n * rows : (n + 1) * rows, :] = block(half, k).astype(LOW)


def second_step(kept, came1, came2, own, along1, along2):
    rows = along1.shape[0]
    part = lambda n: kept[n * rows : (n + 1) * rows, :]
    came = lambda ref, n: ref[n * rows : (n + 1) * rows, :].astype(F32)
    own[:rows, :] = part(0) + came(came1, 0)
    own[rows:, :] = part(2) + came(came2, 0)
    along2[...] = (part(1) + came(came1, 1)).astype(LOW)
    along1[...] = (part(3) + came(came2, 1)).astype(LOW)


def last_sums(own, came1, came2):
    rows = came1.shape[0]
    upper = own[:rows, :] + came2[...].astype(F32)
    lower = own[rows:, :] + came1[...].astype(F32)
    return upper.astype(LOW), lower.astype(LOW)


def join_half(base, mine1, mine2, came1, came2, out):
    rows = out.shape[0] // 8
    order = ((mine1, 0, (0, 2)), (came1, 0, (1, 3)), (mine2, 1, (0, 1)), (came2, 1, (2, 3)))
    for ref, half, ks in order:
        for n, k in enumerate(ks):
            at = pl.ds(pl.multiple_of((4 * half + (base ^ k)) * rows, rows), rows)
            out[at, :] = ref[n * rows : (n + 1) * rows, :]


def feed_send_body(ids, hidden, grad, normed, upward, out, left, right):
    def put(at, value):
        out[at, :] = value.astype(LOW)

    feed_product(1 - ids[2], hidden, grad, normed, upward, left, right, put)


def feed_keep_body(ids, hidden, grad, normed, upward, arrived, kept, along1, along2, left, right, scr):
    def put(at, value):
        scr[at, :] = value + arrived[at, :].astype(F32)

    feed_product(ids[2], hidden, grad, normed, upward, left, right, put)
    rows = along1.shape[0]
    first_step(ids[0], lambda at: scr[at, :], kept, (rows, along1), (rows, along2))


def low_sum(a, b):
    return a.astype(F32) + b.astype(F32)


def step_a_body(
    ids, keep, arrived, small, rel, feed_kept, came1, came2, kept, feed_own, along1, along2, scr, small_scr
):
    size = keep.shape[0]
    few = size // 8
    scr[...] = keep[...] + arrived[:size, :].astype(F32)
    first_step(ids[0], lambda at: scr[at, :], kept, (2 * few, along1), (2 * few, along2))
    at = slice(2 * few, 2 * few + feed_own.shape[0] // 2)
    second_step(feed_kept, came1, came2, feed_own, along1.at[at, :], along2.at[at, :])
    small_scr[...] = low_sum(small[...].astype(LOW), arrived[size:, :])
    small_scr[8:9, : rel.shape[1]] = rel[:1, :]
    along1[at.stop :, :] = small_scr[...].astype(LOW)


def step_b_body(kept, feed_own, sent1, came1, came2, own, along1, along2):
    few = own.shape[0] // 2
    rows = feed_own.shape[0] // 2
    first, at, last = slice(0, 2 * few), slice(2 * few, 2 * few + rows), slice(2 * few + rows, None)
    head = slice(0, few)
    second_step(kept, came1.at[first, :], came2.at[first, :], own, along1.at[head, :], along2.at[head, :])
    upper, lower = last_sums(feed_own, came1.at[at, :], came2.at[at, :])
    for out, parts in ((along1, (lower, upper)), (along2, (upper, lower))):
        for n, part in enumerate(parts):
            out[few + n * rows : few + (n + 1) * rows, :] = part
    along2[few + 2 * rows :, :] = low_sum(sent1[last, :], came1[last, :]).astype(LOW)


def step_c_body(own, sent2, came1, came2, along1, along2, small_out):
    few = along1.shape[0]
    head = slice(0, few)
    last = slice(came1.shape[0], None)
    along2[...], along1[...] = last_sums(own, came1.at[head, :], came2.at[head, :])
    small_out[...] = low_sum(sent2[last, :], came2[last, :]).astype(LOW)


def step_d_body(mid1, mid2, came1, came2, near1, near2, along1, along2):
    few = mid1.shape[0]
    done = along1.shape[0] - 2 * few
    for out, own, came, near in ((along1, mid2, came2, near2), (along2, mid1, came1, near1)):
        out[:few, :] = own[...]
        out[few : 2 * few, :] = came[...]
        out[2 * few :, :] = near[few : few + done, :]


def joins_body(ids, along1, along2, came1, came2, sent1, sent2, near1, near2, small, attend_out, out):
    size = attend_out.shape[0] - small.shape[0]
    join_half(ids[0], along1, along2, came1, came2, attend_out.at[:size, :])
    attend_out[size:, :] = small[...]
    rows = out.shape[0] // 8
    few = sent1.shape[0] - 2 * rows
    skip = came1.shape[0] - rows
    first, second, last = slice(few, few + rows), slice(few + rows, few + 2 * rows), slice(skip, skip + rows)
    upper = ((sent2, first), (near1, second), (near2, first), (came1, last))
    lower = ((sent1, first), (near1, first), (near2, second), (came2, last))
    for half, blocks in enumerate((upper, lower)):
        for k, (ref, at) in enumerate(blocks):
            to = pl.multiple_of((4 * half + (ids[0] ^ k)) * rows, rows)
            out[pl.ds(to, rows), :] = ref[at, :]


def norm_back_body(ids, *refs):
    pieces, (unit, inv, gain, grad_out, low_out, small_out) = refs[:4], refs[4:]
    turn = ids[0] ^ ids[1]
    for k, piece in enumerate(pieces):
        grad_out[turn ^ k] = piece[...].astype(F32)
    grad_normed = grad_out[...].reshape(unit.shape)
    grad = norm_back(grad_normed, unit[...], inv[:, :1], gain[...])
    grad_out[...] = grad.reshape(grad_out.shape)
    low_out[...] = grad.astype(LOW)
    total = lambda a: jnp.sum(a, axis=0, keepdims=True)
    small_out[...] = small_rows(total(grad_normed * unit[...]), total(grad_normed), total(grad))


def row_sums(rows):
    high = rows.astype(LOW)
    rest = (rows - high.astype(F32)).astype(LOW)
    ones = jnp.ones((8, rows.shape[1]), LOW)
    return mm_nt(ones, high) + mm_nt(ones, rest)


def attend_back_body(heads, query_scale, ids, *refs):
    grad, grad_low, wq, wk, wv, wo, probs_ref, qt, kt, vt = refs[:10]
    o = refs[10:14]
    scores_out, stack, sums_out, weights, dct, grad_q, result = refs[14:]
    part = wq.shape[0]
    head = part // heads
    slots, full = qt.shape[1], kt.shape[1]
    half, block_len = slots // 4, full // 4
    quarter = block_len // 4
    weights[:part, :] = wk[...]
    weights[part : 2 * part, :] = wv[...]
    weights[2 * part :, :] = wq[...]
    dct[...] = mm_nt(wo[...], grad_low[...]).astype(LOW)
    for h in range(heads):
        at = slice(h * head, (h + 1) * head)
        probs = probs_ref[h]
        grad_probs = mm_tn(vt[at, :], dct[at, :])
        grad_values = mm_nt(dct[at, :], probs.astype(LOW))
        scores = probs * (grad_probs - jnp.sum(probs * grad_probs, axis=0, keepdims=True))
        scores_out[h] = scores
        scores_low = scores.astype(LOW)
        grad_queries = mm(kt[at, :], scores_low) * query_scale
        stack[at, :] = mm_nt(qt[at, :], scores_low).astype(LOW)
        stack[part + h * head : part + (h + 1) * head, :] = grad_values.astype(LOW)
        grad_q[at, :] = grad_queries.astype(LOW)
        sums_out[h, :8, :] = row_sums(grad_queries)
        sums_out[h, 8:, :] = row_sums(grad_values)
    stack[2 * part :, :] = mm(grad_q[...], pair_matrix(slots, full, False)).astype(LOW)
    result[...] = mm_tn(stack[...], weights[...])
    spread = pair_matrix(quarter, quarter // 2, True)
    for b in range(4):
        to = slice(b * quarter, (b + 1) * quarter)
        rows = lambda k: pl.ds(pl.multiple_of(b * block_len + (ids[1] ^ k) * quarter, quarter), quarter)
        residual = grad[b, pl.ds(pl.multiple_of(ids[1] * (quarter // 2), quarter // 2), quarter // 2), :]
        high = residual.astype(LOW)
        rest = (residual - high.astype(F32)).astype(LOW)
        o[0][to, :] = result[rows(0), :] + (mm(spread, high) + mm(spread, rest))
        for k in range(1, 4):
            o[k][to, :] = result[rows(k), :].astype(LOW)


def attend_weights_body(ids, x, grad, stack, ct, small_feed, small_attend, sums, keep, send, small_out):
    part = ct.shape[0]
    heads = sums.shape[0]
    product = mm(stack[...], x[...])
    outer = mm(ct[...], grad[...])
    rows = (product[2 * part :], product[:part], product[part : 2 * part], outer)
    for half in (0, 1):
        for c, out in ((half, keep), (1 - half, send)):

            @pl.when(ids[2] == c)
            def _(half=half, out=out):
                for n in (0, 1):
                    out[n * part : (n + 1) * part, :] = rows[2 * half + n].astype(out.dtype)

    small_out[...] = jnp.zeros_like(small_out)
    small_out[:4, :] = small_feed[:4, :]
    small_out[4:7, :] = small_attend[:3, :]
    line = [sums[h, at : at + 1, :] for at in (0, 8) for h in range(heads)]
    small_out[7:8, : 2 * part] = jnp.concatenate(line, axis=1)
    send[2 * part :, :] = small_out[...].astype(LOW)


def total_body(r1, r2, r3, own, out):
    out[...] = total_of(own, (r1, r2, r3)).astype(LOW)


def sender(sem):
    copies = []

    def send(source, target):
        copy = pltpu.make_async_copy(source, target, sem.at[len(copies)])
        copy.start()
        copies.append(copy)

    def wait():
        for copy in copies:
            copy.wait()

    return send, wait


def widen(flip, ids, attend, feed, results, scr, wide, sem):
    first, second, dq, dk, dv, do = results
    part = dq.shape[0]
    step = feed.shape[0] // 4
    for c, large, smalls in ((0, first, (dq, dk)), (1, second, (dv, do))):

        @pl.when((ids[2] ^ flip) == c)
        def _(large=large, smalls=smalls):
            send, wait = sender(sem)
            for n in range(4):
                span = pl.ds(n * step, step)
                wide[span, :] = feed[span, :].astype(F32)
                send(wide.at[span, :], large.at[span, :])
            for n, out in enumerate(smalls):
                scr[n] = attend[n * part : (n + 1) * part, :].astype(F32)
                send(scr.at[n], out)
            wait()


def widen_body(ids, attend, feed, *refs):
    widen(0, ids, attend, feed, refs[:6], *refs[6:])


def output_body(ids, n0, q1, q2, q3, output):
    rows = n0.shape[0]
    output[ids[0]] = n0[...]
    for b, q in ((1, q1), (2, q2), (3, q3)):
        output[ids[0] ^ b] = q[q.shape[0] - rows :, :]


def unpack_body(ids, mine, other, feed_other, *refs):
    results, (*rows_out, query_out, value_out, rel_out), scratch = refs[6:12], refs[12:22], refs[22:]
    part = results[2].shape[0]
    heads = rel_out.shape[0]
    last = slice(2 * part, None)
    small = mine[last, :].astype(F32)
    for row, out in enumerate(rows_out):
        out[...] = small[row, :]
    query_out[...] = small[7, :part]
    value_out[...] = small[7, part : 2 * part]
    line = small[8:9, :128] + other[last, :128].astype(F32)[8:9, :]
    for h in range(heads):
        rel_out[h : h + 1, :] = line[:, h * BASES : (h + 1) * BASES]
    widen(1, ids, other, feed_other, results, *scratch)


def quarters_body(met, r1, r2, r3, own, n1, n2, n3, q0, q1, q2, q3):
    total = total_of(own, (r1, r2, r3)).astype(LOW)
    rows = q0.shape[0]
    q0[...] = total[:rows]
    for b, (q, n) in enumerate(((q1, n1), (q2, n2), (q3, n3)), 1):
        q[:rows, :] = total[b * rows : (b + 1) * rows]
        q[rows:, :] = n[...]


def join_body(q0, q1, q2, q3, joined):
    rows = q0.shape[0]
    for b, q in enumerate((q0, q1, q2, q3)):
        joined[b * rows : (b + 1) * rows, :] = q[:rows, :]


def touch_body(t1, t2, t3, out):
    rows = out.shape[0]
    out[...] = t1[:rows, :] + t2[:rows, :] + t3[:rows, :]


def place_body(ids, t0, t1, t2, t3, out, scr, sem):
    send, wait = sender(sem)
    rows = scr.shape[1] // 4
    for b in range(4):
        for k, t in enumerate((t0, t1, t2, t3)):
            at = pl.ds(pl.multiple_of((ids[1] ^ k) * rows, rows), rows)
            scr[b, at, :] = t[b * rows : (b + 1) * rows, :].astype(out.dtype)
        send(scr.at[b], out.at[ids[0] ^ b])
    wait()


def dp_sum(values, dp_size):
    step = 2
    while step < dp_size:
        values = [
            (v.astype(F32) + swap(v, "dp", dp_size, step).astype(F32)).astype(v.dtype) for v in values
        ]
        step *= 2
    return values


def both_ways(along1, along2, size):
    return swap(along1, "seq", size, 1), swap(along2, "seq", size, 2)


def shards(
    inputs,
    lengths,
    query_weight,
    query_bias,
    key_weight,
    value_weight,
    value_bias,
    rel_weight,
    out_weight,
    out_bias,
    attn_gain,
    attn_shift,
    up_weight,
    up_bias,
    down_weight,
    down_bias,
    ffn_gain,
    ffn_shift,
    cotangent,
):
    seq_size, dp_size, mp_size = (lax.axis_size(a) for a in ("seq", "dp", "mp"))
    j, m, c = lax.axis_index("seq"), lax.axis_index("mp"), lax.axis_index("dp") % 2
    sentences, block_len, width = inputs.shape
    assert sentences == seq_size == mp_size == 4 and dp_size % 2 == 0
    half = block_len // 2
    full, slots = 4 * block_len, 4 * half
    heads = rel_weight.shape[0]
    part = query_weight.shape[1]
    head = part // heads
    hidden_here = up_weight.shape[1]
    assert hidden_here == width
    query_scale = head ** (-0.5)
    row = lambda v: v.reshape(1, -1)
    column = lambda v: v.reshape(-1, 1)
    ids = jnp.stack([j, m, c, pick(lengths, j)]).astype(jnp.int32)
    wq, wk, wv = query_weight.T, key_weight.T, value_weight.T

    x = [pick(inputs, j)] + [swap(pick(inputs, j ^ k), "seq", seq_size, k) for k in range(1, 4)]
    bias = kernel(
        functools.partial(bias_body, heads, block_len, 32), f32(heads, full, slots), (ids, rel_weight), smem=2, micros=3.0
    )
    own, p1, p2, p3, probs, qt, kt, vt, ct, tokens = kernel(
        functools.partial(attend_body, heads, query_scale),
        [f32(half, width)]
        + [low(half, width)] * 3
        + [f32(heads, full, slots), low(part, slots), low(part, full), low(part, full), low(part, slots)]
        + [low(full, width)],
        (ids, *x, wq, wk, wv, out_weight, column(query_bias), column(value_bias), row(out_bias), bias),
        smem=1,
        scratch=[
            pltpu.VMEM((4, half, width), F32),
            pltpu.VMEM((heads, full, slots), F32),
            pltpu.VMEM((part, slots), LOW),
            pltpu.VMEM((part, full), LOW),
            pltpu.VMEM((part, full), LOW),
            pltpu.VMEM((part, slots), LOW),
            pltpu.VMEM((full, width), LOW),
            pltpu.VMEM((3 * part, width), LOW),
            pltpu.SemaphoreType.DMA((5 + heads,)),
        ],
        micros=5.0,
        hbm=range(4, 10),
    )
    arrived = scatter_low((p1, p2, p3), "mp", mp_size)
    attended = kernel(total_body, low(half, width), (*arrived, own), micros=0.5)
    later = after(cotangent, attended)
    cots = [pick(later, j)] + [swap(pick(later, j ^ k), "seq", seq_size, k) for k in range(1, 4)]
    own, p1, p2, p3, hidden, slope, normed, unit, inv = kernel(
        feed_body,
        [f32(half, width)]
        + [low(half, width)] * 3
        + [low(slots, hidden_here), f32(slots, hidden_here), low(slots, width), f32(slots, width), f32(slots, 128)],
        (ids, attended, *gather_low(attended, "mp", mp_size), row(attn_gain), row(attn_shift), up_weight)
        + (row(up_bias), down_weight, row(down_bias)),
        smem=1,
        scratch=[pltpu.VMEM((4, half, width), F32)],
        micros=3.0,
    )
    p1, p2, p3 = after((p1, p2, p3), cots)
    mixed = kernel(total_body, low(half, width), (*scatter_low((p1, p2, p3), "mp", mp_size), own), micros=0.5)
    own, p1, p2, p3, *rest = kernel(
        feed_back_body,
        [f32(half, width)]
        + [low(half, width)] * 7
        + [low(slots, width), low(slots, hidden_here), f32(SMALL_ROWS, width)],
        (ids, mixed, *gather_low(mixed, "mp", mp_size, (3, 1, 2)), *cots, row(ffn_gain), row(ffn_shift), slope)
        + (down_weight, up_weight),
        smem=1,
        scratch=[pltpu.VMEM((4, half, width), F32), pltpu.VMEM((slots, width), LOW)],
        micros=3.0,
    )
    outputs, (grad_mixed, upward, small_feed) = rest[:4], rest[4:]
    operands = (hidden, grad_mixed, normed, upward)
    sides = [pltpu.VMEM((slots, width), LOW)] * 2
    feed_send = kernel(
        feed_send_body, low(width, width), (ids, *operands), smem=1, scratch=sides, micros=0.1
    )
    feed_arrived = swap(feed_send, "dp", dp_size, 1)
    arrived = scatter_low((p1, p2, p3), "mp", mp_size)
    grad_normed = kernel(total_body, low(half, width), (*arrived, own), micros=40.0)
    rows = width // 8
    feed_kept, along1, along2 = kernel(
        feed_keep_body,
        [f32(4 * rows, width)] + [low(2 * rows, width)] * 2,
        (ids, *operands, after(feed_arrived, grad_normed)),
        smem=1,
        scratch=sides + [pltpu.VMEM((width, width), F32)],
        micros=0.1,
    )
    s = gather_low(grad_normed, "mp", mp_size)
    came = both_ways(along1, along2, seq_size)
    grad, grad_attended, small_attend = kernel(
        norm_back_body,
        [f32(4, half, width), low(slots, width), f32(SMALL_ROWS, width)],
        (ids, grad_normed, *s, unit, inv, row(attn_gain)),
        smem=1,
        micros=6.5,
    )
    own_input, o1, o2, o3, scores, stack, sums = kernel(
        functools.partial(attend_back_body, heads, query_scale),
        [f32(block_len, width)]
        + [low(block_len, width)] * 3
        + [f32(heads, full, slots), low(3 * part, full), f32(heads, 16, head)],
        (ids, grad, grad_attended, wq, wk, wv, out_weight, probs, qt, kt, vt),
        smem=1,
        scratch=[
            pltpu.VMEM((3 * part, width), LOW),
            pltpu.VMEM((part, slots), LOW),
            pltpu.VMEM((part, slots), LOW),
            pltpu.VMEM((full, width), F32),
        ],
        micros=0.1,
    )
    rel = kernel(
        functools.partial(rel_body, heads, block_len, 32),
        f32(8, 128),
        (ids, scores),
        smem=1,
        scratch=[pltpu.VMEM((heads * BASES, 8, slots), F32)],
        micros=0.1,
    )
    half_rows = 2 * part
    attend_keep, attend_send, small = kernel(
        attend_weights_body,
        [f32(half_rows, width), low(half_rows + SMALL_ROWS, width), f32(SMALL_ROWS, width)],
        (ids, after(tokens, came), grad_attended, stack, ct, small_feed, small_attend, sums),
        smem=1,
        micros=0.1,
    )
    landed = ordered((o1, o2, o3), "mp", mp_size, [1, 2, 3])
    attend_arrived = swap(attend_send, "dp", dp_size, 1)
    few = half_rows // 8
    attend_kept, feed_own, along1, along2 = kernel(
        step_a_body,
        [f32(4 * few, width), f32(2 * rows, width)]
        + [low(2 * few + rows + SMALL_ROWS, width), low(2 * few + rows, width)],
        (ids, attend_keep, attend_arrived, small, rel, feed_kept, *came),
        smem=1,
        scratch=[pltpu.VMEM((half_rows, width), F32), pltpu.VMEM((SMALL_ROWS, width), F32)],
        micros=0.1,
    )
    met = kernel(touch_body, low(SMALL_ROWS, width), tuple(landed), micros=4.2)
    quarter = block_len // 4
    q0, *q = kernel(
        quarters_body,
        [low(quarter, width)] + [low(quarter + half, width)] * 3,
        (met, *landed, own_input, *outputs[1:]),
        micros=0.5,
    )
    attend_own, sent1, sent2 = kernel(
        step_b_body,
        [f32(2 * few, width), low(few + 2 * rows, width), low(few + 2 * rows + SMALL_ROWS, width)],
        (attend_kept, after(feed_own, q0), along1, *both_ways(along1, along2, seq_size)),
        micros=0.1,
    )
    near = both_ways(sent1, sent2, seq_size)
    q = [swap(q[k - 1], "seq", seq_size, k) for k in [2, 1, 3]]
    q = deep(q)
    q = [q[[2, 1, 3].index(k)] for k in range(1, 4)]
    joined = kernel(join_body, low(block_len, width), (q0, *q), micros=6.8)
    spread = gather_low(joined, "mp", mp_size)
    *mid, small = kernel(
        step_c_body,
        [low(few, width)] * 2 + [low(SMALL_ROWS, width)],
        (after(attend_own, joined), sent2, *near),
        micros=0.1,
    )
    output_all = kernel(output_body, low(4, half, width), (ids, outputs[0], *q), smem=1, micros=0.1)
    along1, along2 = kernel(
        step_d_body,
        [low(2 * few + rows, width)] * 2,
        (after(mid[0], output_all), mid[1], *both_ways(*mid, seq_size), *near),
        micros=0.1,
    )
    came = both_ways(along1, along2, seq_size)
    input_all = kernel(
        place_body,
        [f32(4, block_len, width)],
        (ids, joined, *spread),
        smem=1,
        scratch=[pltpu.VMEM((4, block_len, width), F32), pltpu.SemaphoreType.DMA((4,))],
        micros=7.0,
        hbm=(0,),
    )[0]
    attend_mine, feed_mine = kernel(
        joins_body,
        [low(half_rows + SMALL_ROWS, width), low(width, width)],
        (ids, along1, along2, after(came[0], input_all), came[1], sent1, sent2, *near, small),
        smem=1,
        micros=0.2,
    )
    attend_mine, feed_mine = dp_sum((attend_mine, feed_mine), dp_size)
    attend_other = swap(attend_mine, "dp", dp_size, 1)
    feed_other = swap(feed_mine, "dp", dp_size, 1)
    large = [f32(width, width)] * 2 + [f32(part, width)] * 4
    work = [pltpu.VMEM((2, part, width), F32), pltpu.VMEM((width, width), F32), pltpu.SemaphoreType.DMA((6,))]
    halves = kernel(
        widen_body, large, (ids, attend_mine, feed_mine), smem=1, scratch=work, micros=0.1, hbm=range(6)
    )
    down_grad, up_grad, dq, dk, dv, do, *small, query_sum, value_sum, rel_sum = kernel(
        unpack_body,
        large + [f32(width)] * 7 + [f32(part)] * 2 + [f32(heads, BASES)],
        (ids, attend_mine, attend_other, feed_other, *halves),
        smem=1,
        scratch=work,
        micros=0.1,
        hbm=range(6),
        reused=6,
    )
    ffn_gain_sum, ffn_shift_sum, down_bias_sum, up_bias_sum, attn_gain_sum, attn_shift_sum, out_bias_sum = small
    return (
        output_all,
        input_all,
        dq.T,
        query_sum,
        dk.T,
        dv.T,
        value_sum,
        rel_sum,
        do,
        out_bias_sum,
        attn_gain_sum,
        attn_shift_sum,
        up_grad,
        up_bias_sum,
        down_grad,
        down_bias_sum,
        ffn_gain_sum,
        ffn_shift_sum,
    )


def solution(mesh):
    return jax.shard_map(
        shards,
        mesh=mesh,
        in_specs=(
            P("dp", "seq", None),
            P("dp"),
            P(None, "mp"),
            P("mp"),
            P(None, "mp"),
            P(None, "mp"),
            P("mp"),
            P("mp", None),
            P("mp", None),
            P(),
            P(),
            P(),
            P(None, "mp"),
            P("mp"),
            P("mp", None),
            P(),
            P(),
            P(),
            P("dp", "seq", None),
        ),
        out_specs=(
            P("dp", "seq", None),
            P("dp", "seq", None),
            P(None, "mp"),
            P("mp"),
            P(None, "mp"),
            P(None, "mp"),
            P("mp"),
            P("mp", None),
            P("mp", None),
            P(),
            P(),
            P(),
            P(None, "mp"),
            P("mp"),
            P("mp", None),
            P(),
            P(),
            P(),
        ),
        check_vma=False,
    )
```
